32 devices in a mesh: dp: 16 (over z, y, x), mp: 2 (over core).
Axes of the slice: x: 2, y: 2, z: 4, core: 2. Of those that a mesh axis runs over, the one named last changes fastest.
Arguments:
- tokens: float32 [32, 896, 384], P(('dp', 'mp')), may hold values from -90 to 90
- segment_ids: int32 [32, 896], P(('dp', 'mp')), may hold values from 0 to 4, as said below
- gains: float32 [5, 384], replicated, may hold values from 0.5 to 1.5
- shifts: float32 [6, 384], replicated, may hold values from -1 to 1
- kernels: float32 [3, 9, 384], replicated, may hold values from -2 to 2
- qkv_weight: float32 [384, 1152], replicated, may hold values from -0.3125 to 0.3125
- out_weight: float32 [384, 384], replicated, may hold values from -1.75 to 1.75
- mlp_in_weight: float32 [384, 1536], P(None, 'mp'), may hold values from -0.3125 to 0.3125
- mlp_in_bias: float32 [1536], P('mp'), may hold values from -2.5 to 2.5
- mlp_out_weight: float32 [1536, 384], P('mp'), may hold values from -0.15625 to 0.15625
- cotangent: float32 [32, 896, 384], P(('dp', 'mp')), may hold values from -20 to 20
Outputs:
- output: float32 [32, 896, 384], P(('dp', 'mp'))
- grad_tokens: float32 [32, 896, 384], P(('dp', 'mp'))
- grad_gains: float32 [5, 384], replicated
- grad_shifts: float32 [6, 384], replicated
- grad_kernels: float32 [3, 9, 384], replicated
- grad_qkv: float32 [384, 1152], replicated
- grad_out: float32 [384, 384], replicated
- grad_mlp_in: float32 [384, 1536], P(None, 'mp')
- grad_mlp_bias: float32 [1536], P('mp')
- grad_mlp_out: float32 [1536, 384], P('mp')
The draws below stay inside these ranges and needn't reach their ends.
Inputs may be any that keep to these rules, and one draw needn't show every extreme that they name: `segment_ids`: each canvas is 14 rows of 64 columns stored row by row; it holds 4 images of 14 x 14 cells in disjoint runs of 14 whole columns, numbered 1 to 4 from left to right; all other cells are 0.
All inputs are finite; a program needn't handle non-finite values.
Results may differ from the reference program's by a relative error of at most 0.012.
The reference program's roundings to bfloat16 on the way count: a program that leaves them out, or rounds other values in their place, can miss the bound.
Values may be sent and summed in bfloat16 or wider, within the bound.
A program may use at most 192 MiB of HBM per device.

```python
import math
import jax
import jax.numpy as jnp
from jax import lax

D = 384
HEADS = 6
HEAD = 64
FF = 1536
IMG = 14
IMAGES = 4
GAP = 8
CANVAS_W = 64
CT = 896
CANVASES = 32


def draw_segment_ids(key, part):
    key = jax.random.fold_in(key, 23)
    gap_widths = jax.random.randint(key, (CANVASES, IMAGES), 0, GAP // IMAGES + 1)
    image_start = jnp.cumsum(gap_widths, 1) + IMG * jnp.arange(IMAGES)[None, :]
    column = jnp.arange(CANVAS_W)[None, None, :]
    inside = (column >= image_start[:, :, None]) & (column < image_start[:, :, None] + IMG)
    image_ids = jnp.sum(inside.astype(jnp.int32) * (jnp.arange(IMAGES)[None, :, None] + 1), 1)
    return jnp.broadcast_to(image_ids[:, None, :], (CANVASES, IMG, CANVAS_W)).reshape(CANVASES, CT).astype(jnp.int32)


def draw_tokens(key, part):
    key = jax.random.fold_in(key, 11)
    subkeys = jax.random.split(key, 3)
    position = jnp.arange(CANVASES, dtype=jnp.float32)[:, None, None] / (CANVASES - 1)
    noise_part = jax.random.truncated_normal(subkeys[0], -6.0, 6.0, (CANVASES, CT, D), jnp.float32)
    row_scale = jnp.exp(jax.random.uniform(subkeys[1], (CANVASES, CT, 1), jnp.float32, math.log(0.4), math.log(4.0)))
    pattern_level = 0.5 + 1.5 * position
    pattern = jax.random.truncated_normal(subkeys[2], -4.0, 4.0, (1, 1, D), jnp.float32)
    return row_scale * (noise_part + pattern_level * pattern)


def draw_cotangent(key, part):
    key = jax.random.fold_in(key, 37)
    subkeys = jax.random.split(key, 1)
    position = jnp.arange(CANVASES, dtype=jnp.float32)[:, None, None] / (CANVASES - 1)
    noise_part = jax.random.truncated_normal(subkeys[0], -6.0, 6.0, (CANVASES, CT, D), jnp.float32)
    return noise_part * (1.0 + 2.0 * position)


def levels(stream_key, extent, shards, low, high):
    level = 1.0
    for dim, parts in shards:
        heights = jax.random.uniform(jax.random.fold_in(jax.random.fold_in(stream_key, 6), dim), (parts,), jnp.float32, low / len(shards), high / len(shards))
        level = level * jnp.repeat(jnp.exp(heights), extent[dim] // parts).reshape((-1,) + (1,) * (len(extent) - 1 - dim))
    return level


def scatter_about(rng, dims, width, most, cuts=(), kind=jnp.bfloat16):
    gain = levels(rng, dims, cuts, -0.22, 0.18) if cuts else 1.0
    values = jax.random.normal(rng, dims, jnp.float32) * width * gain
    return jnp.minimum(jnp.maximum(values, -most), most).astype(kind)


def setup_inputs(seed: int = 0) -> dict:
    seeds = jax.random.split(jax.random.key(seed), 12)
    return {
        "tokens": draw_tokens(jax.random.fold_in(seeds[11], 71), 0),
        "segment_ids": draw_segment_ids(jax.random.fold_in(seeds[11], 71), 0),
        "gains": jnp.clip(1.0 + 0.1 * jax.random.normal(seeds[2], (5, D), jnp.float32), 0.5, 1.5),
        "shifts": scatter_about(seeds[3], (6, D), 0.2, 1.0, (), jnp.float32),
        "kernels": scatter_about(seeds[4], (3, 9, D), 9 ** -0.5, 2.0, (), jnp.float32),
        "qkv_weight": scatter_about(seeds[5], (D, 3 * D), D ** -0.5, 0.3125, (), jnp.float32),
        "out_weight": scatter_about(seeds[6], (D, D), (D // 32) ** -0.5, 1.75, (), jnp.float32),
        "mlp_in_weight": scatter_about(seeds[7], (D, FF), D ** -0.5, 0.3125, ((1, 2),), jnp.float32),
        "mlp_in_bias": scatter_about(seeds[8], (FF,), 0.5, 2.5, ((0, 2),), jnp.float32),
        "mlp_out_weight": scatter_about(seeds[9], (FF, D), FF ** -0.5, 0.15625, ((0, 2),), jnp.float32),
        "cotangent": draw_cotangent(jax.random.fold_in(seeds[11], 71), 0),
    }


EPS = 1e-05
MASKED = -1e+30

@jax.custom_vjp
def low(v):
    return lax.optimization_barrier(v.astype(jnp.bfloat16)).astype(jnp.float32)

@jax.custom_vjp
def low_back(v):
    return v

def low_keep(v):
    return (low(v), None)

def low_pass(kept, grad):
    return (grad,)

def back_keep(v):
    return (v, None)

def back_low(kept, grad):
    return (low(grad),)
low.defvjp(low_keep, low_pass)
low_back.defvjp(back_keep, back_low)

def norm_rows(values, gain_row, shift_row):
    centred = values - lax.optimization_barrier(jnp.mean(values, -1, keepdims=True))
    variance = lax.optimization_barrier(jnp.mean(centred * centred, -1, keepdims=True))
    return centred * lax.rsqrt(variance + EPS) * gain_row + shift_row

def tap_masks(segment_ids):
    canvases = segment_ids.shape[0]
    layout = segment_ids.reshape(canvases, IMG, CANVAS_W)
    padded = jnp.pad(layout, ((0, 0), (1, 1), (1, 1)), constant_values=-1)
    collected = []
    for row_off in range(3):
        for col_off in range(3):
            neighbour = padded[:, row_off:row_off + IMG, col_off:col_off + CANVAS_W]
            collected.append(((neighbour == layout) & (layout > 0)).reshape(canvases, -1))
    return jnp.stack(collected).astype(jnp.float32)

def shifted(feature_map, row_off, col_off):
    canvases, positions, features = feature_map.shape
    layout = feature_map.reshape(canvases, IMG, CANVAS_W, features)
    padded = jnp.pad(layout, ((0, 0), (1, 1), (1, 1), (0, 0)))
    return padded[:, row_off:row_off + IMG, col_off:col_off + CANVAS_W].reshape(canvases, positions, features)

def depthwise(feature_map, kernels, masks_all):
    accum = jnp.zeros((3,) + feature_map.shape, jnp.float32)
    for offset_index in range(9):
        displaced = shifted(feature_map, offset_index // 3, offset_index % 3) * masks_all[offset_index][:, :, None]
        accum = accum + displaced[None] * kernels[:, offset_index][:, None, None, :]
    return accum

def smooth(values):
    return jax.nn.gelu(values, approximate=False)

def layer(tokens, gains, shifts, kernels, qkv_weight, out_weight, mlp_in_weight, mlp_in_bias, mlp_out_weight, segment_ids):
    highest = lax.Precision.HIGHEST
    group_size = 4
    blocks = tokens.shape[0] // group_size
    tok_blocks = tokens.reshape(blocks, group_size, CT, D)
    seg_blocks = segment_ids.reshape(blocks, group_size, CT)
    total_rows = IMAGES * IMG * IMG * tokens.shape[0]
    score_scale = 1.0 / math.sqrt(HEAD)

    def convolve(block, seg_block):
        normed = norm_rows(block, gains[0], shifts[0])
        inside_mask = (seg_block > 0).astype(jnp.float32)[:, :, None]
        return (depthwise(normed, kernels, tap_masks(seg_block)), inside_mask)

    def add_sums(carry, block_items):
        conv_out, inside_mask = convolve(*block_items)
        return (carry + lax.optimization_barrier(jnp.sum(conv_out * inside_mask, (1, 2))), None)
    bn_sums, _ = lax.scan(jax.checkpoint(add_sums), jnp.zeros((3, D), jnp.float32), (tok_blocks, seg_blocks))
    bn_mean = bn_sums / total_rows

    def add_squares(carry, block_items):
        conv_out, inside_mask = convolve(*block_items)
        centred = conv_out - bn_mean[:, None, None, :]
        return (carry + lax.optimization_barrier(jnp.sum(centred * centred * inside_mask, (1, 2))), None)
    squares, _ = lax.scan(jax.checkpoint(add_squares), jnp.zeros((3, D), jnp.float32), (tok_blocks, seg_blocks))
    inverse = lax.rsqrt(squares / total_rows + EPS)
    bn_shift = jnp.stack([shifts[1], jnp.zeros_like(shifts[1]), shifts[2]])
    qkv_low = low(qkv_weight).reshape(D, 3, D)
    out_low = low(out_weight)
    in_low = low(mlp_in_weight)
    down_low = low(mlp_out_weight)

    def block_out(block_items):
        block, seg_block = block_items
        conv_out, inside_mask = convolve(block, seg_block)
        standard = (conv_out - bn_mean[:, None, None, :]) * inverse[:, None, None, :]
        normal_bn = low(standard * gains[1:4][:, None, None, :] + bn_shift[:, None, None, :])
        projected = low(low_back(jnp.einsum('icte,eif->ictf', normal_bn, qkv_low, precision=highest)))
        queries = projected[0].reshape(group_size, CT, HEADS, HEAD)
        key_rows = projected[1].reshape(group_size, CT, HEADS, HEAD)
        value_rows = projected[2].reshape(group_size, CT, HEADS, HEAD)
        scores = low_back(jnp.einsum('gqhe,gkhe->ghqk', queries, key_rows, precision=highest) * score_scale)
        allowed = seg_block[:, :, None] == seg_block[:, None, :]
        scores = jnp.where(allowed[:, None], scores, MASKED)
        softmaxed = low(jax.nn.softmax(scores, -1))
        attended = jnp.einsum('ghqk,gkhe->gqhe', softmaxed, value_rows, precision=highest).reshape(group_size, CT, D)
        attended = low(low_back(attended))
        attn_branch = low_back(jnp.einsum('gtd,de->gte', attended, out_low, precision=highest)) + shifts[3]
        residual = block + attn_branch
        normed2 = low(norm_rows(residual, gains[4], shifts[4]))
        pre_gelu = low_back(jnp.einsum('gte,ef->gtf', normed2, in_low, precision=highest)) + mlp_in_bias
        activated = low(smooth(pre_gelu))
        branch = low_back(jnp.einsum('gtf,fd->gtd', activated, down_low, precision=highest))
        return residual + branch + shifts[5]
    result = lax.map(jax.checkpoint(block_out), (tok_blocks, seg_blocks))
    return result.reshape(tokens.shape)

def reference(tokens, segment_ids, gains, shifts, kernels, qkv_weight, out_weight, mlp_in_weight, mlp_in_bias, mlp_out_weight, cotangent):

    def forward(tok_arg, gain_arg, shift_arg, kern_arg, qkv_arg, out_arg, in_arg, bias_arg, down_arg):
        return layer(tok_arg, gain_arg, shift_arg, kern_arg, qkv_arg, out_arg, in_arg, bias_arg, down_arg, segment_ids)
    output, pullback = jax.vjp(forward, tokens, gains, shifts, kernels, qkv_weight, out_weight, mlp_in_weight, mlp_in_bias, mlp_out_weight)
    grads = pullback(cotangent)
    return (output, grads[0], grads[1], grads[2], grads[3], grads[4], grads[5], grads[6], grads[7], grads[8])
```

```python
import functools
import math

import jax
import jax.numpy as jnp
from jax import lax
from jax.experimental import pallas as pl
from jax.experimental.pallas import tpu as pltpu
from jax.sharding import PartitionSpec as P

F32 = jnp.float32
BF = jnp.bfloat16
MESH = pl.DeviceIdType.MESH
D = 384
IMG = 14
IMAGES = 4
CW = 64
CELLS = IMG * CW
IR = 224
GAP0 = IMAGES * IR
GAPS = 112
R = 1024
CH = 256
STRIDE = IR + 16
CONVR = IMAGES * STRIDE + 16
EPS = 1e-05
MASKED = -1e30
QUAD = 4
VLIM = 60 * 2**20
SCALE = 0.125


def params(**kw):
    return pltpu.CompilerParams(vmem_limit_bytes=VLIM, **kw)


VM = pl.BlockSpec(memory_space=pltpu.VMEM)
SM = pl.BlockSpec(memory_space=pltpu.SMEM)
ANY = pl.BlockSpec(memory_space=pl.ANY)


def shape(*dims, dtype=F32):
    return jax.ShapeDtypeStruct(dims, dtype)


def dot(a, b):
    return jnp.dot(a, b, preferred_element_type=F32)


def dot_t(a, b):
    return lax.dot_general(a, b, (((1,), (1,)), ((), ())), preferred_element_type=F32)


def t_dot(a, b):
    return lax.dot_general(a, b, (((0,), (0,)), ((), ())), preferred_element_type=F32)


def cell_mask(rows):
    row = lax.broadcasted_iota(jnp.int32, (rows, 1), 0)
    return (row % 16 < IMG).astype(F32)


def rows_at(start, size, align=16):
    return pl.ds(pl.multiple_of(start, align), size)


def find_columns(seg, starts, gaps):
    def step(col, count):
        here = seg[0, col]
        before = jnp.where(col == 0, 0, seg[0, jnp.maximum(col - 1, 0)])

        @pl.when(here == 0)
        def _():
            gaps[count] = col

        @pl.when((here > 0) & (here != before))
        def _():
            starts[here - 1] = col

        return count + jnp.where(here == 0, 1, 0)

    lax.fori_loop(0, CW, step, 0)


def to_images(scr, out, starts, gaps):
    col = lax.broadcasted_iota(jnp.int32, (16, 128), 0)
    sub = lax.broadcasted_iota(jnp.int32, (8, 128), 0)

    def step(r, carry):
        for i in range(IMAGES):
            for t in range(3):
                window = scr[t, pl.ds(r * CW + starts[i], 16), :]
                out[rows_at(i * IR + r * 16, 16), t * 128 : t * 128 + 128] = jnp.where(col < IMG, window, 0.0)
        for t in range(3):
            block = jnp.zeros((8, 128), F32)
            for k in range(8):
                block = jnp.where(sub == k, scr[t, pl.ds(r * CW + gaps[k], 1), :], block)
            out[rows_at(GAP0 + r * 8, 8, 8), t * 128 : t * 128 + 128] = block
        return carry

    lax.fori_loop(0, IMG, step, 0)
    out[GAP0 + GAPS : R, :] = jnp.zeros((R - GAP0 - GAPS, D), F32)


def to_canvas(src, scr, starts, gaps):
    def step(r, carry):
        for t in range(3):
            for i in range(IMAGES):
                block = src[rows_at(i * IR + r * 16, 16), t * 128 : t * 128 + 128]
                scr[t, pl.ds(r * CW + starts[i], 16), :] = block
            block = src[rows_at(GAP0 + r * 8, 8, 8), t * 128 : t * 128 + 128]
            for k in range(8):
                scr[t, pl.ds(r * CW + gaps[k], 1), :] = block[k : k + 1]
        return carry

    lax.fori_loop(0, IMG, step, 0)


def norm_parts(x):
    mean = jnp.sum(x, -1, keepdims=True) * (1.0 / D)
    centred = x - mean
    var = jnp.sum(centred * centred, -1, keepdims=True) * (1.0 / D)
    rstd = lax.rsqrt(var + EPS)
    return centred * rstd, rstd


def store_shifted(dst, i, t, x):
    lanes = slice(t * 128, t * 128 + 128)
    at = rows_at(i * STRIDE + 16, IR)
    dst[0, at, lanes] = pltpu.roll(x, 1, 0)
    dst[1, at, lanes] = x
    dst[2, at, lanes] = pltpu.roll(x, IR - 1, 0)


def zero_borders(dst):
    for i in range(IMAGES + 1):
        for c in range(3):
            dst[c, i * STRIDE : i * STRIDE + 16, :] = jnp.zeros((16, D), F32)


def first_norm(tokp, gains, shifts, nrm):
    zero_borders(nrm)
    mask = cell_mask(IR)

    def step(i, carry):
        xhat, _ = norm_parts(tokp[rows_at(i * IR, IR), :])
        normed = (xhat * gains[0:1] + shifts[0:1]) * mask
        for t in range(3):
            store_shifted(nrm, i, t, normed[:, t * 128 : t * 128 + 128])
        return carry

    lax.fori_loop(0, IMAGES, step, 0)


CB = 32


def conv_forward(nrm, kernels, conv, stats):
    mask = cell_mask(CB)
    blocks = IMAGES * IR // CB
    per = IR // CB
    for t in range(3):
        lanes = slice(t * 128, t * 128 + 128)
        taps = [[kernels[k, o : o + 1, lanes] for o in range(9)] for k in range(3)]

        def step(b, sums):
            base = (b // per) * STRIDE + 16 + (b % per) * CB
            acc = [jnp.zeros((CB, 128), F32)] * 3
            for o in range(9):
                x = nrm[o % 3, rows_at(base + (o // 3 - 1) * 16, CB), lanes]
                for k in range(3):
                    acc[k] = acc[k] + x * taps[k][o]
            new = []
            for k in range(3):
                conv[k, rows_at(b * CB, CB), lanes] = acc[k]
                new.append(sums[k] + jnp.sum((acc[k] * mask).reshape(CB // 8, 8, 128), 0))
            return tuple(new)

        sums = lax.fori_loop(0, blocks, step, (jnp.zeros((8, 128), F32),) * 3)
        means = [jnp.sum(s, 0, keepdims=True) * (1.0 / (IMAGES * IMG * IMG)) for s in sums]

        def spread(b, sums):
            new = []
            for k in range(3):
                away = (conv[k, rows_at(b * CB, CB), lanes] - means[k]) * mask
                new.append(sums[k] + jnp.sum((away * away).reshape(CB // 8, 8, 128), 0))
            return tuple(new)

        squares = lax.fori_loop(0, blocks, spread, (jnp.zeros((8, 128), F32),) * 3)
        for k in range(3):
            stats[k : k + 1, lanes] = means[k]
            stats[3 + k : 4 + k, lanes] = jnp.sum(squares[k], 0, keepdims=True)
        stats[6:8, lanes] = jnp.zeros((2, 128), F32)
    for k in range(3):
        conv[k, GAP0:R, :] = jnp.zeros((R - GAP0, D), F32)


def first_kernel(
    seg, tokens, cot, gains, shifts, kernels, wqkv, wout, win, wmo,
    tokp, cotp, conv, stats, wqkv_b, wout_b, win_b, wmo_b,
    scr, nrm, starts, gaps, sems,
):
    copies = []
    for n, src in enumerate((tokens, cot)):
        for t in range(3):
            copy = pltpu.make_async_copy(
                src.at[0, :, pl.ds(t * 128, 128)], scr.at[n, t, pl.ds(0, CELLS)], sems.at[n, t]
            )
            copy.start()
            copies.append(copy)
    find_columns(seg, starts, gaps)
    for k in range(3):
        wqkv_b[k] = wqkv[:, k * D : k * D + D].astype(BF)
    wout_b[...] = wout[...].astype(BF)
    for j in range(2):
        win_b[j] = win[:, j * D : j * D + D].astype(BF)
        wmo_b[j] = wmo[j * D : j * D + D].astype(BF)
    for copy in copies:
        copy.wait()
    to_images(scr.at[0], tokp, starts, gaps)
    to_images(scr.at[1], cotp, starts, gaps)
    first_norm(tokp, gains, shifts, nrm)
    conv_forward(nrm, kernels, conv, stats)


def first_call(seg, tokens, cot, gains, shifts, kernels, wqkv, wout, win, wmo):
    return pl.pallas_call(
        first_kernel,
        out_shape=(
            shape(R, D), shape(R, D), shape(3, R, D), shape(8, D),
            shape(3, D, D, dtype=BF), shape(D, D, dtype=BF), shape(2, D, D, dtype=BF), shape(2, D, D, dtype=BF),
        ),
        in_specs=[SM, ANY, ANY] + [VM] * 7,
        out_specs=(VM,) * 8,
        scratch_shapes=[
            pltpu.VMEM((2, 3, CELLS + 16, 128), F32),
            pltpu.VMEM((3, CONVR, D), F32),
            pltpu.SMEM((8,), jnp.int32),
            pltpu.SMEM((64,), jnp.int32),
            pltpu.SemaphoreType.DMA((2, 3)),
        ],
        compiler_params=params(),
    )(seg, tokens, cot, gains, shifts, kernels, wqkv, wout, win, wmo)


class Place:
    def __init__(self, groups):
        dp = lax.axis_index("dp")
        self.mp = lax.axis_index("mp")
        self.groups = groups
        self.quad = lax.rem(dp, QUAD)
        self.z = dp // QUAD
        self.slot = self.quad * 2 + self.mp

    def in_eight(self, offset):
        other = lax.rem(self.slot + offset, 8)
        return (self.z * QUAD + other // 2, lax.rem(other, 2))

    def in_quad(self, offset):
        return (self.z * QUAD + lax.rem(self.quad + offset, QUAD), self.mp)

    def along(self, offset):
        return (lax.rem(self.z + offset, self.groups) * QUAD + self.quad, self.mp)

    def other_core(self):
        return (self.z * QUAD + self.quad, 1 - self.mp)

    def greet(self):
        barrier = pltpu.get_barrier_semaphore()
        peers = [self.in_eight(o) for o in range(1, 8)] + [self.along(o) for o in range(1, self.groups)]
        for peer in peers:
            pl.semaphore_signal(barrier, inc=1, device_id=peer, device_id_type=MESH)
        pl.semaphore_wait(barrier, len(peers))


def remote(src, dst, send, recv, peer):
    copy = pltpu.make_async_remote_copy(
        src_ref=src, dst_ref=dst, send_sem=send, recv_sem=recv, device_id=peer, device_id_type=MESH
    )
    copy.start()
    return copy


def send_eight(place, src, rx, send, recv):
    return [remote(src, rx.at[place.slot], send.at[o], recv.at[o], place.in_eight(o)) for o in range(1, 8)]


def send_along(place, src, rx, send, recv):
    return [remote(src, rx.at[place.z], send.at[o], recv.at[o], place.along(o)) for o in range(1, place.groups)]


def finish(copies):
    for copy in copies:
        copy.wait()


def sum_slots(rx, count):
    total = rx[0]
    for s in range(1, count):
        total = total + rx[s]
    return total


def all_sum(place, src, rx1, rx2, sems):
    send1, recv1, send2, recv2 = sems
    copies = send_eight(place, src, rx1, send1, recv1)
    rx1[place.slot] = src[...]
    finish(copies)
    rx2[place.z] = sum_slots(rx1, 8)
    finish(send_along(place, rx2.at[place.z], rx2, send2, recv2))
    return sum_slots(rx2, place.groups)


def merge_moments(rx, count, cells):
    mean = sum([rx[s, 0:3] for s in range(1, count)], rx[0, 0:3]) * (1.0 / count)
    m2 = sum([rx[s, 3:6] for s in range(1, count)], rx[0, 3:6])
    for s in range(count):
        away = rx[s, 0:3] - mean
        m2 = m2 + away * away * float(cells)
    return mean, m2


def pair_weights(place, win_b, wmo_b, bias, win_f, wmo_f, bias_f, send, recv, local):
    copies = []
    half = pl.ds(place.mp * 2, 2)
    for n, (src, dst) in enumerate(((win_b, win_f), (wmo_b, wmo_f))):
        copies.append(remote(src, dst.at[half], send.at[n], recv.at[n], place.other_core()))
        here = pltpu.make_async_copy(src, dst.at[half], local.at[n])
        here.start()
        copies.append(here)
    copies.append(remote(bias, bias_f.at[place.mp], send.at[2], recv.at[2], place.other_core()))
    bias_f[place.mp] = bias[...]
    return copies


def stats_kernel(groups, stats, win_b, wmo_b, bias, moments, win_f, wmo_f, bias_f, rx1, rx2, s1, r1, s2, r2, sw, rw, lw):
    place = Place(groups)
    place.greet()
    copies = send_eight(place, stats, rx1, s1, r1)
    rx1[place.slot] = stats[...]
    weights = pair_weights(place, win_b, wmo_b, bias, win_f, wmo_f, bias_f, sw, rw, lw)
    finish(copies)
    cells = IMAGES * IMG * IMG
    mean, m2 = merge_moments(rx1, 8, cells)
    rx2[place.z, 0:3] = mean
    rx2[place.z, 3:6] = m2
    rx2[place.z, 6:8] = jnp.zeros((2, D), F32)
    finish(send_along(place, rx2.at[place.z], rx2, s2, r2))
    mean, m2 = merge_moments(rx2, groups, 8 * cells)
    moments[0:3] = mean
    moments[3:6] = lax.rsqrt(m2 * (1.0 / (cells * 8 * groups)) + EPS)
    moments[6:8] = jnp.zeros((2, D), F32)
    finish(weights)


def dma(*n):
    return pltpu.SemaphoreType.DMA(n)


def stats_call(groups, stats, win_b, wmo_b, bias):
    return pl.pallas_call(
        functools.partial(stats_kernel, groups),
        out_shape=(shape(8, D), shape(4, D, D, dtype=BF), shape(4, D, D, dtype=BF), shape(2, 8, D)),
        in_specs=[VM] * 4,
        out_specs=(VM,) * 4,
        scratch_shapes=[
            pltpu.VMEM((8, 8, D), F32), pltpu.VMEM((groups, 8, D), F32),
            dma(8), dma(8), dma(groups), dma(groups), dma(3), dma(3), dma(2),
        ],
        compiler_params=params(collective_id=0, has_side_effects=True),
    )(stats, win_b, wmo_b, bias)


def project(conv, moments, gains, shifts, wqkv, bn, qkv):
    def step(c, carry):
        rows = rows_at(c * CH, CH)
        for k in range(3):
            standard = (conv[k, rows, :] - moments[k : k + 1]) * moments[3 + k : 4 + k]
            value = standard * gains[1 + k : 2 + k]
            if k != 1:
                value = value + (shifts[1:2] if k == 0 else shifts[2:3])
            value = value.astype(BF)
            bn[k, rows, :] = value
            out = dot(value, wqkv[k]).astype(BF)
            if k == 0:
                out = (out * SCALE).astype(BF)
            for p in range(3):
                qkv[k, p, rows, :] = out[:, p * 128 : p * 128 + 128]
        return carry

    lax.fori_loop(0, R // CH, step, 0)


def key_bias():
    row = lax.broadcasted_iota(jnp.int32, (16, 256), 0)
    return jnp.where(row < IMG, 0.0, MASKED)


def query_mask():
    lane = lax.broadcasted_iota(jnp.int32, (1, 256), 1)
    return (lane < IR).astype(F32)


def halves(x):
    lane = lax.broadcasted_iota(jnp.int32, x.shape, 1)
    zero = jnp.zeros_like(x)
    return [jnp.where(lane < 64, x, zero), jnp.where(lane < 64, zero, x)]


def attend(qkv, probs, att):
    bias = key_bias()[None]
    live = query_mask()

    def step(n, carry):
        i, p = n // 3, lax.rem(n, 3)
        rows = rows_at(i * IR, IR)
        q = qkv[0, p, rows_at(i * IR, 256), :]
        k = qkv[1, p, rows, :]
        v_t = qkv[2, p, rows, :].T
        parts = []
        for h, k_h in enumerate(halves(k)):
            scores = (dot_t(k_h, q).reshape(IMG, 16, 256) + bias).reshape(IR, 256)
            largest = jnp.max(scores, 0, keepdims=True)
            expo = jnp.exp(scores - largest)
            soft = expo * (live / jnp.sum(expo, 0, keepdims=True))
            probs[n * 2 + h] = soft
            parts.append(dot(v_t[h * 64 : h * 64 + 64], soft.astype(BF)))
        out = jnp.concatenate(parts, 0).T
        att[p, rows, :] = out[:IR].astype(BF)
        return carry

    lax.fori_loop(0, 3 * IMAGES, step, 0)


def even_prob():
    return jnp.full((1, 1), 1.0 / GAPS, F32).astype(BF).astype(F32)


def attend_gap(qkv, att):
    for p in range(3):
        v = qkv[2, p, GAP0 : GAP0 + 16, :].astype(F32)
        out = (v * (even_prob() * float(GAPS))).astype(BF)
        for b in range((R - GAP0) // 16):
            att[p, GAP0 + b * 16 : GAP0 + b * 16 + 16, :] = out


def gelu_parts(x):
    cdf = 0.5 * (1.0 + lax.erf(x * (1.0 / math.sqrt(2.0))))
    density = jnp.exp(x * x * -0.5) * (1.0 / math.sqrt(2.0 * math.pi))
    return x * cdf, cdf + x * density


def col_sum(x):
    return jnp.sum(x, 0, keepdims=True)


def feed_forward(
    tokp, cotp, att, wout, win, wmo, bias, gains, shifts,
    outp, dres, n2, gm, gr, act, dpre, datt, small, acc,
):
    small[...] = jnp.zeros((16, D), F32)

    def step(c, carry):
        rows = rows_at(c * CH, CH)
        attended = jnp.concatenate([att[p, rows, :] for p in range(3)], 1)
        residual = tokp[rows, :] + (dot(attended, wout[...]) + shifts[3:4])
        xhat, rstd = norm_parts(residual)
        n2[rows, :] = (xhat * gains[4:5] + shifts[4:5]).astype(BF)
        cot = cotp[rows, :]
        gm[rows, :] = cot.astype(BF)
        outp[rows, :] = residual + shifts[5:6]
        acc[...] = jnp.zeros((CH, D), F32)

        for j in range(4):
            hidden_at(j, rows, n2, gm, win, wmo, bias, act, dpre, outp, acc, small)
        grad = acc[...]
        scaled = grad * gains[4:5]
        one = jnp.sum(scaled, -1, keepdims=True) * (1.0 / D)
        two = jnp.sum(scaled * xhat, -1, keepdims=True) * (1.0 / D)
        total = cot + rstd * (scaled - one - xhat * two)
        dres[rows, :] = total
        low = total.astype(BF)
        gr[rows, :] = low
        back = dot_t(low, wout[...]).astype(BF)
        for p in range(3):
            datt[p, rows, :] = back[:, p * 128 : p * 128 + 128]
        small[0:1] = small[0:1] + col_sum(grad * xhat)
        small[1:2] = small[1:2] + col_sum(total)
        small[2:3] = small[2:3] + col_sum(grad)
        small[3:4] = small[3:4] + col_sum(cot)
        return carry

    lax.fori_loop(0, R // CH, step, 0)


def hidden_at(j, rows, n2, gm, win, wmo, bias, act, dpre, outp, acc, small):
    pre = dot(n2[rows, :], win[j]) + bias[j // 2, j % 2 : j % 2 + 1]
    value, slope = gelu_parts(pre)
    value = value.astype(BF)
    act[j, rows, :] = value
    grad = dot_t(gm[rows, :], wmo[j]) * slope
    small[4 + j : 5 + j] = small[4 + j : 5 + j] + col_sum(grad)
    grad = grad.astype(BF)
    dpre[j, rows, :] = grad
    outp[rows, :] = outp[rows, :] + dot(value, wmo[j])
    acc[...] = acc[...] + dot_t(grad, win[j])


def feed_forward_grads(n2, gm, act, dpre, att, gr, grads):
    def step(j, carry):
        half, which = j // 2, lax.rem(j, 2)
        grads[0, half, rows_at(which * D, D), :] = t_dot(n2[...], dpre[j]).astype(BF)
        grads[1, half, rows_at(which * D, D), :] = t_dot(act[j], gm[...]).astype(BF)
        return carry

    lax.fori_loop(0, 4, step, 0)
    for p in range(3):
        grads[2, 1, D + p * 128 : D + p * 128 + 128, :] = t_dot(att[p], gr[...]).astype(BF)


def attend_back(qkv, probs, datt, dqkv):
    def step(n, carry):
        i, p = n // 3, lax.rem(n, 3)
        rows = rows_at(i * IR, IR)
        wide = rows_at(i * IR, 256)
        q = qkv[0, p, wide, :]
        k_t = qkv[1, p, rows, :].T
        v = qkv[2, p, rows, :]
        do = datt[p, wide, :]
        dq, dk, dv = [], [], []
        for h, v_h in enumerate(halves(v)):
            soft = probs[n * 2 + h]
            grad = dot_t(v_h, do)
            delta = jnp.sum(soft * grad, 0, keepdims=True)
            ds = (soft * (grad - delta)).astype(BF)
            dv.append(dot(soft.astype(BF), do))
            dk.append(dot(ds, q))
            dq.append(dot(k_t[h * 64 : h * 64 + 64], ds))
        lane = lax.broadcasted_iota(jnp.int32, (IR, 128), 1)
        dqkv[0, p, rows, :] = (jnp.concatenate(dq, 0).T[:IR] * SCALE).astype(BF)
        dqkv[1, p, rows, :] = jnp.where(lane < 64, dk[0], dk[1]).astype(BF)
        dqkv[2, p, rows, :] = jnp.where(lane < 64, dv[0], dv[1]).astype(BF)
        return carry

    lax.fori_loop(0, 3 * IMAGES, step, 0)


def attend_back_gap(datt, dqkv):
    for p in range(3):
        total = col_sum(datt[p, GAP0 : GAP0 + GAPS, :].astype(F32))
        grad = jnp.broadcast_to((total * even_prob()).astype(BF), (16, 128))
        zero = jnp.zeros((16, 128), BF)
        for b in range((R - GAP0) // 16):
            rows = slice(GAP0 + b * 16, GAP0 + b * 16 + 16)
            dqkv[0, p, rows, :] = zero
            dqkv[1, p, rows, :] = zero
            dqkv[2, p, rows, :] = grad if b < GAPS // 16 else zero


def project_back(conv, moments, wqkv, bn, dqkv, dbn, sums, grads):
    sums[...] = jnp.zeros((8, D), F32)

    def step(c, carry):
        rows = rows_at(c * CH, CH)
        for k in range(3):
            grad = jnp.concatenate([dqkv[k, p, rows, :] for p in range(3)], 1)
            back = dot_t(grad, wqkv[k])
            dbn[k, rows, :] = back
            standard = (conv[k, rows, :] - moments[k : k + 1]) * moments[3 + k : 4 + k]
            sums[k : k + 1] = sums[k : k + 1] + col_sum(back)
            sums[3 + k : 4 + k] = sums[3 + k : 4 + k] + col_sum(back * standard)
        return carry

    lax.fori_loop(0, R // CH, step, 0)
    for k in range(3):
        for p in range(3):
            grads[2, k // 2, (k % 2) * D : (k % 2) * D + D, p * 128 : p * 128 + 128] = t_dot(
                bn[k], dqkv[k, p]
            ).astype(BF)


def middle_kernel(
    tokp, cotp, conv, moments, gains, shifts, wqkv, wout, win, wmo, bias,
    outp, dres, dbn, sums, grads, small,
    bn, qkv, probs, att, n2, gm, gr, act, dpre, datt, dqkv, acc,
):
    project(conv, moments, gains, shifts, wqkv, bn, qkv)
    attend(qkv, probs, att)
    attend_gap(qkv, att)
    feed_forward(
        tokp, cotp, att, wout, win, wmo, bias, gains, shifts,
        outp, dres, n2, gm, gr, act, dpre, datt, small, acc,
    )
    feed_forward_grads(n2, gm, act, dpre, att, gr, grads)
    attend_back(qkv, probs, datt, dqkv)
    attend_back_gap(datt, dqkv)
    project_back(conv, moments, wqkv, bn, dqkv, dbn, sums, grads)


def middle_call(*args):
    return pl.pallas_call(
        middle_kernel,
        out_shape=(
            shape(R, D), shape(R, D), shape(3, R, D), shape(8, D), shape(3, 2, 2 * D, D, dtype=BF), shape(16, D),
        ),
        in_specs=[VM] * 11,
        out_specs=(VM,) * 6,
        scratch_shapes=[
            pltpu.VMEM((3, R, D), BF), pltpu.VMEM((3, 3, R, 128), BF), pltpu.VMEM((24, IR, 256), F32),
            pltpu.VMEM((3, R, 128), BF), pltpu.VMEM((R, D), BF), pltpu.VMEM((R, D), BF), pltpu.VMEM((R, D), BF),
            pltpu.VMEM((4, R, D), BF), pltpu.VMEM((4, R, D), BF), pltpu.VMEM((3, R, 128), BF),
            pltpu.VMEM((3, 3, R, 128), BF), pltpu.VMEM((CH, D), F32),
        ],
        compiler_params=params(),
    )(*args)


def sum_kernel(groups, src, out, rx1, rx2, *sems):
    place = Place(groups)
    place.greet()
    out[...] = all_sum(place, src, rx1, rx2, sems)


def sum_call(groups, src, collective_id):
    return pl.pallas_call(
        functools.partial(sum_kernel, groups),
        out_shape=shape(*src.shape),
        in_specs=[VM],
        out_specs=VM,
        scratch_shapes=[
            pltpu.VMEM((8,) + src.shape, F32), pltpu.VMEM((groups,) + src.shape, F32),
            dma(8), dma(8), dma(groups), dma(groups),
        ],
        compiler_params=params(collective_id=collective_id, has_side_effects=True),
    )(src)


def conv_back(dbn, conv, moments, sums, gains, nrm, shifted, kernels, dn, dker, inverse_total):
    mask = cell_mask(IR)
    for k in range(3):
        zero_borders(shifted.at[k])
    for k in range(3):

        def spread(i, carry):
            rows = rows_at(i * IR, IR)
            for t in range(3):
                lanes = slice(t * 128, t * 128 + 128)
                inv = moments[3 + k : 4 + k, lanes]
                standard = (conv[k, rows, lanes] - moments[k : k + 1, lanes]) * inv
                shift = (sums[k : k + 1, lanes] + standard * sums[3 + k : 4 + k, lanes]) * inverse_total
                grad = (gains[1 + k : 2 + k, lanes] * inv) * (dbn[k, rows, lanes] - mask * shift)
                store_shifted(shifted.at[k], i, t, grad)
            return carry

        lax.fori_loop(0, IMAGES, spread, 0)
    blocks = IMAGES * IR // CB
    per = IR // CB
    for t in range(3):
        lanes = slice(t * 128, t * 128 + 128)
        for k in range(3):
            taps = [kernels[k, o : o + 1, lanes] for o in range(9)]

            def step(b, sums9):
                base = (b // per) * STRIDE + 16 + (b % per) * CB
                here = nrm[1, rows_at(base, CB), lanes]
                acc = jnp.zeros((CB, 128), F32)
                new = []
                for o in range(9):
                    x = shifted[k, 2 - o % 3, rows_at(base - (o // 3 - 1) * 16, CB), lanes]
                    acc = acc + x * taps[o]
                    new.append(sums9[o] + jnp.sum((x * here).reshape(CB // 8, 8, 128), 0))
                rows = rows_at(b * CB, CB)
                if k == 0:
                    dn[rows, lanes] = acc
                else:
                    dn[rows, lanes] = dn[rows, lanes] + acc
                return tuple(new)

            sums9 = lax.fori_loop(0, blocks, step, (jnp.zeros((8, 128), F32),) * 9)
            for o in range(9):
                dker[k * 9 + o : k * 9 + o + 1, lanes] = col_sum(sums9[o])


def last_norm_back(tokp, dres, dn, gains, gtok, dker):
    mask = cell_mask(IR)
    dker[27:32] = jnp.zeros((5, D), F32)

    def step(i, carry):
        rows = rows_at(i * IR, IR)
        xhat, rstd = norm_parts(tokp[rows, :])
        grad = dn[rows, :] * mask
        dker[27:28] = dker[27:28] + col_sum(grad * xhat)
        dker[28:29] = dker[28:29] + col_sum(grad)
        scaled = grad * gains[0:1]
        one = jnp.sum(scaled, -1, keepdims=True) * (1.0 / D)
        two = jnp.sum(scaled * xhat, -1, keepdims=True) * (1.0 / D)
        gtok[rows, :] = dres[rows, :] + rstd * (scaled - one - xhat * two)
        return carry

    lax.fori_loop(0, IMAGES, step, 0)
    gtok[GAP0:R, :] = dres[GAP0:R, :]


def back_kernel(inverse_total, tokp, dres, dbn, conv, moments, sums, gains, shifts, kernels, gtok, dker, nrm, shifted, dn):
    first_norm(tokp, gains, shifts, nrm)
    conv_back(dbn, conv, moments, sums, gains, nrm, shifted, kernels, dn, dker, inverse_total)
    last_norm_back(tokp, dres, dn, gains, gtok, dker)


def back_call(inverse_total, *args):
    return pl.pallas_call(
        functools.partial(back_kernel, inverse_total),
        out_shape=(shape(R, D), shape(32, D)),
        in_specs=[VM] * 9,
        out_specs=(VM,) * 2,
        scratch_shapes=[
            pltpu.VMEM((3, CONVR, D), F32), pltpu.VMEM((3, 3, CONVR, D), F32), pltpu.VMEM((IMAGES * IR, D), F32),
        ],
        compiler_params=params(),
    )(*args)


HALF = 2 * D
QR = HALF // QUAD


class GradSum:
    def __init__(self, place, unit, src, bufs, sems):
        self.place, self.unit, self.src = place, unit, src
        self.rx_core, self.own, self.rx_quad, self.mid, self.rx_z, self.done = [b.at[unit] for b in bufs]
        self.send, self.recv = sems[0].at[unit], sems[1].at[unit]
        self.groups = place.groups
        self.part = -(-QR // (16 * self.groups)) * 16
        self.span = self.part * self.groups

    def core_start(self):
        mine = self.src.at[self.unit, 1 - self.place.mp]
        self.copies = [remote(mine, self.rx_core, self.send.at[0], self.recv.at[0], self.place.other_core())]

    def core_end(self):
        finish(self.copies)
        for b in range(HALF // 64):
            rows = slice(b * 64, b * 64 + 64)
            mine = self.src[self.unit, self.place.mp, rows, :].astype(F32)
            self.own[rows, :] = (mine + self.rx_core[rows, :].astype(F32)).astype(BF)

    def quad_start(self):
        self.copies = []
        for o in range(1, QUAD):
            rows = rows_at(lax.rem(self.place.quad + o, QUAD) * QR, QR)
            self.copies.append(
                remote(self.own.at[rows], self.rx_quad.at[o - 1], self.send.at[o], self.recv.at[o], self.place.in_quad(o))
            )

    def quad_end(self):
        finish(self.copies)
        for b in range(QR // 64):
            rows = slice(b * 64, b * 64 + 64)
            total = self.own[rows_at(self.place.quad * QR + b * 64, 64), :].astype(F32)
            for o in range(QUAD - 1):
                total = total + self.rx_quad[o, rows, :].astype(F32)
            self.mid[rows, :] = total.astype(BF)
        if self.span > QR:
            self.mid[QR:, :] = jnp.zeros((self.span - QR, D), BF)

    def z_start(self):
        self.copies = []
        for o in range(1, self.groups):
            rows = rows_at(lax.rem(self.place.z + o, self.groups) * self.part, self.part)
            at = 3 + o
            self.copies.append(
                remote(self.mid.at[rows], self.rx_z.at[o - 1], self.send.at[at], self.recv.at[at], self.place.along(o))
            )

    def z_end(self):
        finish(self.copies)
        total = self.mid[rows_at(self.place.z * self.part, self.part), :].astype(F32)
        for o in range(self.groups - 1):
            total = total + self.rx_z[o].astype(F32)
        self.done[self.place.mp, self.place.quad, rows_at(self.place.z * self.part, self.part), :] = total.astype(BF)

    def z_back_start(self):
        here = self.done.at[self.place.mp, self.place.quad, rows_at(self.place.z * self.part, self.part)]
        self.copies = []
        for o in range(1, self.groups):
            at = 2 + self.groups + o
            self.copies.append(remote(here, here, self.send.at[at], self.recv.at[at], self.place.along(o)))

    def quad_back_start(self):
        here = self.done.at[self.place.mp, self.place.quad]
        self.copies = []
        for o in range(1, QUAD):
            at = 1 + 2 * self.groups + o
            self.copies.append(remote(here, here, self.send.at[at], self.recv.at[at], self.place.in_quad(o)))

    def core_back_start(self):
        here = self.done.at[self.place.mp]
        at = 1 + 2 * self.groups + QUAD
        self.copies = [remote(here, here, self.send.at[at], self.recv.at[at], self.place.other_core())]

    def end(self):
        finish(self.copies)


def grad_buffers(groups):
    part = -(-QR // (16 * groups)) * 16
    return [
        pltpu.VMEM((3, HALF, D), BF),
        pltpu.VMEM((3, HALF, D), BF),
        pltpu.VMEM((3, QUAD - 1, QR, D), BF),
        pltpu.VMEM((3, part * groups, D), BF),
        pltpu.VMEM((3, groups - 1, part, D), BF),
    ], (3, 2, QUAD, part * groups, D)


def grads_kernel(groups, src, done, b0, b1, b2, b3, b4, send, recv):
    place = Place(groups)
    place.greet()
    units = [GradSum(place, u, src, (b0, b1, b2, b3, b4, done), (send, recv)) for u in range(3)]
    for u in units:
        u.core_start()
    for u in units:
        u.core_end()
        u.quad_start()
    for u in units:
        u.quad_end()
        u.z_start()
    for u in units:
        u.z_end()
        u.z_back_start()
    for u in units:
        u.end()
        u.quad_back_start()
    for u in units:
        u.end()
    units[2].core_back_start()
    units[2].end()


def grads_call(groups, src):
    bufs, done = grad_buffers(groups)
    n = 2 + 2 * groups + QUAD
    return pl.pallas_call(
        functools.partial(grads_kernel, groups),
        out_shape=shape(*done, dtype=BF),
        in_specs=[VM],
        out_specs=VM,
        scratch_shapes=bufs + [dma(3, n), dma(3, n)],
        compiler_params=params(collective_id=3, has_side_effects=True),
    )(src)


def last_kernel(seg, outp, gtok, output, grad_tokens, scr, starts, gaps):
    find_columns(seg, starts, gaps)
    for src, dst in ((outp, output), (gtok, grad_tokens)):
        to_canvas(src, scr, starts, gaps)
        for t in range(3):
            dst[0, :, t * 128 : t * 128 + 128] = scr[t, 0:CELLS, :]


def last_call(seg, outp, gtok):
    return pl.pallas_call(
        last_kernel,
        out_shape=(shape(1, CELLS, D), shape(1, CELLS, D)),
        in_specs=[SM, VM, VM],
        out_specs=(VM, VM),
        scratch_shapes=[
            pltpu.VMEM((3, CELLS + 16, 128), F32), pltpu.SMEM((8,), jnp.int32), pltpu.SMEM((64,), jnp.int32),
        ],
        compiler_params=params(),
    )(seg, outp, gtok)


def local(
    groups, total, tokens, segment_ids, gains, shifts, kernels, qkv_weight, out_weight,
    mlp_in_weight, mlp_in_bias, mlp_out_weight, cotangent,
):
    tokp, cotp, conv, stats, wqkv, wout, win_h, wmo_h = first_call(
        segment_ids, tokens, cotangent, gains, shifts, kernels, qkv_weight, out_weight, mlp_in_weight, mlp_out_weight
    )
    bias_h = jnp.pad(mlp_in_bias.reshape(2, D), ((0, 6), (0, 0)))
    moments, win, wmo, bias = stats_call(groups, stats, win_h, wmo_h, bias_h)
    outp, dres, dbn, sums, grads, small = middle_call(
        tokp, cotp, conv, moments, gains, shifts, wqkv, wout, win, wmo, bias
    )
    sums = sum_call(groups, sums, 1)
    gtok, dker = back_call(1.0 / total, tokp, dres, dbn, conv, moments, sums, gains, shifts, kernels)
    done = grads_call(groups, grads)[:, :, :, :QR]
    rest = sum_call(groups, jnp.concatenate([dker, small[:8]], 0), 2)
    output, grad_tokens = last_call(segment_ids, outp, gtok)
    mp = lax.axis_index("mp")
    done = done.reshape(3, 2, 2, D, D).astype(F32)
    mine = lax.dynamic_index_in_dim(done[:2], mp, 1, keepdims=False)
    grad_mlp_in = jnp.concatenate([mine[0, 0], mine[0, 1]], 1)
    grad_mlp_out = mine[1].reshape(2 * D, D)
    grad_qkv = jnp.concatenate([done[2, 0, 0], done[2, 0, 1], done[2, 1, 0]], 1)
    grad_out = done[2, 1, 1]
    grad_kernels = rest[:27].reshape(3, 9, D)
    grad_bias = lax.dynamic_slice_in_dim(rest[36:40], mp * 2, 2, 0).reshape(2 * D)
    grad_gains = jnp.stack([rest[27], sums[3], sums[4], sums[5], rest[32]])
    grad_shifts = jnp.stack([rest[28], sums[0], sums[2], rest[33], rest[34], rest[35]])
    return (
        output, grad_tokens, grad_gains, grad_shifts, grad_kernels, grad_qkv, grad_out,
        grad_mlp_in, grad_bias, grad_mlp_out,
    )


def solution(mesh):
    groups = mesh.shape["dp"] // QUAD
    total = IMAGES * IMG * IMG * mesh.shape["dp"] * mesh.shape["mp"]
    both = P(("dp", "mp"), None, None)
    return jax.shard_map(
        functools.partial(local, groups, total),
        mesh=mesh,
        in_specs=(
            both, P(("dp", "mp"), None), P(), P(), P(), P(), P(), P(None, "mp"), P("mp"), P("mp", None), both,
        ),
        out_specs=(both, both, P(), P(), P(), P(), P(), P(None, "mp"), P("mp"), P("mp", None)),
        check_vma=False,
    )
```

```python
import functools
import math

import jax
import jax.numpy as jnp
from jax import lax
from jax.experimental import pallas as pl
from jax.experimental.pallas import tpu as pltpu
from jax.sharding import PartitionSpec as P

F32 = jnp.float32
BF = jnp.bfloat16
MESH = pl.DeviceIdType.MESH
D = 384
IMG = 14
IMAGES = 4
CW = 64
CELLS = IMG * CW
IR = 224
GAP0 = IMAGES * IR
GAPS = 112
R = 1024
CH = 256
STRIDE = IR + 16
CONVR = IMAGES * STRIDE + 16
EPS = 1e-05
MASKED = -1e30
QUAD = 4
VLIM = 60 * 2**20
SCALE = 0.125


def params(**kw):
    return pltpu.CompilerParams(vmem_limit_bytes=VLIM, **kw)


VM = pl.BlockSpec(memory_space=pltpu.VMEM)
SM = pl.BlockSpec(memory_space=pltpu.SMEM)
ANY = pl.BlockSpec(memory_space=pl.ANY)


def shape(*dims, dtype=F32):
    return jax.ShapeDtypeStruct(dims, dtype)


def dot(a, b):
    return jnp.dot(a, b, preferred_element_type=F32)


def dot_t(a, b):
    return lax.dot_general(a, b, (((1,), (1,)), ((), ())), preferred_element_type=F32)


def t_dot(a, b):
    return lax.dot_general(a, b, (((0,), (0,)), ((), ())), preferred_element_type=F32)


def cell_mask(rows):
    row = lax.broadcasted_iota(jnp.int32, (rows, 1), 0)
    return (row % 16 < IMG).astype(F32)


def rows_at(start, size, align=16):
    return pl.ds(pl.multiple_of(start, align), size)


def find_columns(seg):
    def step(col, found):
        count, starts, gaps = found
        here = seg[0, col]
        starts = tuple(jnp.minimum(s, jnp.where(here == i + 1, col, CW)) for i, s in enumerate(starts))
        empty = here == 0
        gaps = tuple(jnp.where(empty & (count == k), col, g) for k, g in enumerate(gaps))
        return count + jnp.where(empty, 1, 0), starts, gaps

    start = (jnp.int32(0), (jnp.int32(CW),) * IMAGES, (jnp.int32(0),) * 8)
    _, starts, gaps = lax.fori_loop(0, CW, step, start)
    return starts, gaps


SCR = CELLS + 16
POOL = 48 * IR


def empty_before(seg):
    lane = lax.broadcasted_iota(jnp.int32, (1, 128), 1)
    ids = seg[0:1, 0:128]
    firsts = [jnp.where((ids == i + 1) & (lane < CW), lane, CW).astype(F32) for i in range(IMAGES)]
    return [jnp.min(f, -1, keepdims=True) - float(i * IMG) for i, f in enumerate(firsts)]


def to_images(pool, base, out, ahead):
    col = lax.broadcasted_iota(jnp.int32, (16, 128), 0)
    sub = lax.broadcasted_iota(jnp.int32, (8, 128), 0).astype(F32)
    before = sum([jnp.where(a <= sub, 1.0, 0.0) for a in ahead])

    def step(r, carry):
        for t in range(3):
            row = base + t * SCR + r * CW
            for i in range(IMAGES):
                window = pool[pl.ds(row + i * IMG, 16), :]
                for e in range(1, 9):
                    moved = pool[pl.ds(row + i * IMG + e, 16), :]
                    window = jnp.where(ahead[i] == float(e), moved, window)
                out[rows_at(i * IR + r * 16, 16), t * 128 : t * 128 + 128] = jnp.where(col < IMG, window, 0.0)
            block = pool[rows_at(row, 8, 8), :]
            for n in range(1, IMAGES + 1):
                block = jnp.where(before == float(n), pool[pl.ds(row + n * IMG, 8), :], block)
            out[rows_at(GAP0 + r * 8, 8, 8), t * 128 : t * 128 + 128] = block
        return carry

    lax.fori_loop(0, IMG, step, 0)
    out[GAP0 + GAPS : R, :] = jnp.zeros((R - GAP0 - GAPS, D), F32)


def to_canvas(src, scr, starts, gaps):
    def step(r, carry):
        for t in range(3):
            for i in range(IMAGES):
                block = src[rows_at(i * IR + r * 16, 16), t * 128 : t * 128 + 128]
                scr[t, pl.ds(r * CW + starts[i], 16), :] = block
            block = src[rows_at(GAP0 + r * 8, 8, 8), t * 128 : t * 128 + 128]
            for k in range(8):
                scr[t, pl.ds(r * CW + gaps[k], 1), :] = block[k : k + 1]
        return carry

    lax.fori_loop(0, IMG, step, 0)


def norm_parts(x):
    mean = jnp.sum(x, -1, keepdims=True) * (1.0 / D)
    centred = x - mean
    var = jnp.sum(centred * centred, -1, keepdims=True) * (1.0 / D)
    rstd = lax.rsqrt(var + EPS)
    return centred * rstd, rstd


def store_shifted(dst, i, t, x):
    lanes = slice(t * 128, t * 128 + 128)
    at = rows_at(i * STRIDE + 16, IR)
    dst[0, at, lanes] = pltpu.roll(x, 1, 0)
    dst[1, at, lanes] = x
    dst[2, at, lanes] = pltpu.roll(x, IR - 1, 0)


def zero_borders(dst):
    for i in range(IMAGES + 1):
        for c in range(3):
            dst[c, i * STRIDE : i * STRIDE + 16, :] = jnp.zeros((16, D), F32)


def first_norm(tokp, gains, shifts, nrm):
    zero_borders(nrm)
    mask = cell_mask(IR)

    def step(i, carry):
        xhat, _ = norm_parts(tokp[rows_at(i * IR, IR), :])
        normed = (xhat * gains[0:1] + shifts[0:1]) * mask
        for t in range(3):
            store_shifted(nrm, i, t, normed[:, t * 128 : t * 128 + 128])
        return carry

    lax.fori_loop(0, IMAGES, step, 0)


CB = 32


def conv_forward(nrm, kernels, conv, stats):
    mask = cell_mask(CB)
    blocks = IMAGES * IR // CB
    per = IR // CB
    for t in range(3):
        lanes = slice(t * 128, t * 128 + 128)
        taps = [[kernels[k, o : o + 1, lanes] for o in range(9)] for k in range(3)]

        def step(b, sums):
            base = (b // per) * STRIDE + 16 + (b % per) * CB
            acc = [jnp.zeros((CB, 128), F32)] * 3
            for o in range(9):
                x = nrm[o % 3, rows_at(base + (o // 3 - 1) * 16, CB), lanes]
                for k in range(3):
                    acc[k] = acc[k] + x * taps[k][o]
            new = []
            for k in range(3):
                conv[k, rows_at(b * CB, CB), lanes] = acc[k]
                new.append(sums[k] + jnp.sum((acc[k] * mask).reshape(CB // 8, 8, 128), 0))
            return tuple(new)

        sums = lax.fori_loop(0, blocks, step, (jnp.zeros((8, 128), F32),) * 3)
        means = [jnp.sum(s, 0, keepdims=True) * (1.0 / (IMAGES * IMG * IMG)) for s in sums]

        def spread(b, sums):
            new = []
            for k in range(3):
                away = (conv[k, rows_at(b * CB, CB), lanes] - means[k]) * mask
                new.append(sums[k] + jnp.sum((away * away).reshape(CB // 8, 8, 128), 0))
            return tuple(new)

        squares = lax.fori_loop(0, blocks, spread, (jnp.zeros((8, 128), F32),) * 3)
        for k in range(3):
            stats[k : k + 1, lanes] = means[k]
            stats[3 + k : 4 + k, lanes] = jnp.sum(squares[k], 0, keepdims=True)
        stats[6:8, lanes] = jnp.zeros((2, 128), F32)
    for k in range(3):
        conv[k, GAP0:R, :] = jnp.zeros((R - GAP0, D), F32)


class Place:
    def __init__(self, groups):
        dp = lax.axis_index("dp")
        self.mp = lax.axis_index("mp")
        self.groups = groups
        self.quad = lax.rem(dp, QUAD)
        self.z = dp // QUAD
        self.slot = self.quad * 2 + self.mp

    def in_eight(self, offset):
        other = lax.rem(self.slot + offset, 8)
        return (self.z * QUAD + other // 2, lax.rem(other, 2))

    def in_quad(self, offset):
        return (self.z * QUAD + lax.rem(self.quad + offset, QUAD), self.mp)

    def along(self, offset):
        return (lax.rem(self.z + offset, self.groups) * QUAD + self.quad, self.mp)

    def other_core(self):
        return (self.z * QUAD + self.quad, 1 - self.mp)

    def peers(self):
        return [self.in_eight(o) for o in range(1, 8)] + [self.along(o) for o in range(1, self.groups)]

    def greet(self):
        barrier = pltpu.get_barrier_semaphore()
        for peer in self.peers():
            pl.semaphore_signal(barrier, inc=1, device_id=peer, device_id_type=MESH)

    def greeted(self):
        pl.semaphore_wait(pltpu.get_barrier_semaphore(), 7 + self.groups - 1)


def remote(src, dst, send, recv, peer):
    copy = pltpu.make_async_remote_copy(
        src_ref=src, dst_ref=dst, send_sem=send, recv_sem=recv, device_id=peer, device_id_type=MESH
    )
    copy.start()
    return copy


def send_eight(place, src, rx, send, recv):
    return [remote(src, rx.at[place.slot], send.at[o], recv.at[o], place.in_eight(o)) for o in range(1, 8)]


def send_along(place, src, rx, send, recv):
    return [remote(src, rx.at[place.z], send.at[o], recv.at[o], place.along(o)) for o in range(1, place.groups)]


def finish(copies):
    for copy in copies:
        copy.wait()


def sum_slots(rx, count):
    total = rx[0]
    for s in range(1, count):
        total = total + rx[s]
    return total


def merge_moments(rx, count, cells):
    mean = sum([rx[s, 0:3] for s in range(1, count)], rx[0, 0:3]) * (1.0 / count)
    m2 = sum([rx[s, 3:6] for s in range(1, count)], rx[0, 3:6])
    for s in range(count):
        away = rx[s, 0:3] - mean
        m2 = m2 + away * away * float(cells)
    return mean, m2


def dma(*n):
    return pltpu.SemaphoreType.DMA(n)


def project(conv, moments, gains, shifts, wqkv, bn, qkv):
    def step(c, carry):
        rows = rows_at(c * CH, CH)
        for k in range(3):
            standard = (conv[k, rows, :] - moments[k : k + 1]) * moments[3 + k : 4 + k]
            value = standard * gains[1 + k : 2 + k]
            if k != 1:
                value = value + (shifts[1:2] if k == 0 else shifts[2:3])
            value = value.astype(BF)
            bn[k, rows, :] = value
            out = dot(value, wqkv[k]).astype(BF)
            if k == 0:
                out = (out * SCALE).astype(BF)
            for p in range(3):
                qkv[k, p, rows, :] = out[:, p * 128 : p * 128 + 128]
        return carry

    lax.fori_loop(0, R // CH, step, 0)


def key_bias():
    row = lax.broadcasted_iota(jnp.int32, (16, 256), 0)
    return jnp.where(row < IMG, 0.0, MASKED)


def query_mask():
    lane = lax.broadcasted_iota(jnp.int32, (1, 256), 1)
    return (lane < IR).astype(F32)


def halves(x):
    lane = lax.broadcasted_iota(jnp.int32, x.shape, 1)
    zero = jnp.zeros_like(x)
    return [jnp.where(lane < 64, x, zero), jnp.where(lane < 64, zero, x)]


def probs_at(pool, n):
    return [rows_at((2 * n + half) * IR, IR) for half in range(2)]


def attend(qkv, pool, att):
    bias = key_bias()[None]
    live = query_mask()

    def step(n, carry):
        i, p = n // 3, lax.rem(n, 3)
        rows = rows_at(i * IR, IR)
        q = qkv[0, p, rows_at(i * IR, 256), :]
        k = qkv[1, p, rows, :]
        v_t = qkv[2, p, rows, :].T
        parts = []
        for h, k_h in enumerate(halves(k)):
            scores = (dot_t(k_h, q).reshape(IMG, 16, 256) + bias).reshape(IR, 256)
            largest = jnp.max(scores, 0, keepdims=True)
            expo = jnp.exp(scores - largest)
            soft = expo * (live / jnp.sum(expo, 0, keepdims=True))
            for half, at in enumerate(probs_at(pool, n * 2 + h)):
                pool[at, :] = soft[:, half * 128 : half * 128 + 128]
            parts.append(dot(v_t[h * 64 : h * 64 + 64], soft.astype(BF)))
        out = jnp.concatenate(parts, 0).T
        att[p, rows, :] = out[:IR].astype(BF)
        return carry

    lax.fori_loop(0, 3 * IMAGES, step, 0)


def even_prob():
    return jnp.full((1, 1), 1.0 / GAPS, F32).astype(BF).astype(F32)


def attend_gap(qkv, att):
    for p in range(3):
        v = qkv[2, p, GAP0 : GAP0 + 16, :].astype(F32)
        out = (v * (even_prob() * float(GAPS))).astype(BF)
        for b in range((R - GAP0) // 16):
            att[p, GAP0 + b * 16 : GAP0 + b * 16 + 16, :] = out


def gelu_parts(x):
    cdf = 0.5 * (1.0 + lax.erf(x * (1.0 / math.sqrt(2.0))))
    density = jnp.exp(x * x * -0.5) * (1.0 / math.sqrt(2.0 * math.pi))
    return x * cdf, cdf + x * density


def col_sum(x):
    return jnp.sum(x, 0, keepdims=True)


def feed_forward_in(tokp, cotp, att, wout, gains, shifts, dres, n2, gm, small):
    small[...] = jnp.zeros((8, D), F32)

    def step(c, carry):
        rows = rows_at(c * CH, CH)
        attended = jnp.concatenate([att[p, rows, :] for p in range(3)], 1)
        residual = tokp[rows, :] + (dot(attended, wout[...]) + shifts[3:4])
        dres[rows, :] = residual
        xhat, _ = norm_parts(residual)
        n2[rows, :] = (xhat * gains[4:5] + shifts[4:5]).astype(BF)
        cot = cotp[rows, :]
        gm[rows, :] = cot.astype(BF)
        small[3:4] = small[3:4] + col_sum(cot)
        return carry

    lax.fori_loop(0, R // CH, step, 0)


def hidden_tile(j, first, n2, gm, win, wmo, bias, act, dpre, outp, acc, small, grads):
    def step(c, carry):
        rows = rows_at(c * CH, CH)
        pre = dot(n2[rows, :], win[j]) + bias[j // 2, j % 2 : j % 2 + 1]
        value, slope = gelu_parts(pre)
        value = value.astype(BF)
        act[rows, :] = value
        grad = dot_t(gm[rows, :], wmo[j]) * slope
        small[4 + j : 5 + j] = small[4 + j : 5 + j] + col_sum(grad)
        grad = grad.astype(BF)
        dpre[rows, :] = grad
        forward = dot(value, wmo[j])
        back = dot_t(grad, win[j])
        outp[rows, :] = forward if first else outp[rows, :] + forward
        acc[rows, :] = back if first else acc[rows, :] + back
        return carry

    lax.fori_loop(0, R // CH, step, 0)
    unit, half = j % 2, j // 2
    grads[unit, half, 0:D, :] = t_dot(n2[...], dpre[...]).astype(BF)
    grads[unit, half, D : 2 * D, :] = t_dot(act[...], gm[...]).astype(BF)


def feed_forward_out(cotp, wout, gains, shifts, outp, acc, dres, gr, datt, small):
    def step(c, carry):
        rows = rows_at(c * CH, CH)
        residual = dres[rows, :]
        outp[rows, :] = residual + outp[rows, :] + shifts[5:6]
        xhat, rstd = norm_parts(residual)
        grad = acc[rows, :]
        scaled = grad * gains[4:5]
        one = jnp.sum(scaled, -1, keepdims=True) * (1.0 / D)
        two = jnp.sum(scaled * xhat, -1, keepdims=True) * (1.0 / D)
        total = cotp[rows, :] + rstd * (scaled - one - xhat * two)
        dres[rows, :] = total
        low = total.astype(BF)
        gr[rows, :] = low
        back = dot_t(low, wout[...]).astype(BF)
        for p in range(3):
            datt[p, rows, :] = back[:, p * 128 : p * 128 + 128]
        small[0:1] = small[0:1] + col_sum(grad * xhat)
        small[1:2] = small[1:2] + col_sum(total)
        small[2:3] = small[2:3] + col_sum(grad)
        return carry

    lax.fori_loop(0, R // CH, step, 0)


def attend_back(p, qkv, pool, datt, dqkv):
    def step(i, carry):
        n = i * 3 + p
        rows = rows_at(i * IR, IR)
        wide = rows_at(i * IR, 256)
        q = qkv[0, p, wide, :]
        k_t = qkv[1, p, rows, :].T
        v = qkv[2, p, rows, :]
        do = datt[p, wide, :]
        dq, dk, dv = [], [], []
        for h, v_h in enumerate(halves(v)):
            soft = jnp.concatenate([pool[at, :] for at in probs_at(pool, n * 2 + h)], 1)
            grad = dot_t(v_h, do)
            delta = jnp.sum(soft * grad, 0, keepdims=True)
            ds = (soft * (grad - delta)).astype(BF)
            dv.append(dot(soft.astype(BF), do))
            dk.append(dot(ds, q))
            dq.append(dot(k_t[h * 64 : h * 64 + 64], ds))
        lane = lax.broadcasted_iota(jnp.int32, (IR, 128), 1)
        dqkv[0, p, rows, :] = (jnp.concatenate(dq, 0).T[:IR] * SCALE).astype(BF)
        dqkv[1, p, rows, :] = jnp.where(lane < 64, dk[0], dk[1]).astype(BF)
        dqkv[2, p, rows, :] = jnp.where(lane < 64, dv[0], dv[1]).astype(BF)
        return carry

    lax.fori_loop(0, IMAGES, step, 0)


def attend_back_gap(datt, dqkv):
    for p in range(3):
        total = col_sum(datt[p, GAP0 : GAP0 + GAPS, :].astype(F32))
        grad = jnp.broadcast_to((total * even_prob()).astype(BF), (16, 128))
        zero = jnp.zeros((16, 128), BF)
        for b in range((R - GAP0) // 16):
            rows = slice(GAP0 + b * 16, GAP0 + b * 16 + 16)
            dqkv[0, p, rows, :] = zero
            dqkv[1, p, rows, :] = zero
            dqkv[2, p, rows, :] = grad if b < GAPS // 16 else zero


def project_back(conv, moments, wqkv, dqkv, dbn, sums):
    sums[...] = jnp.zeros((8, D), F32)

    def step(c, carry):
        rows = rows_at(c * CH, CH)
        for k in range(3):
            grad = jnp.concatenate([dqkv[k, p, rows, :] for p in range(3)], 1)
            back = dot_t(grad, wqkv[k])
            dbn[rows_at(k * R + c * CH, CH), :] = back
            standard = (conv[k, rows, :] - moments[k : k + 1]) * moments[3 + k : 4 + k]
            sums[k : k + 1] = sums[k : k + 1] + col_sum(back)
            sums[3 + k : 4 + k] = sums[3 + k : 4 + k] + col_sum(back * standard)
        return carry

    lax.fori_loop(0, R // CH, step, 0)


def project_grads(bn, dqkv, grads):
    for k in range(3):
        for p in range(3):
            grads[2, k // 2, (k % 2) * D : (k % 2) * D + D, p * 128 : p * 128 + 128] = t_dot(
                bn[k], dqkv[k, p]
            ).astype(BF)


def shifted_at(c, t, row, size):
    return rows_at((c * 3 + t) * CONVR + row, size)


def conv_back_zero(pool):
    for c in range(3):
        for t in range(3):
            for i in range(IMAGES + 1):
                pool[shifted_at(c, t, i * STRIDE, 16), :] = jnp.zeros((16, 128), F32)


def conv_back(k, dbn, conv, moments, sums, gains, nrm, pool, kernels, dn, dker, inverse_total):
    mask = cell_mask(IR)

    def spread(i, carry):
        rows = rows_at(i * IR, IR)
        for t in range(3):
            lanes = slice(t * 128, t * 128 + 128)
            inv = moments[3 + k : 4 + k, lanes]
            standard = (conv[k, rows, lanes] - moments[k : k + 1, lanes]) * inv
            shift = (sums[k : k + 1, lanes] + standard * sums[3 + k : 4 + k, lanes]) * inverse_total
            grad = dbn[rows_at(k * R + i * IR, IR), lanes]
            grad = (gains[1 + k : 2 + k, lanes] * inv) * (grad - mask * shift)
            pool[shifted_at(0, t, i * STRIDE + 16, IR), :] = pltpu.roll(grad, 1, 0)
            pool[shifted_at(1, t, i * STRIDE + 16, IR), :] = grad
            pool[shifted_at(2, t, i * STRIDE + 16, IR), :] = pltpu.roll(grad, IR - 1, 0)
        return carry

    lax.fori_loop(0, IMAGES, spread, 0)
    blocks = IMAGES * IR // CB
    per = IR // CB
    for t in range(3):
        lanes = slice(t * 128, t * 128 + 128)
        taps = [kernels[k, o : o + 1, lanes] for o in range(9)]

        def step(b, sums9):
            base = (b // per) * STRIDE + 16 + (b % per) * CB
            here = nrm[1, rows_at(base, CB), lanes]
            acc = jnp.zeros((CB, 128), F32)
            new = []
            for o in range(9):
                x = pool[shifted_at(2 - o % 3, t, base - (o // 3 - 1) * 16, CB), :]
                acc = acc + x * taps[o]
                new.append(sums9[o] + jnp.sum((x * here).reshape(CB // 8, 8, 128), 0))
            rows = rows_at(b * CB, CB)
            dn[rows, lanes] = acc if k == 0 else dn[rows, lanes] + acc
            return tuple(new)

        sums9 = lax.fori_loop(0, blocks, step, (jnp.zeros((8, 128), F32),) * 9)
        for o in range(9):
            dker[k * 9 + o : k * 9 + o + 1, lanes] = col_sum(sums9[o])


def last_norm_back(tokp, dres, dn, gains, gtok, dker):
    mask = cell_mask(IR)
    dker[27:32] = jnp.zeros((5, D), F32)

    def step(i, carry):
        rows = rows_at(i * IR, IR)
        xhat, rstd = norm_parts(tokp[rows, :])
        grad = dn[rows, :] * mask
        dker[27:28] = dker[27:28] + col_sum(grad * xhat)
        dker[28:29] = dker[28:29] + col_sum(grad)
        scaled = grad * gains[0:1]
        one = jnp.sum(scaled, -1, keepdims=True) * (1.0 / D)
        two = jnp.sum(scaled * xhat, -1, keepdims=True) * (1.0 / D)
        gtok[rows, :] = dres[rows, :] + rstd * (scaled - one - xhat * two)
        return carry

    lax.fori_loop(0, IMAGES, step, 0)
    gtok[GAP0:R, :] = dres[GAP0:R, :]


HALF = 2 * D
QR = HALF // QUAD


class GradSum:
    def __init__(self, place, unit, src, bufs, sems):
        self.place, self.unit, self.src = place, unit, src
        self.rx_core, self.rx_quad, self.mid, self.rx_z = [b.at[unit] for b in bufs[:4]]
        self.done = bufs[4]
        self.at = unit if unit < 2 else 2 + place.mp
        self.own = src.at[unit, place.mp]
        self.send, self.recv = sems[0].at[unit], sems[1].at[unit]
        self.groups = place.groups
        self.part = -(-QR // (16 * self.groups)) * 16
        self.span = self.part * self.groups

    def core_start(self):
        mine = self.src.at[self.unit, 1 - self.place.mp]
        self.copies = [remote(mine, self.rx_core, self.send.at[0], self.recv.at[0], self.place.other_core())]

    def core_end(self):
        finish(self.copies)
        for b in range(HALF // 64):
            rows = slice(b * 64, b * 64 + 64)
            mine = self.own[rows, :].astype(F32)
            self.own[rows, :] = (mine + self.rx_core[rows, :].astype(F32)).astype(BF)

    def quad_start(self):
        self.copies = []
        for o in range(1, QUAD):
            rows = rows_at(lax.rem(self.place.quad + o, QUAD) * QR, QR)
            self.copies.append(
                remote(self.own.at[rows], self.rx_quad.at[o - 1], self.send.at[o], self.recv.at[o], self.place.in_quad(o))
            )

    def quad_end(self):
        finish(self.copies)
        for b in range(QR // 64):
            rows = slice(b * 64, b * 64 + 64)
            total = self.own[rows_at(self.place.quad * QR + b * 64, 64), :].astype(F32)
            for o in range(QUAD - 1):
                total = total + self.rx_quad[o, rows, :].astype(F32)
            self.mid[rows, :] = total.astype(BF)
        if self.span > QR:
            self.mid[QR:, :] = jnp.zeros((self.span - QR, D), BF)

    def z_start(self):
        self.copies = []
        for o in range(1, self.groups):
            rows = rows_at(lax.rem(self.place.z + o, self.groups) * self.part, self.part)
            at = 3 + o
            self.copies.append(
                remote(self.mid.at[rows], self.rx_z.at[o - 1], self.send.at[at], self.recv.at[at], self.place.along(o))
            )

    def z_end(self):
        finish(self.copies)
        total = self.mid[rows_at(self.place.z * self.part, self.part), :].astype(F32)
        for o in range(self.groups - 1):
            total = total + self.rx_z[o].astype(F32)
        self.done[self.at, self.place.quad, rows_at(self.place.z * self.part, self.part), :] = total.astype(BF)

    def z_back_start(self):
        here = self.done.at[self.at, self.place.quad, rows_at(self.place.z * self.part, self.part)]
        self.copies = []
        for o in range(1, self.groups):
            at = 2 + self.groups + o
            self.copies.append(remote(here, here, self.send.at[at], self.recv.at[at], self.place.along(o)))

    def quad_back_start(self):
        here = self.done.at[self.at, self.place.quad]
        self.copies = []
        for o in range(1, QUAD):
            at = 1 + 2 * self.groups + o
            self.copies.append(remote(here, here, self.send.at[at], self.recv.at[at], self.place.in_quad(o)))

    def core_back_start(self):
        here = self.done.at[self.at]
        at = 1 + 2 * self.groups + QUAD
        self.copies = [remote(here, here, self.send.at[at], self.recv.at[at], self.place.other_core())]

    def end(self):
        finish(self.copies)


    def store(self, out, sem):
        copies = []
        for n in (2, 3) if self.unit == 2 else (self.unit,):
            for q in range(QUAD):
                copy = pltpu.make_async_copy(self.done.at[n, q, pl.ds(0, QR)], out.at[n, q], sem.at[n, q])
                copy.start()
                copies.append(copy)
        return copies


def grad_buffers(groups):
    part = -(-QR // (16 * groups)) * 16
    return [
        pltpu.VMEM((3, HALF, D), BF),
        pltpu.VMEM((3, QUAD - 1, QR, D), BF),
        pltpu.VMEM((3, part * groups, D), BF),
        pltpu.VMEM((3, groups - 1, part, D), BF),
        pltpu.VMEM((4, QUAD, part * groups, D), BF),
    ]


def main_kernel(
    groups, seg, tokens, cot, gains, shifts, kernels, wqkv, wout, win, wmo, bias_h,
    out_hbm, gtok_hbm, dw_hbm, rest_out, sums_out,
    pool, tokp, cotp, conv, nrm, dbn, outp, dres, bn, qkv, att, n2, gm, gr, act, dpre, datt, dqkv,
    wqkv_b, wout_b, win_f, wmo_f, bias_f, stats, moments, sums, small, rest,
    grads, b0, b1, b2, b3, b4, rx1, rx2, rx3, rx4, rx5, rx6,
    in_sems, w_sems, pair_s, pair_r, pair_l, es, er, zs, zr, gs, gr_sem, out_sems, dw_sems,
):
    place = Place(groups)
    place.greet()
    copies = []
    for n, src in enumerate((tokens, cot)):
        for t in range(3):
            copy = pltpu.make_async_copy(
                src.at[0, :, pl.ds(t * 128, 128)], pool.at[pl.ds((n * 3 + t) * SCR, CELLS)], in_sems.at[n, t]
            )
            copy.start()
            copies.append(copy)
    ahead = empty_before(seg)
    finish(copies)
    to_images(pool, 0, tokp, ahead)
    to_images(pool, 3 * SCR, cotp, ahead)
    blocks = [wqkv.at[:, pl.ds(k * D, D)] for k in range(3)] + [wout]
    blocks += [win.at[:, pl.ds(j * D, D)] for j in range(2)] + [wmo.at[pl.ds(j * D, D)] for j in range(2)]
    weights = []
    for n, src in enumerate(blocks):
        copy = pltpu.make_async_copy(src, dbn.at[pl.ds(n * D, D)], w_sems.at[n])
        copy.start()
        weights.append(copy)
    first_norm(tokp, gains, shifts, nrm)
    conv_forward(nrm, kernels, conv, stats)
    place.greeted()

    cells = IMAGES * IMG * IMG
    copies = send_eight(place, stats, rx1, es.at[0], er.at[0])
    rx1[place.slot] = stats[...]
    finish(weights)
    targets = [wqkv_b.at[k] for k in range(3)] + [wout_b]
    targets += [win_f.at[place.mp * 2 + j] for j in range(2)] + [wmo_f.at[place.mp * 2 + j] for j in range(2)]
    for n, dst in enumerate(targets):
        dst[...] = dbn[n * D : n * D + D, :].astype(BF)
    mine = pl.ds(place.mp * 2, 2)
    pairs = [
        remote(ref.at[mine], ref.at[mine], pair_s.at[n], pair_r.at[n], place.other_core())
        for n, ref in enumerate((win_f, wmo_f))
    ]
    pairs.append(remote(bias_h, bias_f.at[place.mp], pair_s.at[2], pair_r.at[2], place.other_core()))
    bias_f[place.mp] = bias_h[...]
    finish(copies)
    mean, m2 = merge_moments(rx1, 8, cells)
    rx2[place.z, 0:3] = mean
    rx2[place.z, 3:6] = m2
    rx2[place.z, 6:8] = jnp.zeros((2, D), F32)
    copies = send_along(place, rx2.at[place.z], rx2, zs.at[0], zr.at[0])
    finish(copies)
    mean, m2 = merge_moments(rx2, groups, 8 * cells)
    moments[0:3] = mean
    moments[3:6] = lax.rsqrt(m2 * (1.0 / (cells * 8 * groups)) + EPS)
    moments[6:8] = jnp.zeros((2, D), F32)

    project(conv, moments, gains, shifts, wqkv_b, bn, qkv)
    attend(qkv, pool, att)
    attend_gap(qkv, att)
    feed_forward_in(tokp, cotp, att, wout_b, gains, shifts, dres, n2, gm, small)
    finish(pairs)

    units = [GradSum(place, u, grads, (b0, b1, b2, b3, b4), (gs, gr_sem)) for u in range(3)]
    acc = dbn.at[pl.ds(0, R)]

    def hidden(j, first=False):
        hidden_tile(j, first, n2, gm, win_f, wmo_f, bias_f, act, dpre, outp, acc, small, grads)

    hidden(0, True)
    hidden(2)
    units[0].core_start()
    hidden(1)
    units[0].core_end()
    units[0].quad_start()
    hidden(3)
    units[1].core_start()
    feed_forward_out(cotp, wout_b, gains, shifts, outp, acc, dres, gr, datt, small)
    stores = [pltpu.make_async_copy(outp, out_hbm, out_sems.at[0])]
    stores[0].start()
    for p in range(3):
        grads[2, 1, D + p * 128 : D + p * 128 + 128, :] = t_dot(att[p], gr[...]).astype(BF)
    units[1].core_end()
    units[1].quad_start()
    attend_back_gap(datt, dqkv)
    attend_back(0, qkv, pool, datt, dqkv)
    units[0].quad_end()
    units[0].z_start()
    attend_back(1, qkv, pool, datt, dqkv)
    units[0].z_end()
    units[0].z_back_start()
    attend_back(2, qkv, pool, datt, dqkv)
    units[1].quad_end()
    units[1].z_start()
    project_back(conv, moments, wqkv_b, dqkv, dbn, sums)
    copies = send_eight(place, sums, rx3, es.at[1], er.at[1])
    rx3[place.slot] = sums[...]
    units[0].end()
    units[0].quad_back_start()
    project_grads(bn, dqkv, grads)
    units[2].core_start()
    finish(copies)
    rx4[place.z] = sum_slots(rx3, 8)
    copies = send_along(place, rx4.at[place.z], rx4, zs.at[1], zr.at[1])
    units[1].z_end()
    units[1].z_back_start()
    conv_back_zero(pool)
    units[2].core_end()
    units[2].quad_start()
    finish(copies)
    sums[...] = sum_slots(rx4, groups)
    sums_out[...] = sums[...]

    def back(k):
        conv_back(
            k, dbn, conv, moments, sums, gains, nrm, pool, kernels, cotp, rest, 1.0 / (cells * 8 * groups)
        )

    back(0)
    units[1].end()
    units[1].quad_back_start()
    back(1)
    units[2].quad_end()
    units[2].z_start()
    back(2)
    units[2].z_end()
    units[2].z_back_start()
    last_norm_back(tokp, dres, cotp, gains, outp_free(stores, outp), rest)
    rest[32:40] = small[...]
    copies = send_eight(place, rest, rx5, es.at[2], er.at[2])
    stores.append(pltpu.make_async_copy(outp, gtok_hbm, out_sems.at[1]))
    stores[-1].start()
    rx5[place.slot] = rest[...]
    units[2].end()
    units[2].quad_back_start()
    finish(copies)
    rx6[place.z] = sum_slots(rx5, 8)
    copies = send_along(place, rx6.at[place.z], rx6, zs.at[2], zr.at[2])
    units[0].end()
    stores += units[0].store(dw_hbm, dw_sems)
    units[1].end()
    stores += units[1].store(dw_hbm, dw_sems)
    finish(copies)
    rest[...] = sum_slots(rx6, groups)
    rest_out[0:36] = rest[0:36]
    rest_out[36:38] = jnp.where(place.mp == 0, rest[36:38], rest[38:40])
    rest_out[38:40] = jnp.zeros((2, D), F32)
    units[2].end()
    units[2].core_back_start()
    units[2].end()
    stores += units[2].store(dw_hbm, dw_sems)
    finish(stores[1:])


def outp_free(stores, outp):
    stores[0].wait()
    return outp


def main_call(groups, *args):
    n = 2 + 2 * groups + QUAD
    return pl.pallas_call(
        functools.partial(main_kernel, groups),
        out_shape=(
            shape(R, D), shape(R, D), shape(4, QUAD, QR, D, dtype=BF), shape(40, D), shape(8, D),
        ),
        in_specs=[VM, ANY, ANY, VM, VM, VM, ANY, ANY, ANY, ANY, VM],
        out_specs=(ANY, ANY, ANY, VM, VM),
        scratch_shapes=[
            pltpu.VMEM((POOL, 128), F32),
            pltpu.VMEM((R, D), F32), pltpu.VMEM((R, D), F32), pltpu.VMEM((3, R, D), F32),
            pltpu.VMEM((3, CONVR, D), F32), pltpu.VMEM((3 * R, D), F32),
            pltpu.VMEM((R, D), F32), pltpu.VMEM((R, D), F32),
            pltpu.VMEM((3, R, D), BF), pltpu.VMEM((3, 3, R, 128), BF), pltpu.VMEM((3, R, 128), BF),
            pltpu.VMEM((R, D), BF), pltpu.VMEM((R, D), BF), pltpu.VMEM((R, D), BF),
            pltpu.VMEM((R, D), BF), pltpu.VMEM((R, D), BF), pltpu.VMEM((3, R, 128), BF), pltpu.VMEM((3, 3, R, 128), BF),
            pltpu.VMEM((3, D, D), BF), pltpu.VMEM((D, D), BF), pltpu.VMEM((4, D, D), BF), pltpu.VMEM((4, D, D), BF),
            pltpu.VMEM((2, 8, D), F32),
            pltpu.VMEM((8, D), F32), pltpu.VMEM((8, D), F32), pltpu.VMEM((8, D), F32), pltpu.VMEM((8, D), F32),
            pltpu.VMEM((40, D), F32),
            pltpu.VMEM((3, 2, HALF, D), BF),
        ] + grad_buffers(groups) + [
            pltpu.VMEM((8, 8, D), F32), pltpu.VMEM((groups, 8, D), F32),
            pltpu.VMEM((8, 8, D), F32), pltpu.VMEM((groups, 8, D), F32),
            pltpu.VMEM((8, 40, D), F32), pltpu.VMEM((groups, 40, D), F32),
            dma(2, 3), dma(8), dma(3), dma(3), dma(2), dma(3, 8), dma(3, 8), dma(3, groups), dma(3, groups),
            dma(3, n), dma(3, n), dma(2), dma(4, QUAD),
        ],
        compiler_params=params(collective_id=0, has_side_effects=True),
    )(*args)


def last_kernel(
    seg, outp, gtok, dw, rest, sums,
    output, grad_tokens, grad_gains, grad_shifts, grad_kernels, grad_qkv, grad_out, grad_in, grad_bias, grad_down,
    scr,
):
    starts, gaps = find_columns(seg)
    for src, dst in ((outp, output), (gtok, grad_tokens)):
        to_canvas(src, scr, starts, gaps)
        for t in range(3):
            dst[0, :, t * 128 : t * 128 + 128] = scr[t, 0:CELLS, :]
    for u in range(2):
        grad_in[:, u * D : u * D + D] = dw[u, 0:D, :].astype(F32)
        grad_down[u * D : u * D + D, :] = dw[u, D : 2 * D, :].astype(F32)
    for k in range(3):
        grad_qkv[:, k * D : k * D + D] = dw[2 + k // 2, (k % 2) * D : (k % 2) * D + D, :].astype(F32)
        grad_kernels[k] = rest[k * 9 : k * 9 + 9]
    grad_out[...] = dw[3, D : 2 * D, :].astype(F32)
    grad_gains[0:1] = rest[27:28]
    grad_gains[1:4] = sums[3:6]
    grad_gains[4:5] = rest[32:33]
    grad_shifts[0:1] = rest[28:29]
    grad_shifts[1:2] = sums[0:1]
    grad_shifts[2:3] = sums[2:3]
    grad_shifts[3:4] = rest[33:34]
    grad_shifts[4:5] = rest[34:35]
    grad_shifts[5:6] = rest[35:36]
    grad_bias[...] = rest[36:38]


def last_call(*args):
    return pl.pallas_call(
        last_kernel,
        out_shape=(
            shape(1, CELLS, D), shape(1, CELLS, D), shape(5, D), shape(6, D), shape(3, 9, D), shape(D, 3 * D),
            shape(D, D), shape(D, 2 * D), shape(2, D), shape(2 * D, D),
        ),
        in_specs=[SM] + [VM] * 5,
        out_specs=(VM,) * 10,
        scratch_shapes=[pltpu.VMEM((3, CELLS + 16, 128), F32)],
        compiler_params=params(),
    )(*args)


def local(
    groups, tokens, segment_ids, gains, shifts, kernels, qkv_weight, out_weight,
    mlp_in_weight, mlp_in_bias, mlp_out_weight, cotangent,
):
    bias_h = jnp.pad(mlp_in_bias.reshape(2, D), ((0, 6), (0, 0)))
    outp, gtok, dw, rest, sums = main_call(
        groups, segment_ids, tokens, cotangent, gains, shifts, kernels,
        qkv_weight, out_weight, mlp_in_weight, mlp_out_weight, bias_h,
    )
    outs = list(last_call(segment_ids, outp, gtok, dw.reshape(4, HALF, D), rest, sums))
    outs[8] = outs[8].reshape(2 * D)
    return tuple(outs)


def solution(mesh):
    groups = mesh.shape["dp"] // QUAD
    both = P(("dp", "mp"), None, None)
    return jax.shard_map(
        functools.partial(local, groups),
        mesh=mesh,
        in_specs=(
            both, P(("dp", "mp"), None), P(), P(), P(), P(), P(), P(None, "mp"), P("mp"), P("mp", None), both,
        ),
        out_specs=(both, both, P(), P(), P(), P(), P(), P(None, "mp"), P("mp"), P("mp", None)),
        check_vma=False,
    )
```

```python
import functools
import math

import jax
import jax.numpy as jnp
from jax import lax
from jax.experimental import pallas as pl
from jax.experimental.pallas import tpu as pltpu
from jax.sharding import PartitionSpec as P

F32 = jnp.float32
BF = jnp.bfloat16
MESH = pl.DeviceIdType.MESH
D = 384
IMG = 14
IMAGES = 4
CW = 64
CELLS = IMG * CW
IR = 224
GAP0 = IMAGES * IR
GAPS = 112
R = 1024
CH = 256
STRIDE = IR + 16
CONVR = IMAGES * STRIDE + 16
EPS = 1e-05
MASKED = -1e30
QUAD = 4
HH = 2 * D
VLIM = 62 * 2**20
SCALE = 0.125
PCH = 512


def params(**kw):
    return pltpu.CompilerParams(vmem_limit_bytes=VLIM, **kw)


VM = pl.BlockSpec(memory_space=pltpu.VMEM)
SM = pl.BlockSpec(memory_space=pltpu.SMEM)
ANY = pl.BlockSpec(memory_space=pl.ANY)


def shape(*dims, dtype=F32):
    return jax.ShapeDtypeStruct(dims, dtype)


def dot(a, b):
    return jnp.dot(a, b, preferred_element_type=F32)


def dot_t(a, b):
    return lax.dot_general(a, b, (((1,), (1,)), ((), ())), preferred_element_type=F32)


def t_dot(a, b):
    return lax.dot_general(a, b, (((0,), (0,)), ((), ())), preferred_element_type=F32)


def cell_mask(rows):
    row = lax.broadcasted_iota(jnp.int32, (rows, 1), 0)
    return (row % 16 < IMG).astype(F32)


def rows_at(start, size, align=16):
    return pl.ds(pl.multiple_of(start, align), size)


def find_columns(seg):
    def step(col, found):
        count, starts, gaps = found
        here = seg[0, col]
        starts = tuple(jnp.minimum(s, jnp.where(here == i + 1, col, CW)) for i, s in enumerate(starts))
        empty = here == 0
        gaps = tuple(jnp.where(empty & (count == k), col, g) for k, g in enumerate(gaps))
        return count + jnp.where(empty, 1, 0), starts, gaps

    start = (jnp.int32(0), (jnp.int32(CW),) * IMAGES, (jnp.int32(0),) * 8)
    _, starts, gaps = lax.fori_loop(0, CW, step, start)
    return starts, gaps


SCR = CELLS + 16
POOL = 48 * IR


def empty_before(seg):
    lane = lax.broadcasted_iota(jnp.int32, (1, 128), 1)
    ids = seg[0:1, 0:128]
    firsts = [jnp.where((ids == i + 1) & (lane < CW), lane, CW).astype(F32) for i in range(IMAGES)]
    return [jnp.min(f, -1, keepdims=True) - float(i * IMG) for i, f in enumerate(firsts)]


def to_images(pool, base, out, ahead):
    col = lax.broadcasted_iota(jnp.int32, (16, 128), 0)
    sub = lax.broadcasted_iota(jnp.int32, (8, 128), 0).astype(F32)
    before = sum([jnp.where(a <= sub, 1.0, 0.0) for a in ahead])

    def step(r, carry):
        for t in range(3):
            row = base + t * SCR + r * CW
            for i in range(IMAGES):
                window = pool[pl.ds(row + i * IMG, 16), :]
                for e in range(1, 9):
                    moved = pool[pl.ds(row + i * IMG + e, 16), :]
                    window = jnp.where(ahead[i] == float(e), moved, window)
                out[rows_at(i * IR + r * 16, 16), t * 128 : t * 128 + 128] = jnp.where(col < IMG, window, 0.0)
            block = pool[rows_at(row, 8, 8), :]
            for n in range(1, IMAGES + 1):
                block = jnp.where(before == float(n), pool[pl.ds(row + n * IMG, 8), :], block)
            out[rows_at(GAP0 + r * 8, 8, 8), t * 128 : t * 128 + 128] = block
        return carry

    lax.fori_loop(0, IMG, step, 0)
    out[GAP0 + GAPS : R, :] = jnp.zeros((R - GAP0 - GAPS, D), F32)


def to_canvas(src, scr, starts, gaps):
    def step(r, carry):
        for t in range(3):
            for i in range(IMAGES):
                block = src[rows_at(i * IR + r * 16, 16), t * 128 : t * 128 + 128]
                scr[t, pl.ds(r * CW + starts[i], 16), :] = block
            block = src[rows_at(GAP0 + r * 8, 8, 8), t * 128 : t * 128 + 128]
            for k in range(8):
                scr[t, pl.ds(r * CW + gaps[k], 1), :] = block[k : k + 1]
        return carry

    lax.fori_loop(0, IMG, step, 0)


def norm_parts(x):
    mean = jnp.sum(x, -1, keepdims=True) * (1.0 / D)
    centred = x - mean
    var = jnp.sum(centred * centred, -1, keepdims=True) * (1.0 / D)
    rstd = lax.rsqrt(var + EPS)
    return centred * rstd, rstd


def store_shifted(dst, i, t, x):
    lanes = slice(t * 128, t * 128 + 128)
    at = rows_at(i * STRIDE + 16, IR)
    dst[0, at, lanes] = pltpu.roll(x, 1, 0)
    dst[1, at, lanes] = x
    dst[2, at, lanes] = pltpu.roll(x, IR - 1, 0)


def zero_borders(dst):
    for i in range(IMAGES + 1):
        for c in range(3):
            dst[c, i * STRIDE : i * STRIDE + 16, :] = jnp.zeros((16, D), F32)


def first_norm(tokp, gains, shifts, nrm):
    zero_borders(nrm)
    mask = cell_mask(IR)

    def step(i, carry):
        xhat, _ = norm_parts(tokp[rows_at(i * IR, IR), :])
        normed = (xhat * gains[0:1] + shifts[0:1]) * mask
        for t in range(3):
            store_shifted(nrm, i, t, normed[:, t * 128 : t * 128 + 128])
        return carry

    lax.fori_loop(0, IMAGES, step, 0)


CB = 224


def conv_forward(nrm, kernels, conv, stats):
    mask = cell_mask(CB)
    blocks = IMAGES * IR // CB
    per = IR // CB
    for t in range(3):
        lanes = slice(t * 128, t * 128 + 128)
        taps = [[kernels[o, k : k + 1, lanes] for o in range(9)] for k in range(3)]

        def step(b, sums):
            base = (b // per) * STRIDE + 16 + (b % per) * CB
            acc = [jnp.zeros((CB, 128), F32)] * 3
            for o in range(9):
                x = nrm[o % 3, rows_at(base + (o // 3 - 1) * 16, CB), lanes]
                for k in range(3):
                    acc[k] = acc[k] + x * taps[k][o]
            new = []
            for k in range(3):
                conv[k, rows_at(b * CB, CB), lanes] = acc[k]
                new.append(sums[k] + jnp.sum((acc[k] * mask).reshape(CB // 8, 8, 128), 0))
            return tuple(new)

        sums = lax.fori_loop(0, blocks, step, (jnp.zeros((8, 128), F32),) * 3)
        means = [jnp.sum(s, 0, keepdims=True) * (1.0 / (IMAGES * IMG * IMG)) for s in sums]

        def spread(b, sums):
            new = []
            for k in range(3):
                away = (conv[k, rows_at(b * CB, CB), lanes] - means[k]) * mask
                new.append(sums[k] + jnp.sum((away * away).reshape(CB // 8, 8, 128), 0))
            return tuple(new)

        squares = lax.fori_loop(0, blocks, spread, (jnp.zeros((8, 128), F32),) * 3)
        for k in range(3):
            stats[k : k + 1, lanes] = means[k]
            stats[3 + k : 4 + k, lanes] = jnp.sum(squares[k], 0, keepdims=True)
        stats[6:8, lanes] = jnp.zeros((2, 128), F32)
    for k in range(3):
        conv[k, GAP0:R, :] = jnp.zeros((R - GAP0, D), F32)


class Place:
    def __init__(self, groups):
        dp = lax.axis_index("dp")
        self.mp = lax.axis_index("mp")
        self.groups = groups
        self.quad = lax.rem(dp, QUAD)
        self.z = dp // QUAD
        self.slot = self.quad * 2 + self.mp

    def in_eight(self, offset):
        other = lax.rem(self.slot + offset, 8)
        return (self.z * QUAD + other // 2, lax.rem(other, 2))

    def in_quad(self, offset):
        return (self.z * QUAD + lax.rem(self.quad + offset, QUAD), self.mp)

    def along(self, offset):
        return (lax.rem(self.z + offset, self.groups) * QUAD + self.quad, self.mp)

    def other_core(self):
        return (self.z * QUAD + self.quad, 1 - self.mp)

    def peers(self):
        return [self.in_eight(o) for o in range(1, 8)] + [self.along(o) for o in range(1, self.groups)]

    def greet(self):
        barrier = pltpu.get_barrier_semaphore()
        for peer in self.peers():
            pl.semaphore_signal(barrier, inc=1, device_id=peer, device_id_type=MESH)

    def greeted(self):
        pl.semaphore_wait(pltpu.get_barrier_semaphore(), 7 + self.groups - 1)


def remote(src, dst, send, recv, peer):
    copy = pltpu.make_async_remote_copy(
        src_ref=src, dst_ref=dst, send_sem=send, recv_sem=recv, device_id=peer, device_id_type=MESH
    )
    copy.start()
    return copy


def send_eight(place, src, rx, send, recv):
    for o in range(1, 8):
        remote(src, rx.at[place.slot], send, recv, place.in_eight(o))
    return Pending(rx.at[pl.ds(0, 7)], send, recv)


def send_along(place, src, rx, send, recv):
    for o in range(1, place.groups):
        remote(src, rx.at[place.z], send, recv, place.along(o))
    return Pending(rx.at[pl.ds(0, place.groups - 1)], send, recv)


class Pending:
    def __init__(self, ref, send, recv):
        self.ref, self.sems = ref, (send, recv)

    def wait(self):
        for sem in self.sems:
            pltpu.make_async_copy(self.ref, self.ref, sem).wait()


def finish(copies):
    for copy in copies if isinstance(copies, list) else [copies]:
        copy.wait()


def sum_slots(rx, count):
    total = rx[0]
    for s in range(1, count):
        total = total + rx[s]
    return total


class SmallSum:
    def __init__(self, place, src, rx1, rx2, sems, n, done):
        self.place, self.src, self.rx1, self.rx2, self.done = place, src, rx1, rx2, done
        self.sems = [sems.at[n, i] for i in range(3)]
        self.steps = [self.middle, self.end]

    def start(self):
        self.copies = send_eight(self.place, self.src, self.rx1, self.sems[0], self.sems[1])
        self.rx1[self.place.slot] = self.src[...]

    def step(self):
        self.steps.pop(0)()

    def middle(self):
        finish(self.copies)
        self.rx2[self.place.z] = sum_slots(self.rx1, 8)
        self.copies = send_along(self.place, self.rx2.at[self.place.z], self.rx2, self.sems[0], self.sems[2])

    def end(self):
        finish(self.copies)
        self.done(sum_slots(self.rx2, self.place.groups))


def merge_moments(rx, count, cells):
    mean = sum([rx[s, 0:3] for s in range(1, count)], rx[0, 0:3]) * (1.0 / count)
    m2 = sum([rx[s, 3:6] for s in range(1, count)], rx[0, 3:6])
    for s in range(count):
        away = rx[s, 0:3] - mean
        m2 = m2 + away * away * float(cells)
    return mean, m2


def dma(*n):
    return pltpu.SemaphoreType.DMA(n)


def project(conv, moments, gains, shifts, wqkv, bn, qkv):
    def step(c, carry):
        rows = rows_at(c * CH, CH)
        for k in range(3):
            standard = (conv[k, rows, :] - moments[k : k + 1]) * moments[3 + k : 4 + k]
            value = standard * gains[1 + k : 2 + k]
            if k != 1:
                value = value + (shifts[1:2] if k == 0 else shifts[2:3])
            value = value.astype(BF)
            bn[k, rows, :] = value
            out = dot(value, wqkv[k]).astype(BF)
            if k == 0:
                out = (out * SCALE).astype(BF)
            for p in range(3):
                qkv[k, p, rows, :] = out[:, p * 128 : p * 128 + 128]
        return carry

    lax.fori_loop(0, R // CH, step, 0)


def key_bias():
    row = lax.broadcasted_iota(jnp.int32, (16, 256), 0)
    return jnp.where(row < IMG, 0.0, MASKED)


def query_mask():
    lane = lax.broadcasted_iota(jnp.int32, (1, 256), 1)
    return (lane < IR).astype(F32)


def by_head(x):
    lane = lax.broadcasted_iota(jnp.int32, x.shape, 1)
    zero = jnp.zeros_like(x)
    return jnp.concatenate([jnp.where(lane < 64, x, zero), jnp.where(lane < 64, zero, x)], 0)


def own_columns(x, rows):
    lane = lax.broadcasted_iota(jnp.int32, (IR, 128), 1)
    return jnp.where(lane < 64, x[:IR], x[rows : rows + IR])


def probs_at(pool, n):
    return [rows_at((2 * n + half) * IR, IR) for half in range(2)]


def attend(qkv, pool, att):
    bias = key_bias()[None]
    live = query_mask()

    def step(i, carry):
        rows = rows_at(i * IR, IR)
        for p in range(3):
            q = qkv[0, p, rows_at(i * IR, 256), :]
            both = dot_t(by_head(qkv[1, p, rows, :]), q)
            low = []
            for h in range(2):
                scores = (both[h * IR : h * IR + IR].reshape(IMG, 16, 256) + bias).reshape(IR, 256)
                largest = jnp.max(scores, 0, keepdims=True)
                expo = jnp.exp(scores - largest)
                soft = expo * (live / jnp.sum(expo, 0, keepdims=True))
                for half, at in enumerate(probs_at(pool, (i * 3 + p) * 2 + h)):
                    pool[at, :] = soft[:, half * 128 : half * 128 + 128]
                low.append(soft.astype(BF))
            out = t_dot(jnp.concatenate(low, 1), qkv[2, p, rows, :])
            att[p, rows, :] = own_columns(out, 256).astype(BF)
        return carry

    lax.fori_loop(0, IMAGES, step, 0)


def even_prob():
    return jnp.full((1, 1), 1.0 / GAPS, F32).astype(BF).astype(F32)


def attend_gap(qkv, att):
    for p in range(3):
        v = qkv[2, p, GAP0 : GAP0 + 16, :].astype(F32)
        out = (v * (even_prob() * float(GAPS))).astype(BF)
        for b in range((R - GAP0) // 16):
            att[p, GAP0 + b * 16 : GAP0 + b * 16 + 16, :] = out


def gelu_parts(x):
    cdf = 0.5 * (1.0 + lax.erf(x * (1.0 / math.sqrt(2.0))))
    density = jnp.exp(x * x * -0.5) * (1.0 / math.sqrt(2.0 * math.pi))
    return x * cdf, cdf + x * density


def col_sum(x):
    return jnp.sum(x, 0, keepdims=True)


def feed_forward_in(tokp, cotp, att, wout, gains, shifts, dres, n2, gm, small):
    small[...] = jnp.zeros((8, D), F32)

    def step(c, carry):
        rows = rows_at(c * CH, CH)
        attended = jnp.concatenate([att[p, rows, :] for p in range(3)], 1)
        residual = tokp[rows, :] + (dot(attended, wout[...]) + shifts[3:4])
        dres[rows, :] = residual
        xhat, _ = norm_parts(residual)
        n2[rows, :] = (xhat * gains[4:5] + shifts[4:5]).astype(BF)
        cot = cotp[rows, :]
        gm[rows, :] = cot.astype(BF)
        small[3:4] = small[3:4] + col_sum(cot)
        return carry

    lax.fori_loop(0, R // CH, step, 0)


HCH = 512
PARTS = 3
PW = HH // PARTS
BIAS_TILES = 2 * HH // 128


def hidden_part(part, n2, gm, win, wmo, bias, act, dpre, outp, acc, dbias):
    both = slice(0, 2 * PW)
    dbias[part, 0:1, :] = jnp.zeros((1, 2 * PW), F32)

    def step(c, carry):
        rows = rows_at(c * HCH, HCH)
        up = jnp.concatenate([win[part, h] for h in range(2)], 1)
        down = wmo[part].reshape(2 * PW, D)
        shift = jnp.concatenate([bias[h, 0:1, part * PW : part * PW + PW] for h in range(2)], 1)
        value, slope = gelu_parts(dot(n2[rows, :], up) + shift)
        value = value.astype(BF)
        act[rows, both] = value
        grad = dot_t(gm[rows, :], down) * slope
        dbias[part, 0:1, both] = dbias[part, 0:1, both] + col_sum(grad)
        grad = grad.astype(BF)
        dpre[rows, both] = grad
        forward = dot(value, down)
        back = dot_t(grad, up)
        outp[rows, :] = forward if part == 0 else outp[rows, :] + forward
        acc[rows, :] = back if part == 0 else acc[rows, :] + back
        return carry

    lax.fori_loop(0, R // HCH, step, 0)


def hidden_grads(half, n2, gm, act, dpre, grads):
    units = pl.ds(pl.multiple_of(half * PW, 128), PW)
    grads[half, 0:PW, :] = t_dot(dpre[:, units], n2[...]).astype(BF)
    grads[half, PW : 2 * PW, :] = t_dot(act[:, units], gm[...]).astype(BF)


def feed_forward_out(cotp, wout, gains, shifts, outp, acc, dres, gr, datt, small):
    def step(c, carry):
        rows = rows_at(c * CH, CH)
        residual = dres[rows, :]
        outp[rows, :] = residual + outp[rows, :] + shifts[5:6]
        xhat, rstd = norm_parts(residual)
        grad = acc[rows, :]
        scaled = grad * gains[4:5]
        one = jnp.sum(scaled, -1, keepdims=True) * (1.0 / D)
        two = jnp.sum(scaled * xhat, -1, keepdims=True) * (1.0 / D)
        total = cotp[rows, :] + rstd * (scaled - one - xhat * two)
        dres[rows, :] = total
        low = total.astype(BF)
        gr[rows, :] = low
        back = dot_t(low, wout[...]).astype(BF)
        for p in range(3):
            datt[p, rows, :] = back[:, p * 128 : p * 128 + 128]
        small[0:1] = small[0:1] + col_sum(grad * xhat)
        small[1:2] = small[1:2] + col_sum(total)
        small[2:3] = small[2:3] + col_sum(grad)
        return carry

    lax.fori_loop(0, R // CH, step, 0)


def attend_back_values(pool, datt, dqkv):
    def step(i, carry):
        rows = rows_at(i * IR, IR)
        for p in range(3):
            low = []
            for h in range(2):
                soft = [pool[at, :] for at in probs_at(pool, (i * 3 + p) * 2 + h)]
                low.append(jnp.concatenate(soft, 1).astype(BF))
            dv = dot(jnp.concatenate(low, 0), datt[p, rows_at(i * IR, 256), :])
            dqkv[2, p, rows, :] = own_columns(dv, IR).astype(BF)
        return carry

    lax.fori_loop(0, IMAGES, step, 0)


def attend_back(first, last, qkv, pool, datt, dqkv):
    def step(i, carry):
        rows = rows_at(i * IR, IR)
        wide = rows_at(i * IR, 256)
        for p in range(3):
            both = dot_t(by_head(qkv[2, p, rows, :]), datt[p, wide, :])
            ds = []
            for h in range(2):
                soft = jnp.concatenate([pool[at, :] for at in probs_at(pool, (i * 3 + p) * 2 + h)], 1)
                grad = both[h * IR : h * IR + IR]
                delta = jnp.sum(soft * grad, 0, keepdims=True)
                ds.append((soft * (grad - delta)).astype(BF))
            dk = dot(jnp.concatenate(ds, 0), qkv[0, p, wide, :])
            dq = t_dot(jnp.concatenate(ds, 1), qkv[1, p, rows, :])
            dqkv[0, p, rows, :] = (own_columns(dq, 256) * SCALE).astype(BF)
            dqkv[1, p, rows, :] = own_columns(dk, IR).astype(BF)
        return carry

    lax.fori_loop(first, last, step, 0)


def attend_back_gap(datt, dqkv):
    for p in range(3):
        total = col_sum(datt[p, GAP0 : GAP0 + GAPS, :].astype(F32))
        grad = jnp.broadcast_to((total * even_prob()).astype(BF), (16, 128))
        zero = jnp.zeros((16, 128), BF)
        for b in range((R - GAP0) // 16):
            rows = slice(GAP0 + b * 16, GAP0 + b * 16 + 16)
            dqkv[0, p, rows, :] = zero
            dqkv[1, p, rows, :] = zero
            dqkv[2, p, rows, :] = grad if b < GAPS // 16 else zero


def project_back(k, conv, moments, wqkv, dqkv, dbn, sums, one, two):
    sums[one : one + 1] = jnp.zeros((1, D), F32)
    sums[two : two + 1] = jnp.zeros((1, D), F32)

    def step(c, carry):
        rows = rows_at(c * PCH, PCH)
        grad = jnp.concatenate([dqkv[k, p, rows, :] for p in range(3)], 1)
        back = dot_t(grad, wqkv[k])
        dbn[rows_at(k * R + c * PCH, PCH), :] = back
        standard = (conv[k, rows, :] - moments[k : k + 1]) * moments[3 + k : 4 + k]
        sums[one : one + 1] = sums[one : one + 1] + col_sum(back)
        sums[two : two + 1] = sums[two : two + 1] + col_sum(back * standard)
        return carry

    lax.fori_loop(0, R // PCH, step, 0)


def project_grads(k, bn, dqkv, grads):
    for p in range(3):
        grads[:, p * 128 : p * 128 + 128] = t_dot(bn[k], dqkv[k, p]).astype(BF)


def shifted_at(c, t, row, size):
    return rows_at((c * 3 + t) * CONVR + row, size)


def conv_back_zero(pool):
    for c in range(3):
        for t in range(3):
            for i in range(IMAGES + 1):
                pool[shifted_at(c, t, i * STRIDE, 16), :] = jnp.zeros((16, 128), F32)


CONV_ROWS = 16


def conv_back(k, first, last, dbn, conv, moments, one, two, gains, shifts, nrm, pool, kernels, dn, dker, inverse_total):
    mask = cell_mask(IR)
    cells = cell_mask(CB)

    def spread(i, carry):
        rows = rows_at(i * IR, IR)
        for t in range(3):
            lanes = slice(t * 128, t * 128 + 128)
            inv = moments[3 + k : 4 + k, lanes]
            standard = (conv[k, rows, lanes] - moments[k : k + 1, lanes]) * inv
            shift = (one[:, lanes] + standard * two[:, lanes]) * inverse_total
            grad = dbn[rows_at(k * R + i * IR, IR), lanes]
            grad = (gains[1 + k : 2 + k, lanes] * inv) * (grad - mask * shift)
            pool[shifted_at(0, t, i * STRIDE + 16, IR), :] = pltpu.roll(grad, 1, 0)
            pool[shifted_at(1, t, i * STRIDE + 16, IR), :] = grad
            pool[shifted_at(2, t, i * STRIDE + 16, IR), :] = pltpu.roll(grad, IR - 1, 0)
        return carry

    lax.fori_loop(0, IMAGES, spread, 0)
    blocks = IMAGES * IR // CB
    per = IR // CB
    for t in range(3):
        lanes = slice(t * 128, t * 128 + 128)
        taps = [kernels[o, k : k + 1, lanes] for o in range(9)]

        def step(b, sums9):
            base = (b // per) * STRIDE + 16 + (b % per) * CB
            here = nrm[1, rows_at(base, CB), lanes]
            acc = jnp.zeros((CB, 128), F32)
            new = []
            for o in range(9):
                x = pool[shifted_at(2 - o % 3, t, base - (o // 3 - 1) * 16, CB), :]
                acc = acc + x * taps[o]
                new.append(sums9[o] + jnp.sum((x * here).reshape(CB // 8, 8, 128), 0))
            rows = rows_at(b * CB, CB)
            if not first:
                acc = acc + dn[rows, lanes]
            dn[rows, lanes] = acc
            if last:
                new.append(sums9[9] + jnp.sum((acc * here).reshape(CB // 8, 8, 128), 0))
                new.append(sums9[10] + jnp.sum((acc * cells).reshape(CB // 8, 8, 128), 0))
            return tuple(new)

        found = lax.fori_loop(0, blocks, step, (jnp.zeros((8, 128), F32),) * (11 if last else 9))
        found = [col_sum(f) for f in found]
        for o in range(9):
            dker[k, o : o + 1, lanes] = found[o]
        if last:
            dker[k, 9:10, lanes] = (found[9] - found[10] * shifts[0:1, lanes]) / gains[0:1, lanes]
            dker[k, 10:11, lanes] = found[10]


def last_norm_back(tokp, dres, dn, gains, gtok):
    mask = cell_mask(IR)

    def step(i, carry):
        rows = rows_at(i * IR, IR)
        xhat, rstd = norm_parts(tokp[rows, :])
        scaled = dn[rows, :] * mask * gains[0:1]
        one = jnp.sum(scaled, -1, keepdims=True) * (1.0 / D)
        two = jnp.sum(scaled * xhat, -1, keepdims=True) * (1.0 / D)
        gtok[rows, :] = dres[rows, :] + rstd * (scaled - one - xhat * two)
        return carry

    lax.fori_loop(0, IMAGES, step, 0)
    gtok[GAP0:R, :] = dres[GAP0:R, :]


class GradSum:
    def __init__(self, place, grads, bufs, sems, both):
        self.place, self.grads, self.both = place, grads, both
        self.rx_core, self.rx_one, self.mid, self.rx_z, self.fin, self.done = bufs
        self.own = grads.at[place.mp]
        self.slot = place.mp if both else 0
        self.rows = grads.shape[1]
        self.quarter = self.rows // QUAD
        self.part = z_part(self.rows, place.groups)
        self.block = min(self.quarter, 128)
        self.sems = sems
        self.stage = 0
        self.pending = []
        self.steps = [[self.core_start], [self.core_end, self.quad_start], [self.quad_end, self.z_start]]
        self.steps += [[self.z_end, self.z_back_start], [self.z_back_end, self.quad_back_start]]
        self.steps += [[self.end, self.core_back_start], [self.end]] if both else [[self.end]]

    def step(self):
        for part in self.steps.pop(0):
            part()

    def copies(self, ref, triples):
        self.stage += 1
        for src, dst, peer in triples:
            remote(src, dst, self.sems.at[0], self.sems.at[self.stage], peer)
        self.pending = [Pending(ref, self.sems.at[0], self.sems.at[self.stage])]

    def end(self):
        finish(self.pending)
        self.pending = []

    def add(self, dst, dst_at, mine, mine_at, theirs, rows, lanes):
        def step(b, carry):
            at = b * self.block
            total = mine[rows_at(mine_at + at, self.block), lanes].astype(F32)
            for ref in theirs:
                total = total + ref[rows_at(at, self.block), lanes].astype(F32)
            dst[rows_at(dst_at + at, self.block), lanes] = total.astype(BF)
            return carry

        lax.fori_loop(0, rows // self.block, step, 0)

    def core_start(self):
        self.copies(self.rx_core, [(self.grads.at[1 - self.place.mp], self.rx_core, self.place.other_core())])

    def core_end(self):
        self.end()
        self.add(self.own, 0, self.own, 0, [self.rx_core], self.rows, slice(None))

    def fill(self):
        if self.part * self.place.groups > self.quarter:
            self.mid[self.quarter :, :] = jnp.zeros((self.part * self.place.groups - self.quarter, D), BF)

    def quad_start(self):
        triples = []
        for o in range(1, QUAD):
            there = rows_at(lax.rem(self.place.quad + o, QUAD) * self.quarter, self.quarter)
            triples.append((self.own.at[there], self.rx_one.at[o - 1], self.place.in_quad(o)))
        self.copies(self.rx_one, triples)

    def quad_end(self):
        self.end()
        theirs = [self.rx_one.at[o] for o in range(QUAD - 1)]
        self.add(self.mid, 0, self.own, self.place.quad * self.quarter, theirs, self.quarter, slice(None))
        self.fill()

    def z_start(self):
        triples = []
        for o in range(1, self.place.groups):
            there = rows_at(lax.rem(self.place.z + o, self.place.groups) * self.part, self.part)
            triples.append((self.mid.at[there], self.rx_z.at[o - 1], self.place.along(o)))
        self.copies(self.rx_z, triples)

    def z_end(self):
        self.end()
        here = rows_at(self.place.z * self.part, self.part)
        total = self.mid[here, :].astype(F32)
        for o in range(self.place.groups - 1):
            total = total + self.rx_z[o].astype(F32)
        self.fin[here, :] = total.astype(BF)

    def z_back_start(self):
        here = self.fin.at[rows_at(self.place.z * self.part, self.part)]
        self.copies(self.rx_z, [(here, here, self.place.along(o)) for o in range(1, self.place.groups)])

    def z_back_end(self):
        self.end()
        here = rows_at(self.place.quad * self.quarter, self.quarter)
        self.done[self.slot, here, :] = self.fin[0 : self.quarter, :]

    def quad_back_start(self):
        here = self.done.at[self.slot, rows_at(self.place.quad * self.quarter, self.quarter)]
        self.copies(self.rx_one, [(here, here, self.place.in_quad(o)) for o in range(1, QUAD)])

    def core_back_start(self):
        here = self.done.at[self.place.mp]
        self.copies(self.rx_core, [(here, here, self.place.other_core())])


def z_part(rows, groups):
    return -(-rows // QUAD // (16 * groups)) * 16


UNITS = ((2 * PW, False), (2 * PW, False), (2 * PW, False), (D, True), (D, True))


def unit_buffers(groups, rows, both):
    span = z_part(rows, groups) * groups
    dims = [(rows, D), (QUAD - 1, rows // QUAD, D), (span, D)]
    dims += [(groups - 1, span // groups, D), (span, D), (2 if both else 1, rows, D)]
    return [pltpu.VMEM((2, rows, D), BF)] + [pltpu.VMEM(d, BF) for d in dims]


def main_kernel(
    groups, seg, tokens, cot, gains, shifts, kernels, wqkv, wout, win, wmo, bias_h,
    out_hbm, gtok_hbm, dw0, dw1, dw2, dw3, dw4, rest_out,
    pool, tokp, cotp, conv, nrm, dbn, outp, dres, bn, qkv, att, n2, gm, gr, act, dpre, datt, dqkv,
    wqkv_b, wout_b, win_f, wmo_f, bias_f, stats, moments, sums, sums_v, small, dbias, dker,
    mx1, mx2, sx1, sx2, lx1, lx2, vx1, vx2, kx1, kx2,
    in_sems, w_sems, pair_s, pair_r, sems, unit_sems, out_sems, dw_sems, *unit_flat,
):
    dws = (dw0, dw1, dw2, dw3, dw4)
    unit_refs = [unit_flat[n * 7 : n * 7 + 7] for n in range(len(UNITS))]
    place = Place(groups)
    place.greet()
    copies = []
    for n, src in enumerate((tokens, cot)):
        for t in range(3):
            copy = pltpu.make_async_copy(
                src.at[0, :, pl.ds(t * 128, 128)], pool.at[pl.ds((n * 3 + t) * SCR, CELLS)], in_sems.at[n, t]
            )
            copy.start()
            copies.append(copy)
    blocks = [(wqkv.at[:, pl.ds(k * D, D)], dbn.at[pl.ds(k * D, D)]) for k in range(3)]
    blocks.append((wout, dbn.at[pl.ds(3 * D, D)]))
    for j in range(PARTS):
        blocks.append((win.at[:, pl.ds(j * PW, PW)], dbn.at[pl.ds((4 + j) * D, D), pl.ds(0, PW)]))
    blocks.append((wmo, dres.at[pl.ds(0, HH)]))
    weights = []
    for n, (src, dst) in enumerate(blocks):
        copy = pltpu.make_async_copy(src, dst, w_sems.at[n])
        copy.start()
        weights.append(copy)
    ahead = empty_before(seg)
    finish(copies)
    to_images(pool, 0, tokp, ahead)
    first_norm(tokp, gains, shifts, nrm)
    conv_forward(nrm, kernels, conv, stats)
    place.greeted()

    cells = IMAGES * IMG * IMG
    copies = send_eight(place, stats, mx1, sems.at[0, 0], sems.at[0, 1])
    mx1[place.slot] = stats[...]
    finish(weights)
    for k in range(3):
        wqkv_b[k] = dbn[k * D : k * D + D, :].astype(BF)
    wout_b[...] = dbn[3 * D : 4 * D, :].astype(BF)
    for j in range(PARTS):
        win_f[j, place.mp] = dbn[(4 + j) * D : (5 + j) * D, 0:PW].astype(BF)
        wmo_f[j, place.mp] = dres[j * PW : j * PW + PW, :].astype(BF)
    bias_f[place.mp] = jnp.broadcast_to(bias_h[...].reshape(1, HH), (8, HH))
    pairs = [
        remote(ref, ref, pair_s.at[n], pair_r.at[n], place.other_core())
        for n, ref in enumerate((win_f.at[:, place.mp], wmo_f.at[:, place.mp], bias_f.at[place.mp]))
    ]
    to_images(pool, 3 * SCR, cotp, ahead)
    finish(copies)
    mean, m2 = merge_moments(mx1, 8, cells)
    mx2[place.z, 0:3] = mean
    mx2[place.z, 3:6] = m2
    mx2[place.z, 6:8] = jnp.zeros((2, D), F32)
    finish(send_along(place, mx2.at[place.z], mx2, sems.at[0, 0], sems.at[0, 2]))
    mean, m2 = merge_moments(mx2, groups, 8 * cells)
    moments[0:3] = mean
    moments[3:6] = lax.rsqrt(m2 * (1.0 / (cells * 8 * groups)) + EPS)
    moments[6:8] = jnp.zeros((2, D), F32)

    project(conv, moments, gains, shifts, wqkv_b, bn, qkv)
    attend(qkv, pool, att)
    attend_gap(qkv, att)
    feed_forward_in(tokp, cotp, att, wout_b, gains, shifts, dres, n2, gm, small)
    finish(pairs)

    units = []
    for n, (rows, both) in enumerate(UNITS):
        units.append(GradSum(place, unit_refs[n][0], unit_refs[n][1:], unit_sems.at[n], both))
    ua, ub, ue, uc, ud = units
    grads = [refs[0] for refs in unit_refs]
    acc = dbn.at[pl.ds(0, R)]
    mine, theirs = place.mp, 1 - place.mp
    stores = []

    def keep(at, ref=None):
        def done(total):
            rest_out[at : at + total.shape[0]] = total
            if ref is not None:
                ref[...] = total

        return done

    def keep_small(total):
        rest_out[8:16] = total
        tiles = [total[4 + c // 3 : 5 + c // 3, c % 3 * 128 : c % 3 * 128 + 128] for c in range(BIAS_TILES)]
        for c in range(BIAS_TILES // 2):
            at = c // 2 * 4 + c % 2
            kept = jnp.where(place.mp == 0, tiles[at], tiles[at + 2])
            rest_out[72 + c // 2 : 73 + c // 2, c % 2 * 128 : c % 2 * 128 + 128] = kept

    small_sum = SmallSum(place, small, lx1, lx2, sems, 2, keep_small)
    sum_v = SmallSum(place, sums_v, vx1, vx2, sems, 6, keep(64, sums_v))
    sum_qk = SmallSum(place, sums, sx1, sx2, sems, 1, keep(0, sums))
    ker_sums = [SmallSum(place, dker.at[k], kx1.at[k], kx2.at[k], sems, 3 + k, keep(16 + 16 * k)) for k in range(3)]

    def forward(part):
        hidden_part(part, n2, gm, win_f, wmo_f, bias_f, act, dpre, outp, acc, dbias)

    def hidden(half, part):
        hidden_grads(half, n2, gm, act, dpre, grads[part])
        if half is theirs:
            units[part].step()

    def values():
        attend_back_values(pool, datt, dqkv)
        attend_back_gap(datt, dqkv)

    def after_forward():
        feed_forward_out(cotp, wout_b, gains, shifts, outp, acc, dres, gr, datt, small)
        for c in range(BIAS_TILES):
            tile = slice(c % 4 * 128, c % 4 * 128 + 128)
            small[4 + c // 3 : 5 + c // 3, c % 3 * 128 : c % 3 * 128 + 128] = dbias[c // 4, 0:1, tile]
        small_sum.start()
        stores.append(pltpu.make_async_copy(outp, out_hbm, out_sems.at[0]))
        stores[0].start()

    def out_grad():
        for p in range(3):
            grads[3][1, p * 128 : p * 128 + 128, :] = t_dot(att[p], gr[...]).astype(BF)

    def value_grads():
        project_grads(2, bn, dqkv, grads[3].at[0])
        uc.step()

    def query_grads():
        for k in range(2):
            project_grads(k, bn, dqkv, grads[4].at[k])
        ud.step()

    def value_back():
        project_back(2, conv, moments, wqkv_b, dqkv, dbn, sums_v, 0, 1)
        sum_v.start()

    def query_back():
        for k in range(2):
            project_back(k, conv, moments, wqkv_b, dqkv, dbn, sums, k, 2 + k)
        sum_qk.start()
        conv_back_zero(pool)

    def back(k, begin=False, last=False):
        one, two = (sums_v[0:1], sums_v[1:2]) if k == 2 else (sums[k : k + 1], sums[2 + k : 3 + k])
        conv_back(
            k, begin, last, dbn, conv, moments, one, two, gains, shifts, nrm, pool, kernels, cotp, dker,
            1.0 / (cells * 8 * groups),
        )
        ker_sums[k].start()

    def last_norm():
        stores[0].wait()
        last_norm_back(tokp, dres, cotp, gains, outp)
        stores.append(pltpu.make_async_copy(outp, gtok_hbm, out_sems.at[1]))
        stores[-1].start()

    def unit(n):
        units[n].step()
        if not units[n].steps:
            stores.append(pltpu.make_async_copy(units[n].done, dws[n], dw_sems.at[n]))
            stores[-1].start()

    forward(0)
    hidden(theirs, 0)
    hidden(mine, 0)
    forward(1)
    unit(0)
    hidden(theirs, 1)
    hidden(mine, 1)
    forward(2)
    unit(1)
    hidden(theirs, 2)
    hidden(mine, 2)
    after_forward()
    unit(0)
    unit(2)
    values()
    out_grad()
    value_grads()
    unit(1)
    value_back()
    small_sum.step()
    unit(0)
    unit(3)
    attend_back(0, 2, qkv, pool, datt, dqkv)
    unit(1)
    unit(2)
    attend_back(2, 4, qkv, pool, datt, dqkv)
    unit(0)
    small_sum.step()
    sum_v.step()
    unit(3)
    query_grads()
    query_back()
    unit(4)
    unit(1)
    unit(0)
    unit(2)
    sum_qk.step()
    sum_v.step()
    back(2, begin=True)
    unit(4)
    unit(3)
    unit(2)
    sum_qk.step()
    back(1)
    unit(4)
    unit(1)
    ker_sums[2].step()
    back(0, last=True)
    unit(3)
    last_norm()
    unit(2)
    unit(4)
    ker_sums[1].step()
    ker_sums[0].step()
    ker_sums[2].step()
    unit(3)
    unit(3)
    ker_sums[1].step()
    unit(4)
    ker_sums[0].step()
    unit(4)
    finish(stores[1:])


def main_call(groups, *args):
    units = [buf for unit in UNITS for buf in unit_buffers(groups, *unit)]
    return pl.pallas_call(
        functools.partial(main_kernel, groups),
        out_shape=(shape(R, D), shape(R, D))
        + tuple(shape(2 if both else 1, rows, D, dtype=BF) for rows, both in UNITS)
        + (shape(80, D),),
        in_specs=[VM, ANY, ANY, VM, VM, VM, ANY, ANY, ANY, ANY, VM],
        out_specs=(ANY,) * 7 + (VM,),
        scratch_shapes=[
            pltpu.VMEM((POOL, 128), F32),
            pltpu.VMEM((R, D), F32), pltpu.VMEM((R, D), F32), pltpu.VMEM((3, R, D), F32),
            pltpu.VMEM((3, CONVR, D), F32), pltpu.VMEM((3 * R, D), F32),
            pltpu.VMEM((R, D), F32), pltpu.VMEM((R, D), F32),
            pltpu.VMEM((3, R, D), BF), pltpu.VMEM((3, 3, R, 128), BF), pltpu.VMEM((3, R, 128), BF),
            pltpu.VMEM((R, D), BF), pltpu.VMEM((R, D), BF), pltpu.VMEM((R, D), BF),
            pltpu.VMEM((R, 512), BF), pltpu.VMEM((R, 512), BF), pltpu.VMEM((3, R, 128), BF), pltpu.VMEM((3, 3, R, 128), BF),
            pltpu.VMEM((3, D, D), BF), pltpu.VMEM((D, D), BF), pltpu.VMEM((PARTS, 2, D, PW), BF), pltpu.VMEM((PARTS, 2, PW, D), BF),
            pltpu.VMEM((2, 8, HH), F32),
            pltpu.VMEM((8, D), F32), pltpu.VMEM((8, D), F32), pltpu.VMEM((8, D), F32), pltpu.VMEM((8, D), F32),
            pltpu.VMEM((8, D), F32), pltpu.VMEM((PARTS, 8, 2 * PW), F32), pltpu.VMEM((3, CONV_ROWS, D), F32),
            pltpu.VMEM((8, 8, D), F32), pltpu.VMEM((groups, 8, D), F32),
            pltpu.VMEM((8, 8, D), F32), pltpu.VMEM((groups, 8, D), F32),
            pltpu.VMEM((8, 8, D), F32), pltpu.VMEM((groups, 8, D), F32),
            pltpu.VMEM((8, 8, D), F32), pltpu.VMEM((groups, 8, D), F32),
            pltpu.VMEM((3, 8, CONV_ROWS, D), F32), pltpu.VMEM((3, groups, CONV_ROWS, D), F32),
            dma(2, 3), dma(8), dma(3), dma(3), dma(7, 3), dma(5, 7), dma(2), dma(5),
        ] + units,
        compiler_params=params(collective_id=0, has_side_effects=True),
    )(*args)


def last_kernel(
    seg, outp, gtok, dwa, dwb, dwe, dwc, dwd, rest,
    output, grad_tokens, grad_gains, grad_shifts, grad_kernels, grad_qkv, grad_out, grad_in, grad_bias, grad_down,
    held, lowa, lowb, lowe, lowc, lowd, scr, wide, in_sems, out_sems,
):
    loads = []
    pairs = ((outp, held.at[0]), (gtok, held.at[1]))
    pairs += ((dwa, lowa), (dwb, lowb), (dwe, lowe), (dwc, lowc), (dwd, lowd))
    for n, (src, dst) in enumerate(pairs):
        copy = pltpu.make_async_copy(src, dst, in_sems.at[n])
        copy.start()
        loads.append(copy)
    starts, gaps = find_columns(seg)
    stores = []

    def store(src, dst):
        copy = pltpu.make_async_copy(src, dst, out_sems.at[len(stores)])
        copy.start()
        stores.append(copy)

    for n, dst in enumerate((output, grad_tokens)):
        loads[n].wait()
        to_canvas(held.at[n], scr.at[n], starts, gaps)
        for t in range(3):
            store(scr.at[n, t, pl.ds(0, CELLS)], dst.at[0, :, pl.ds(t * 128, 128)])
    for n, low in enumerate((lowa, lowb, lowe)):
        loads[2 + n].wait()
        start, size = n * PW, PW
        grad_in[:, start : start + size] = low[0, 0:size, :].astype(F32).T
        wide[start : start + size, :] = low[0, size : 2 * size, :].astype(F32)
        store(wide.at[pl.ds(start, size)], grad_down.at[pl.ds(start, size)])
    for n, low in enumerate((lowc, lowd)):
        loads[5 + n].wait()
        for j in range(2):
            at = HH + (n * 2 + j) * D
            wide[at : at + D, :] = low[j].astype(F32)
            here = wide.at[pl.ds(at, D)]
            if n == 0 and j == 1:
                store(here, grad_out)
            else:
                store(here, grad_qkv.at[:, pl.ds((2 if n == 0 else j) * D, D)])
    for k in range(3):
        for o in range(9):
            row = 16 + k * CONV_ROWS + o
            grad_kernels[o, k : k + 1] = rest[row : row + 1]
    grad_gains[0:1] = rest[25:26]
    grad_gains[1:3] = rest[2:4]
    grad_gains[3:4] = rest[65:66]
    grad_gains[4:5] = rest[8:9]
    grad_shifts[0:1] = rest[26:27]
    grad_shifts[1:2] = rest[0:1]
    grad_shifts[2:3] = rest[64:65]
    grad_shifts[3:4] = rest[9:10]
    grad_shifts[4:5] = rest[10:11]
    grad_shifts[5:6] = rest[11:12]
    for j in range(PARTS):
        grad_bias[j * PW : j * PW + PW] = rest[72 + j, 0:PW]
    finish(stores)


def last_call(*args):
    return pl.pallas_call(
        last_kernel,
        out_shape=(
            shape(1, CELLS, D), shape(1, CELLS, D), shape(5, D), shape(6, D), shape(9, 3, D), shape(D, 3 * D),
            shape(D, D), shape(D, HH), shape(HH), shape(HH, D),
        ),
        in_specs=[SM] + [ANY] * 7 + [VM],
        out_specs=(ANY, ANY, VM, VM, VM, ANY, ANY, VM, VM, ANY),
        scratch_shapes=[
            pltpu.VMEM((2, R, D), F32),
            *(pltpu.VMEM((2 if both else 1, rows, D), BF) for rows, both in UNITS),
            pltpu.VMEM((2, 3, CELLS + 16, 128), F32), pltpu.VMEM((HH + 4 * D, D), F32), dma(7), dma(13),
        ],
        compiler_params=params(),
    )(*args)


def local(
    groups, tokens, segment_ids, gains, shifts, kernels, qkv_weight, out_weight,
    mlp_in_weight, mlp_in_bias, mlp_out_weight, cotangent,
):
    found = main_call(
        groups, segment_ids, tokens, cotangent, gains, shifts, kernels.transpose(1, 0, 2),
        qkv_weight, out_weight, mlp_in_weight, mlp_out_weight, mlp_in_bias,
    )
    outs = list(last_call(segment_ids, *found))
    outs[4] = outs[4].transpose(1, 0, 2)
    return tuple(outs)


def solution(mesh):
    groups = mesh.shape["dp"] // QUAD
    both = P(("dp", "mp"), None, None)
    return jax.shard_map(
        functools.partial(local, groups),
        mesh=mesh,
        in_specs=(
            both, P(("dp", "mp"), None), P(), P(), P(), P(), P(), P(None, "mp"), P("mp"), P("mp", None), both,
        ),
        out_specs=(both, both, P(), P(), P(), P(), P(), P(None, "mp"), P("mp"), P("mp", None)),
        check_vma=False,
    )
```

```python
import functools
import math

import jax
import jax.numpy as jnp
from jax import lax
from jax.experimental import pallas as pl
from jax.experimental.pallas import tpu as pltpu
from jax.sharding import PartitionSpec as P

F32 = jnp.float32
BF = jnp.bfloat16
MESH = pl.DeviceIdType.MESH
D = 384
IMG = 14
IMAGES = 4
CW = 64
CELLS = IMG * CW
IR = 224
GAP0 = IMAGES * IR
GAPS = 112
R = 1024
DCH = 1024
STRIDE = IR + 16
CONVR = IMAGES * STRIDE + 16
EPS = 1e-05
MASKED = -1e30
QUAD = 4
HH = 2 * D
VLIM = 62 * 2**20
SCALE = 0.125
PCH = 512


def params(**kw):
    return pltpu.CompilerParams(vmem_limit_bytes=VLIM, **kw)


VM = pl.BlockSpec(memory_space=pltpu.VMEM)
SM = pl.BlockSpec(memory_space=pltpu.SMEM)
ANY = pl.BlockSpec(memory_space=pl.ANY)


def shape(*dims, dtype=F32):
    return jax.ShapeDtypeStruct(dims, dtype)


def dot(a, b):
    return jnp.dot(a, b, preferred_element_type=F32)


def dot_t(a, b):
    return lax.dot_general(a, b, (((1,), (1,)), ((), ())), preferred_element_type=F32)


def t_dot(a, b):
    return lax.dot_general(a, b, (((0,), (0,)), ((), ())), preferred_element_type=F32)


def cell_mask(rows):
    row = lax.broadcasted_iota(jnp.int32, (rows, 1), 0)
    return (row % 16 < IMG).astype(F32)


def rows_at(start, size, align=16):
    return pl.ds(pl.multiple_of(start, align), size)


def find_columns(seg):
    def step(col, found):
        count, starts, gaps = found
        here = seg[0, col]
        starts = tuple(jnp.minimum(s, jnp.where(here == i + 1, col, CW)) for i, s in enumerate(starts))
        empty = here == 0
        gaps = tuple(jnp.where(empty & (count == k), col, g) for k, g in enumerate(gaps))
        return count + jnp.where(empty, 1, 0), starts, gaps

    start = (jnp.int32(0), (jnp.int32(CW),) * IMAGES, (jnp.int32(0),) * 8)
    _, starts, gaps = lax.fori_loop(0, CW, step, start)
    return starts, gaps


SCR = CELLS + 16
POOL = 48 * IR


def empty_before(seg):
    lane = lax.broadcasted_iota(jnp.int32, (1, 128), 1)
    ids = seg[0:1, 0:128]
    firsts = [jnp.where((ids == i + 1) & (lane < CW), lane, CW).astype(F32) for i in range(IMAGES)]
    return [jnp.min(f, -1, keepdims=True) - float(i * IMG) for i, f in enumerate(firsts)]


def to_images(pool, base, out, ahead):
    col = lax.broadcasted_iota(jnp.int32, (16, 128), 0)
    sub = lax.broadcasted_iota(jnp.int32, (8, 128), 0).astype(F32)
    before = sum([jnp.where(a <= sub, 1.0, 0.0) for a in ahead])

    def step(r, carry):
        for t in range(3):
            row = base + t * SCR + r * CW
            for i in range(IMAGES):
                window = pool[pl.ds(row + i * IMG, 16), :]
                for e in range(1, 9):
                    moved = pool[pl.ds(row + i * IMG + e, 16), :]
                    window = jnp.where(ahead[i] == float(e), moved, window)
                out[rows_at(i * IR + r * 16, 16), t * 128 : t * 128 + 128] = jnp.where(col < IMG, window, 0.0)
            block = pool[rows_at(row, 8, 8), :]
            for n in range(1, IMAGES + 1):
                block = jnp.where(before == float(n), pool[pl.ds(row + n * IMG, 8), :], block)
            out[rows_at(GAP0 + r * 8, 8, 8), t * 128 : t * 128 + 128] = block
        return carry

    lax.fori_loop(0, IMG, step, 0)
    out[GAP0 + GAPS : R, :] = jnp.zeros((R - GAP0 - GAPS, D), F32)


def to_canvas(src, scr, starts, gaps):
    def step(r, carry):
        for t in range(3):
            for i in range(IMAGES):
                block = src[rows_at(i * IR + r * 16, 16), t * 128 : t * 128 + 128]
                scr[t, pl.ds(r * CW + starts[i], 16), :] = block
            block = src[rows_at(GAP0 + r * 8, 8, 8), t * 128 : t * 128 + 128]
            for k in range(8):
                scr[t, pl.ds(r * CW + gaps[k], 1), :] = block[k : k + 1]
        return carry

    lax.fori_loop(0, IMG, step, 0)


def norm_parts(x):
    mean = jnp.sum(x, -1, keepdims=True) * (1.0 / D)
    centred = x - mean
    var = jnp.sum(centred * centred, -1, keepdims=True) * (1.0 / D)
    rstd = lax.rsqrt(var + EPS)
    return centred * rstd, rstd


def store_shifted(dst, i, t, x):
    lanes = slice(t * 128, t * 128 + 128)
    at = rows_at(i * STRIDE + 16, IR)
    dst[0, at, lanes] = pltpu.roll(x, 1, 0)
    dst[1, at, lanes] = x
    dst[2, at, lanes] = pltpu.roll(x, IR - 1, 0)


def zero_borders(dst):
    for i in range(IMAGES + 1):
        for c in range(3):
            dst[c, i * STRIDE : i * STRIDE + 16, :] = jnp.zeros((16, D), F32)


def first_norm(tokp, gains, shifts, nrm):
    zero_borders(nrm)
    mask = cell_mask(IR)

    def step(i, carry):
        xhat, _ = norm_parts(tokp[rows_at(i * IR, IR), :])
        normed = (xhat * gains[0:1] + shifts[0:1]) * mask
        for t in range(3):
            store_shifted(nrm, i, t, normed[:, t * 128 : t * 128 + 128])
        return carry

    lax.fori_loop(0, IMAGES, step, 0)


CB = 224


def conv_forward(nrm, kernels, conv, stats):
    mask = cell_mask(CB)
    blocks = IMAGES * IR // CB
    per = IR // CB
    for t in range(3):
        lanes = slice(t * 128, t * 128 + 128)
        taps = [[kernels[o, k : k + 1, lanes] for o in range(9)] for k in range(3)]

        def step(b, sums):
            base = (b // per) * STRIDE + 16 + (b % per) * CB
            acc = [jnp.zeros((CB, 128), F32)] * 3
            for o in range(9):
                x = nrm[o % 3, rows_at(base + (o // 3 - 1) * 16, CB), lanes]
                for k in range(3):
                    acc[k] = acc[k] + x * taps[k][o]
            new = []
            for k in range(3):
                conv[k, rows_at(b * CB, CB), lanes] = acc[k]
                new.append(sums[k] + jnp.sum((acc[k] * mask).reshape(CB // 8, 8, 128), 0))
            return tuple(new)

        sums = lax.fori_loop(0, blocks, step, (jnp.zeros((8, 128), F32),) * 3)
        means = [jnp.sum(s, 0, keepdims=True) * (1.0 / (IMAGES * IMG * IMG)) for s in sums]

        def spread(b, sums):
            new = []
            for k in range(3):
                away = (conv[k, rows_at(b * CB, CB), lanes] - means[k]) * mask
                new.append(sums[k] + jnp.sum((away * away).reshape(CB // 8, 8, 128), 0))
            return tuple(new)

        squares = lax.fori_loop(0, blocks, spread, (jnp.zeros((8, 128), F32),) * 3)
        for k in range(3):
            stats[k : k + 1, lanes] = means[k]
            stats[3 + k : 4 + k, lanes] = jnp.sum(squares[k], 0, keepdims=True)
        stats[6:8, lanes] = jnp.zeros((2, 128), F32)
    for k in range(3):
        conv[k, GAP0:R, :] = jnp.zeros((R - GAP0, D), F32)


class Place:
    def __init__(self, groups):
        dp = lax.axis_index("dp")
        self.mp = lax.axis_index("mp")
        self.groups = groups
        self.quad = lax.rem(dp, QUAD)
        self.z = dp // QUAD
        self.slot = self.quad * 2 + self.mp

    def in_eight(self, offset):
        other = lax.rem(self.slot + offset, 8)
        return (self.z * QUAD + other // 2, lax.rem(other, 2))

    def in_quad(self, offset):
        return (self.z * QUAD + lax.rem(self.quad + offset, QUAD), self.mp)

    def along(self, offset):
        return (lax.rem(self.z + offset, self.groups) * QUAD + self.quad, self.mp)

    def other_core(self):
        return (self.z * QUAD + self.quad, 1 - self.mp)

    def peers(self):
        return [self.in_eight(o) for o in range(1, 8)] + [self.along(o) for o in range(1, self.groups)]

    def greet(self):
        barrier = pltpu.get_barrier_semaphore()
        for peer in self.peers():
            pl.semaphore_signal(barrier, inc=1, device_id=peer, device_id_type=MESH)

    def greeted(self):
        pl.semaphore_wait(pltpu.get_barrier_semaphore(), 7 + self.groups - 1)


def remote(src, dst, send, recv, peer):
    copy = pltpu.make_async_remote_copy(
        src_ref=src, dst_ref=dst, send_sem=send, recv_sem=recv, device_id=peer, device_id_type=MESH
    )
    copy.start()
    return copy


def send_eight(place, src, rx, send, recv):
    for o in range(1, 8):
        remote(src, rx.at[place.slot], send, recv, place.in_eight(o))
    return Pending(rx.at[pl.ds(0, 7)], send, recv)


def send_along(place, src, rx, send, recv):
    for o in range(1, place.groups):
        remote(src, rx.at[place.z], send, recv, place.along(o))
    return Pending(rx.at[pl.ds(0, place.groups - 1)], send, recv)


class Pending:
    def __init__(self, ref, send, recv):
        self.ref, self.sems = ref, (send, recv)

    def wait(self):
        for sem in self.sems:
            pltpu.make_async_copy(self.ref, self.ref, sem).wait()


def finish(copies):
    for copy in copies if isinstance(copies, list) else [copies]:
        copy.wait()


def sum_slots(rx, count):
    total = rx[0].astype(F32)
    for s in range(1, count):
        total = total + rx[s].astype(F32)
    return total


class SmallSum:
    def __init__(self, place, src, rx1, rx2, sems, n, done):
        self.place, self.src, self.rx1, self.rx2, self.done = place, src, rx1, rx2, done
        self.sems = [sems.at[n, i] for i in range(3)]
        self.steps = [self.middle, self.end]

    def start(self):
        self.copies = send_eight(self.place, self.src, self.rx1, self.sems[0], self.sems[1])
        self.rx1[self.place.slot] = self.src[...]

    def step(self):
        self.steps.pop(0)()

    def middle(self):
        finish(self.copies)
        self.rx2[self.place.z] = sum_slots(self.rx1, 8).astype(self.rx2.dtype)
        self.copies = send_along(self.place, self.rx2.at[self.place.z], self.rx2, self.sems[0], self.sems[2])

    def end(self):
        finish(self.copies)
        self.done(sum_slots(self.rx2, self.place.groups))


class PairedSum:
    def __init__(self, place, src, rx_core, rx_quad, rx_z, both, sems, n, done):
        self.place, self.src, self.both, self.done = place, src, both, done
        self.rx_core, self.rx_quad, self.rx_z = rx_core, rx_quad, rx_z
        self.sems = [sems.at[n, i] for i in range(5)]
        self.steps = [self.quad, self.along, self.core_back, self.end]

    def exchange(self, stage, ref, src, dst, peers):
        for peer in peers:
            remote(src, dst, self.sems[0], self.sems[stage], peer)
        self.copies = Pending(ref, self.sems[0], self.sems[stage])

    def half(self, mp):
        return rows_at(mp * 8, 8, 8)

    def start(self):
        there = self.src.at[self.half(1 - self.place.mp)]
        self.exchange(1, self.rx_core, there, self.rx_core, [self.place.other_core()])

    def step(self):
        finish(self.copies)
        self.steps.pop(0)()

    def quad(self):
        slot = self.place.quad
        self.rx_quad[slot] = self.src[self.half(self.place.mp), :] + self.rx_core[...]
        here = self.rx_quad.at[slot]
        peers = [self.place.in_quad(o) for o in range(1, QUAD)]
        self.exchange(2, self.rx_quad.at[pl.ds(0, QUAD - 1)], here, here, peers)

    def along(self):
        self.rx_z[self.place.z] = sum_slots(self.rx_quad, QUAD)
        here = self.rx_z.at[self.place.z]
        peers = [self.place.along(o) for o in range(1, self.place.groups)]
        self.exchange(3, self.rx_z.at[pl.ds(0, self.place.groups - 1)], here, here, peers)

    def core_back(self):
        self.both[self.half(self.place.mp), :] = sum_slots(self.rx_z, self.place.groups)
        here = self.both.at[self.half(self.place.mp)]
        self.exchange(4, here, here, here, [self.place.other_core()])

    def end(self):
        self.done(self.both[...])


def merge_moments(rx, count, cells):
    mean = sum([rx[s, 0:3] for s in range(1, count)], rx[0, 0:3]) * (1.0 / count)
    m2 = sum([rx[s, 3:6] for s in range(1, count)], rx[0, 3:6])
    for s in range(count):
        away = rx[s, 0:3] - mean
        m2 = m2 + away * away * float(cells)
    return mean, m2


def dma(*n):
    return pltpu.SemaphoreType.DMA(n)


def project(conv, moments, gains, shifts, wqkv, bn, qkv):
    def step(c, carry):
        rows = rows_at(c * DCH, DCH)
        for k in range(3):
            standard = (conv[k, rows, :] - moments[k : k + 1]) * moments[3 + k : 4 + k]
            value = standard * gains[1 + k : 2 + k]
            if k != 1:
                value = value + (shifts[1:2] if k == 0 else shifts[2:3])
            value = value.astype(BF)
            bn[k, rows, :] = value
            out = dot(value, wqkv[k]).astype(BF)
            if k == 0:
                out = (out * SCALE).astype(BF)
            for p in range(3):
                qkv[k, p, rows, :] = out[:, p * 128 : p * 128 + 128]
        return carry

    lax.fori_loop(0, R // DCH, step, 0)


def key_bias():
    row = lax.broadcasted_iota(jnp.int32, (16, 256), 0)
    return jnp.where(row < IMG, 0.0, MASKED)


def query_mask():
    lane = lax.broadcasted_iota(jnp.int32, (1, 256), 1)
    return (lane < IR).astype(F32)


def by_head(x):
    lane = lax.broadcasted_iota(jnp.int32, x.shape, 1)
    zero = jnp.zeros_like(x)
    return jnp.concatenate([jnp.where(lane < 64, x, zero), jnp.where(lane < 64, zero, x)], 0)


def own_columns(x, rows):
    lane = lax.broadcasted_iota(jnp.int32, (IR, 128), 1)
    return jnp.where(lane < 64, x[:IR], x[rows : rows + IR])


def probs_at(pool, n):
    return [rows_at((2 * n + half) * IR, IR) for half in range(2)]


def attend(qkv, pool, att):
    bias = key_bias()[None]
    live = query_mask()

    def step(i, carry):
        rows = rows_at(i * IR, IR)
        for p in range(3):
            q = qkv[0, p, rows_at(i * IR, 256), :]
            both = dot_t(by_head(qkv[1, p, rows, :]), q)
            low = []
            for h in range(2):
                scores = (both[h * IR : h * IR + IR].reshape(IMG, 16, 256) + bias).reshape(IR, 256)
                largest = jnp.max(scores, 0, keepdims=True)
                expo = jnp.exp(scores - largest)
                soft = expo * (live / jnp.sum(expo, 0, keepdims=True))
                for half, at in enumerate(probs_at(pool, (i * 3 + p) * 2 + h)):
                    pool[at, :] = soft[:, half * 128 : half * 128 + 128]
                low.append(soft.astype(BF))
            out = t_dot(jnp.concatenate(low, 1), qkv[2, p, rows, :])
            att[p, rows, :] = own_columns(out, 256).astype(BF)
        return carry

    lax.fori_loop(0, IMAGES, step, 0, unroll=4)


def even_prob():
    return jnp.full((1, 1), 1.0 / GAPS, F32).astype(BF).astype(F32)


def attend_gap(qkv, att):
    for p in range(3):
        v = qkv[2, p, GAP0 : GAP0 + 16, :].astype(F32)
        out = (v * (even_prob() * float(GAPS))).astype(BF)
        for b in range((R - GAP0) // 16):
            att[p, GAP0 + b * 16 : GAP0 + b * 16 + 16, :] = out


def gelu_parts(x):
    cdf = 0.5 * (1.0 + lax.erf(x * (1.0 / math.sqrt(2.0))))
    density = jnp.exp(x * x * -0.5) * (1.0 / math.sqrt(2.0 * math.pi))
    return x * cdf, cdf + x * density


def col_sum(x):
    return jnp.sum(x, 0, keepdims=True)


def feed_forward_in(tokp, cotp, att, wout, gains, shifts, dres, n2, gm, small):
    small[...] = jnp.zeros((8, D), F32)

    def step(c, carry):
        rows = rows_at(c * DCH, DCH)
        attended = jnp.concatenate([att[p, rows, :] for p in range(3)], 1)
        residual = tokp[rows, :] + (dot(attended, wout[...]) + shifts[3:4])
        dres[rows, :] = residual
        xhat, _ = norm_parts(residual)
        n2[rows, :] = (xhat * gains[4:5] + shifts[4:5]).astype(BF)
        cot = cotp[rows, :]
        gm[rows, :] = cot.astype(BF)
        small[3:4] = small[3:4] + col_sum(cot)
        return carry

    lax.fori_loop(0, R // DCH, step, 0)


HCH = 1024
PARTS = 3
PW = HH // PARTS
BIAS_TILES = 2 * HH // 128


def hidden_part(part, n2, gm, win, wmo, bias, act, dpre, outp, acc, dbias):
    both = slice(0, 2 * PW)
    dbias[part, 0:1, :] = jnp.zeros((1, 2 * PW), F32)

    def step(c, carry):
        rows = rows_at(c * HCH, HCH)
        up = jnp.concatenate([win[part, h] for h in range(2)], 1)
        down = wmo[part].reshape(2 * PW, D)
        shift = jnp.concatenate([bias[h, 0:1, part * PW : part * PW + PW] for h in range(2)], 1)
        value, slope = gelu_parts(dot(n2[rows, :], up) + shift)
        value = value.astype(BF)
        act[rows, both] = value
        grad = dot_t(gm[rows, :], down) * slope
        dbias[part, 0:1, both] = dbias[part, 0:1, both] + col_sum(grad)
        grad = grad.astype(BF)
        dpre[rows, both] = grad
        forward = dot(value, down)
        back = dot_t(grad, up)
        outp[rows, :] = forward if part == 0 else outp[rows, :] + forward
        acc[rows, :] = back if part == 0 else acc[rows, :] + back
        return carry

    lax.fori_loop(0, R // HCH, step, 0)


def hidden_grads(half, n2, gm, act, dpre, grads):
    units = pl.ds(pl.multiple_of(half * PW, 128), PW)
    grads[half, 0:PW, :] = t_dot(dpre[:, units], n2[...]).astype(BF)
    grads[half, PW : 2 * PW, :] = t_dot(act[:, units], gm[...]).astype(BF)


def feed_forward_out(cotp, wout, gains, shifts, outp, acc, dres, gr, datt, small):
    def step(c, carry):
        rows = rows_at(c * DCH, DCH)
        residual = dres[rows, :]
        outp[rows, :] = residual + outp[rows, :] + shifts[5:6]
        xhat, rstd = norm_parts(residual)
        grad = acc[rows, :]
        scaled = grad * gains[4:5]
        one = jnp.sum(scaled, -1, keepdims=True) * (1.0 / D)
        two = jnp.sum(scaled * xhat, -1, keepdims=True) * (1.0 / D)
        total = cotp[rows, :] + rstd * (scaled - one - xhat * two)
        dres[rows, :] = total
        low = total.astype(BF)
        gr[rows, :] = low
        back = dot_t(low, wout[...]).astype(BF)
        for p in range(3):
            datt[p, rows, :] = back[:, p * 128 : p * 128 + 128]
        small[0:1] = small[0:1] + col_sum(grad * xhat)
        small[1:2] = small[1:2] + col_sum(total)
        small[2:3] = small[2:3] + col_sum(grad)
        return carry

    lax.fori_loop(0, R // DCH, step, 0)


def attend_back_values(pool, datt, dqkv):
    def step(i, carry):
        rows = rows_at(i * IR, IR)
        for p in range(3):
            low = []
            for h in range(2):
                soft = [pool[at, :] for at in probs_at(pool, (i * 3 + p) * 2 + h)]
                low.append(jnp.concatenate(soft, 1).astype(BF))
            dv = dot(jnp.concatenate(low, 0), datt[p, rows_at(i * IR, 256), :])
            dqkv[2, p, rows, :] = own_columns(dv, IR).astype(BF)
        return carry

    lax.fori_loop(0, IMAGES, step, 0)


def attend_back(first, last, qkv, pool, datt, dqkv):
    def step(i, carry):
        rows = rows_at(i * IR, IR)
        wide = rows_at(i * IR, 256)
        for p in range(3):
            both = dot_t(by_head(qkv[2, p, rows, :]), datt[p, wide, :])
            ds = []
            for h in range(2):
                soft = jnp.concatenate([pool[at, :] for at in probs_at(pool, (i * 3 + p) * 2 + h)], 1)
                grad = both[h * IR : h * IR + IR]
                delta = jnp.sum(soft * grad, 0, keepdims=True)
                ds.append((soft * (grad - delta)).astype(BF))
            dk = dot(jnp.concatenate(ds, 0), qkv[0, p, wide, :])
            dq = t_dot(jnp.concatenate(ds, 1), qkv[1, p, rows, :])
            dqkv[0, p, rows, :] = (own_columns(dq, 256) * SCALE).astype(BF)
            dqkv[1, p, rows, :] = own_columns(dk, IR).astype(BF)
        return carry

    lax.fori_loop(first, last, step, 0, unroll=2)


def attend_back_gap(datt, dqkv):
    for p in range(3):
        total = col_sum(datt[p, GAP0 : GAP0 + GAPS, :].astype(F32))
        grad = jnp.broadcast_to((total * even_prob()).astype(BF), (16, 128))
        zero = jnp.zeros((16, 128), BF)
        for b in range((R - GAP0) // 16):
            rows = slice(GAP0 + b * 16, GAP0 + b * 16 + 16)
            dqkv[0, p, rows, :] = zero
            dqkv[1, p, rows, :] = zero
            dqkv[2, p, rows, :] = grad if b < GAPS // 16 else zero


def project_back(k, conv, moments, wqkv, dqkv, dbn, sums, at):
    def step(c, carry):
        rows = rows_at(c * PCH, PCH)
        grad = jnp.concatenate([dqkv[k, p, rows, :] for p in range(3)], 1)
        back = dot_t(grad, wqkv[k])
        dbn[rows_at(k * R + c * PCH, PCH), :] = back
        standard = (conv[k, rows, :] - moments[k : k + 1]) * moments[3 + k : 4 + k]
        return carry[0] + col_sum(back), carry[1] + col_sum(back * standard)

    found = lax.fori_loop(0, R // PCH, step, (jnp.zeros((1, D), F32),) * 2)
    for n in range(2):
        for t in range(3):
            row = at + n * 3 + t
            sums[row : row + 1] = found[n][:, t * 128 : t * 128 + 128]


def project_grads(k, bn, dqkv, grads):
    for p in range(3):
        grads[:, p * 128 : p * 128 + 128] = t_dot(bn[k], dqkv[k, p]).astype(BF)


def shifted_at(c, t, row, size):
    return rows_at((c * 3 + t) * CONVR + row, size)


def conv_back_zero(pool):
    for c in range(3):
        for t in range(3):
            for i in range(IMAGES + 1):
                pool[shifted_at(c, t, i * STRIDE, 16), :] = jnp.zeros((16, 128), F32)


CONV_ROWS = 16


def conv_back(k, t, first, last, dbn, conv, moments, sums, at, gains, shifts, nrm, pool, kernels, dn, dker, inverse_total):
    mask = cell_mask(IR)
    cells = cell_mask(CB)
    lanes = slice(t * 128, t * 128 + 128)
    inv = moments[3 + k : 4 + k, lanes]

    def spread(i, carry):
        rows = rows_at(i * IR, IR)
        standard = (conv[k, rows, lanes] - moments[k : k + 1, lanes]) * inv
        shift = (sums[at + t : at + t + 1] + standard * sums[at + 3 + t : at + 4 + t]) * inverse_total
        grad = dbn[rows_at(k * R + i * IR, IR), lanes]
        grad = (gains[1 + k : 2 + k, lanes] * inv) * (grad - mask * shift)
        pool[shifted_at(0, t, i * STRIDE + 16, IR), :] = pltpu.roll(grad, 1, 0)
        pool[shifted_at(1, t, i * STRIDE + 16, IR), :] = grad
        pool[shifted_at(2, t, i * STRIDE + 16, IR), :] = pltpu.roll(grad, IR - 1, 0)
        return carry

    lax.fori_loop(0, IMAGES, spread, 0)
    taps = [kernels[o, k : k + 1, lanes] for o in range(9)]

    def step(b, found):
        base = b * STRIDE + 16
        here = nrm[1, rows_at(base, CB), lanes]
        acc = jnp.zeros((CB, 128), F32)
        new = []
        for o in range(9):
            x = pool[shifted_at(2 - o % 3, t, base - (o // 3 - 1) * 16, CB), :]
            acc = acc + x * taps[o]
            new.append(found[o] + jnp.sum((x * here).reshape(CB // 8, 8, 128), 0))
        rows = rows_at(b * CB, CB)
        if not first:
            acc = acc + dn[rows, lanes]
        dn[rows, lanes] = acc
        if last:
            new.append(found[9] + jnp.sum((acc * here).reshape(CB // 8, 8, 128), 0))
            new.append(found[10] + jnp.sum((acc * cells).reshape(CB // 8, 8, 128), 0))
        return tuple(new)

    found = lax.fori_loop(0, IMAGES, step, (jnp.zeros((8, 128), F32),) * (11 if last else 9))
    found = [col_sum(f) for f in found]
    if last:
        found[9] = (found[9] - found[10] * shifts[0:1, lanes]) / gains[0:1, lanes]
    found += [jnp.zeros((1, 128), F32)] * (CONV_ROWS - len(found))
    dker[k, :, lanes] = jnp.concatenate(found, 0)


def last_norm_back(tokp, dres, dn, gains, gtok):
    mask = cell_mask(IR)

    def step(i, carry):
        rows = rows_at(i * IR, IR)
        xhat, rstd = norm_parts(tokp[rows, :])
        scaled = dn[rows, :] * mask * gains[0:1]
        one = jnp.sum(scaled, -1, keepdims=True) * (1.0 / D)
        two = jnp.sum(scaled * xhat, -1, keepdims=True) * (1.0 / D)
        gtok[rows, :] = dres[rows, :] + rstd * (scaled - one - xhat * two)
        return carry

    lax.fori_loop(0, IMAGES, step, 0)
    gtok[GAP0:R, :] = dres[GAP0:R, :]


class GradSum:
    def __init__(self, place, grads, bufs, sems, both):
        self.place, self.grads, self.both = place, grads, both
        self.rx_core, self.rx_one, self.mid, self.rx_z, self.fin, self.done = bufs
        self.own = grads.at[place.mp]
        self.slot = place.mp if both else 0
        self.rows = grads.shape[1]
        self.quarter = self.rows // QUAD
        self.part = z_part(self.rows, place.groups)
        self.block = min(self.quarter, 128)
        self.sems = sems
        self.stage = 0
        self.pending = []
        self.steps = [[self.core_start], [self.core_end, self.quad_start], [self.quad_end, self.z_start]]
        self.steps += [[self.z_end, self.z_back_start], [self.z_back_end, self.quad_back_start]]
        self.steps += [[self.end, self.core_back_start], [self.end]] if both else [[self.end]]

    def step(self):
        for part in self.steps.pop(0):
            part()

    def copies(self, ref, triples):
        self.stage += 1
        for src, dst, peer in triples:
            remote(src, dst, self.sems.at[0], self.sems.at[self.stage], peer)
        self.pending = [Pending(ref, self.sems.at[0], self.sems.at[self.stage])]

    def end(self):
        finish(self.pending)
        self.pending = []

    def add(self, dst, dst_at, mine, mine_at, theirs, rows, lanes):
        def step(b, carry):
            at = b * self.block
            total = mine[rows_at(mine_at + at, self.block), lanes].astype(F32)
            for ref in theirs:
                total = total + ref[rows_at(at, self.block), lanes].astype(F32)
            dst[rows_at(dst_at + at, self.block), lanes] = total.astype(BF)
            return carry

        lax.fori_loop(0, rows // self.block, step, 0)

    def core_start(self):
        self.copies(self.rx_core, [(self.grads.at[1 - self.place.mp], self.rx_core, self.place.other_core())])

    def core_end(self):
        self.end()
        self.add(self.own, 0, self.own, 0, [self.rx_core], self.rows, slice(None))

    def fill(self):
        if self.part * self.place.groups > self.quarter:
            self.mid[self.quarter :, :] = jnp.zeros((self.part * self.place.groups - self.quarter, D), BF)

    def quad_start(self):
        triples = []
        for o in range(1, QUAD):
            there = rows_at(lax.rem(self.place.quad + o, QUAD) * self.quarter, self.quarter)
            triples.append((self.own.at[there], self.rx_one.at[o - 1], self.place.in_quad(o)))
        self.copies(self.rx_one, triples)

    def quad_end(self):
        self.end()
        theirs = [self.rx_one.at[o] for o in range(QUAD - 1)]
        self.add(self.mid, 0, self.own, self.place.quad * self.quarter, theirs, self.quarter, slice(None))
        self.fill()

    def z_start(self):
        triples = []
        for o in range(1, self.place.groups):
            there = rows_at(lax.rem(self.place.z + o, self.place.groups) * self.part, self.part)
            triples.append((self.mid.at[there], self.rx_z.at[o - 1], self.place.along(o)))
        self.copies(self.rx_z, triples)

    def z_end(self):
        self.end()
        here = rows_at(self.place.z * self.part, self.part)
        total = self.mid[here, :].astype(F32)
        for o in range(self.place.groups - 1):
            total = total + self.rx_z[o].astype(F32)
        self.fin[here, :] = total.astype(BF)

    def z_back_start(self):
        here = self.fin.at[rows_at(self.place.z * self.part, self.part)]
        self.copies(self.rx_z, [(here, here, self.place.along(o)) for o in range(1, self.place.groups)])

    def z_back_end(self):
        self.end()
        here = rows_at(self.place.quad * self.quarter, self.quarter)
        self.done[self.slot, here, :] = self.fin[0 : self.quarter, :]

    def quad_back_start(self):
        here = self.done.at[self.slot, rows_at(self.place.quad * self.quarter, self.quarter)]
        self.copies(self.rx_one, [(here, here, self.place.in_quad(o)) for o in range(1, QUAD)])

    def core_back_start(self):
        here = self.done.at[self.place.mp]
        self.copies(self.rx_core, [(here, here, self.place.other_core())])


def z_part(rows, groups):
    return -(-rows // QUAD // (16 * groups)) * 16


UNITS = ((2 * PW, False), (2 * PW, False), (2 * PW, False), (D, True), (D, True))


def unit_buffers(groups, rows, both):
    span = z_part(rows, groups) * groups
    dims = [(rows, D), (QUAD - 1, rows // QUAD, D), (span, D)]
    dims += [(groups - 1, span // groups, D), (span, D), (2 if both else 1, rows, D)]
    return [pltpu.VMEM((2, rows, D), BF)] + [pltpu.VMEM(d, BF) for d in dims]


def main_kernel(
    groups, seg, tokens, cot, gains, shifts, kernels, wqkv, wout, win, wmo, bias_h,
    out_hbm, gtok_hbm, dw0, dw1, dw2, dw3, dw4, rest_out,
    pool, tokp, cotp, conv, nrm, dbn, outp, dres, bn, qkv, att, n2, gm, gr, act, dpre, datt, dqkv,
    wqkv_b, wout_b, win_f, wmo_f, bias_f, stats, moments, sums, sums_v, small, dbias, dker,
    mx1, mx2, sx1, sx2, lx1, lx2, vx1, vx2, kx1, kx2, kx3, kx4,
    in_sems, w_sems, pair_s, pair_r, sems, unit_sems, out_sems, dw_sems, *unit_flat,
):
    dws = (dw0, dw1, dw2, dw3, dw4)
    unit_refs = [unit_flat[n * 7 : n * 7 + 7] for n in range(len(UNITS))]
    place = Place(groups)
    place.greet()
    copies = []
    for n, src in enumerate((tokens, cot)):
        for t in range(3):
            copy = pltpu.make_async_copy(
                src.at[0, :, pl.ds(t * 128, 128)], pool.at[pl.ds((n * 3 + t) * SCR, CELLS)], in_sems.at[n, t]
            )
            copy.start()
            copies.append(copy)
    blocks = [(wqkv.at[:, pl.ds(k * D, D)], dbn.at[pl.ds(k * D, D)]) for k in range(3)]
    blocks.append((wout, dbn.at[pl.ds(3 * D, D)]))
    for j in range(PARTS):
        blocks.append((win.at[:, pl.ds(j * PW, PW)], dbn.at[pl.ds((4 + j) * D, D), pl.ds(0, PW)]))
    blocks.append((wmo, dres.at[pl.ds(0, HH)]))
    weights = []
    for n, (src, dst) in enumerate(blocks):
        copy = pltpu.make_async_copy(src, dst, w_sems.at[n])
        copy.start()
        weights.append(copy)
    ahead = empty_before(seg)
    finish(copies)
    to_images(pool, 0, tokp, ahead)
    first_norm(tokp, gains, shifts, nrm)
    conv_forward(nrm, kernels, conv, stats)
    place.greeted()

    cells = IMAGES * IMG * IMG
    copies = send_eight(place, stats, mx1, sems.at[0, 0], sems.at[0, 1])
    mx1[place.slot] = stats[...]
    finish(weights)
    for k in range(3):
        wqkv_b[k] = dbn[k * D : k * D + D, :].astype(BF)
    wout_b[...] = dbn[3 * D : 4 * D, :].astype(BF)
    for j in range(PARTS):
        win_f[j, place.mp] = dbn[(4 + j) * D : (5 + j) * D, 0:PW].astype(BF)
        wmo_f[j, place.mp] = dres[j * PW : j * PW + PW, :].astype(BF)
    bias_f[place.mp] = jnp.broadcast_to(bias_h[...].reshape(1, HH), (8, HH))
    pairs = [
        remote(ref, ref, pair_s.at[n], pair_r.at[n], place.other_core())
        for n, ref in enumerate((win_f.at[:, place.mp], wmo_f.at[:, place.mp], bias_f.at[place.mp]))
    ]
    to_images(pool, 3 * SCR, cotp, ahead)
    finish(copies)
    mean, m2 = merge_moments(mx1, 8, cells)
    mx2[place.z, 0:3] = mean
    mx2[place.z, 3:6] = m2
    mx2[place.z, 6:8] = jnp.zeros((2, D), F32)
    finish(send_along(place, mx2.at[place.z], mx2, sems.at[0, 0], sems.at[0, 2]))
    mean, m2 = merge_moments(mx2, groups, 8 * cells)
    moments[0:3] = mean
    moments[3:6] = lax.rsqrt(m2 * (1.0 / (cells * 8 * groups)) + EPS)
    moments[6:8] = jnp.zeros((2, D), F32)

    project(conv, moments, gains, shifts, wqkv_b, bn, qkv)
    attend(qkv, pool, att)
    attend_gap(qkv, att)
    feed_forward_in(tokp, cotp, att, wout_b, gains, shifts, dres, n2, gm, small)
    finish(pairs)

    units = []
    for n, (rows, both) in enumerate(UNITS):
        units.append(GradSum(place, unit_refs[n][0], unit_refs[n][1:], unit_sems.at[n], both))
    ua, ub, ue, uc, ud = units
    grads = [refs[0] for refs in unit_refs]
    acc = dbn.at[pl.ds(0, R)]
    mine, theirs = place.mp, 1 - place.mp
    stores = []

    def keep(at, ref=None):
        def done(total):
            rest_out[at : at + total.shape[0], 0 : total.shape[1]] = total
            if ref is not None:
                ref[...] = total

        return done

    def keep_small(total):
        rest_out[80:88] = total
        tiles = [total[4 + c // 3 : 5 + c // 3, c % 3 * 128 : c % 3 * 128 + 128] for c in range(BIAS_TILES)]
        for c in range(BIAS_TILES // 2):
            at = c // 2 * 4 + c % 2
            kept = jnp.where(place.mp == 0, tiles[at], tiles[at + 2])
            rest_out[72 + c // 2 : 73 + c // 2, c % 2 * 128 : c % 2 * 128 + 128] = kept

    small_sum = SmallSum(place, small, lx1, lx2, sems, 2, keep_small)
    sum_v = SmallSum(place, sums_v, vx1, vx2, sems, 6, keep(64, sums_v))
    sum_qk = SmallSum(place, sums, sx1, sx2, sems, 1, keep(0, sums))
    ker_sums = [
        PairedSum(place, dker.at[k], *(x.at[k] for x in (kx1, kx2, kx3, kx4)), sems, 3 + k, keep(16 + 16 * k))
        for k in range(3)
    ]

    def forward(part):
        hidden_part(part, n2, gm, win_f, wmo_f, bias_f, act, dpre, outp, acc, dbias)

    def hidden(half, part):
        hidden_grads(half, n2, gm, act, dpre, grads[part])
        if half is theirs:
            units[part].step()

    def values():
        attend_back_values(pool, datt, dqkv)

    def after_forward():
        feed_forward_out(cotp, wout_b, gains, shifts, outp, acc, dres, gr, datt, small)
        for c in range(BIAS_TILES):
            tile = slice(c % 4 * 128, c % 4 * 128 + 128)
            small[4 + c // 3 : 5 + c // 3, c % 3 * 128 : c % 3 * 128 + 128] = dbias[c // 4, 0:1, tile]
        small_sum.start()
        attend_back_gap(datt, dqkv)
        stores.append(pltpu.make_async_copy(outp, out_hbm, out_sems.at[0]))
        stores[0].start()

    def out_grad():
        for p in range(3):
            grads[3][1, p * 128 : p * 128 + 128, :] = t_dot(att[p], gr[...]).astype(BF)

    def value_grads():
        project_grads(2, bn, dqkv, grads[3].at[0])
        uc.step()

    def query_grads():
        for k in range(2):
            project_grads(k, bn, dqkv, grads[4].at[k])
        ud.step()

    def value_back():
        project_back(2, conv, moments, wqkv_b, dqkv, dbn, sums_v, 0)
        sum_v.start()

    def query_back(k):
        project_back(k, conv, moments, wqkv_b, dqkv, dbn, sums, 6 * k)
        if k == 1:
            sum_qk.start()

    def back(k, t):
        held, at = (sums_v, 0) if k == 2 else (sums, 6 * k)
        conv_back(
            k, t, k == 0, k == 2, dbn, conv, moments, held, at, gains, shifts, nrm, pool, kernels, cotp, dker,
            1.0 / (cells * 8 * groups),
        )
        if t == 2:
            ker_sums[k].start()

    def last_norm():
        stores[0].wait()
        last_norm_back(tokp, dres, cotp, gains, outp)
        stores.append(pltpu.make_async_copy(outp, gtok_hbm, out_sems.at[1]))
        stores[-1].start()

    def unit(n):
        units[n].step()
        if not units[n].steps:
            stores.append(pltpu.make_async_copy(units[n].done, dws[n], dw_sems.at[n]))
            stores[-1].start()

    forward(0)
    hidden(theirs, 0)
    hidden(mine, 0)
    forward(1)
    unit(0)
    hidden(theirs, 1)
    hidden(mine, 1)
    forward(2)
    unit(1)
    hidden(theirs, 2)
    hidden(mine, 2)
    after_forward()
    unit(0)
    unit(2)
    attend_back(0, 2, qkv, pool, datt, dqkv)
    attend_back(2, 4, qkv, pool, datt, dqkv)
    unit(0)
    small_sum.step()
    unit(1)
    query_back(0)
    query_back(1)
    values()
    unit(0)
    unit(2)
    out_grad()
    value_grads()
    sum_qk.step()
    small_sum.step()
    unit(1)
    unit(3)
    query_grads()
    unit(2)
    value_back()
    unit(0)
    unit(4)
    sum_qk.step()
    unit(1)
    conv_back_zero(pool)
    back(0, 0)
    back(0, 1)
    unit(3)
    unit(2)
    back(0, 2)
    sum_v.step()
    back(1, 0)
    ker_sums[0].step()
    back(1, 1)
    unit(4)
    back(1, 2)
    unit(3)
    ker_sums[1].step()
    sum_v.step()
    back(2, 0)
    back(2, 1)
    unit(1)
    unit(4)
    back(2, 2)
    last_norm()
    ker_sums[2].step()
    unit(3)
    unit(2)
    ker_sums[0].step()
    ker_sums[1].step()
    unit(4)
    ker_sums[2].step()
    unit(3)
    ker_sums[0].step()
    ker_sums[1].step()
    unit(3)
    ker_sums[2].step()
    unit(4)
    ker_sums[1].step()
    ker_sums[2].step()
    ker_sums[0].step()
    unit(4)
    finish(stores[1:])


def main_call(groups, *args):
    units = [buf for unit in UNITS for buf in unit_buffers(groups, *unit)]
    return pl.pallas_call(
        functools.partial(main_kernel, groups),
        out_shape=(shape(R, D), shape(R, D))
        + tuple(shape(2 if both else 1, rows, D, dtype=BF) for rows, both in UNITS)
        + (shape(88, D),),
        in_specs=[VM, ANY, ANY, VM, VM, VM, ANY, ANY, ANY, ANY, VM],
        out_specs=(ANY,) * 7 + (VM,),
        scratch_shapes=[
            pltpu.VMEM((POOL, 128), F32),
            pltpu.VMEM((R, D), F32), pltpu.VMEM((R, D), F32), pltpu.VMEM((3, R, D), F32),
            pltpu.VMEM((3, CONVR, D), F32), pltpu.VMEM((3 * R, D), F32),
            pltpu.VMEM((R, D), F32), pltpu.VMEM((R, D), F32),
            pltpu.VMEM((3, R, D), BF), pltpu.VMEM((3, 3, R, 128), BF), pltpu.VMEM((3, R, 128), BF),
            pltpu.VMEM((R, D), BF), pltpu.VMEM((R, D), BF), pltpu.VMEM((R, D), BF),
            pltpu.VMEM((R, 512), BF), pltpu.VMEM((R, 512), BF), pltpu.VMEM((3, R, 128), BF), pltpu.VMEM((3, 3, R, 128), BF),
            pltpu.VMEM((3, D, D), BF), pltpu.VMEM((D, D), BF), pltpu.VMEM((PARTS, 2, D, PW), BF), pltpu.VMEM((PARTS, 2, PW, D), BF),
            pltpu.VMEM((2, 8, HH), F32),
            pltpu.VMEM((8, D), F32), pltpu.VMEM((8, D), F32), pltpu.VMEM((16, 128), F32), pltpu.VMEM((8, 128), F32),
            pltpu.VMEM((8, D), F32), pltpu.VMEM((PARTS, 8, 2 * PW), F32), pltpu.VMEM((3, CONV_ROWS, D), F32),
            pltpu.VMEM((8, 8, D), F32), pltpu.VMEM((groups, 8, D), F32),
            pltpu.VMEM((8, 16, 128), F32), pltpu.VMEM((groups, 16, 128), F32),
            pltpu.VMEM((8, 8, D), F32), pltpu.VMEM((groups, 8, D), F32),
            pltpu.VMEM((8, 8, 128), F32), pltpu.VMEM((groups, 8, 128), F32),
            pltpu.VMEM((3, 8, D), F32), pltpu.VMEM((3, QUAD, 8, D), F32), pltpu.VMEM((3, groups, 8, D), F32),
            pltpu.VMEM((3, CONV_ROWS, D), F32),
            dma(2, 3), dma(8), dma(3), dma(3), dma(7, 5), dma(5, 7), dma(2), dma(5),
        ] + units,
        compiler_params=params(collective_id=0, has_side_effects=True),
    )(*args)


def last_kernel(
    seg, outp, gtok, dwa, dwb, dwe, dwc, dwd, rest,
    output, grad_tokens, grad_gains, grad_shifts, grad_kernels, grad_qkv, grad_out, grad_in, grad_bias, grad_down,
    held, lowa, lowb, lowe, lowc, lowd, scr, wide, turned, in_sems, out_sems,
):
    loads = []
    pairs = ((outp, held.at[0]), (gtok, held.at[1]))
    pairs += ((dwa, lowa), (dwb, lowb), (dwe, lowe), (dwc, lowc), (dwd, lowd))
    for n, (src, dst) in enumerate(pairs):
        copy = pltpu.make_async_copy(src, dst, in_sems.at[n])
        copy.start()
        loads.append(copy)
    starts, gaps = find_columns(seg)
    stores = []

    def store(src, dst):
        copy = pltpu.make_async_copy(src, dst, out_sems.at[len(stores)])
        copy.start()
        stores.append(copy)

    for n, dst in enumerate((output, grad_tokens)):
        loads[n].wait()
        to_canvas(held.at[n], scr.at[n], starts, gaps)
        for t in range(3):
            store(scr.at[n, t, pl.ds(0, CELLS)], dst.at[0, :, pl.ds(t * 128, 128)])
    for n, low in enumerate((lowa, lowb, lowe)):
        loads[2 + n].wait()
        start, size = n * PW, PW
        turned[:, start : start + size] = low[0, 0:size, :].astype(F32).T
        wide[start : start + size, :] = low[0, size : 2 * size, :].astype(F32)
        store(turned.at[:, pl.ds(start, size)], grad_in.at[:, pl.ds(start, size)])
        store(wide.at[pl.ds(start, size)], grad_down.at[pl.ds(start, size)])
    for n, low in enumerate((lowc, lowd)):
        loads[5 + n].wait()
        for j in range(2):
            at = HH + (n * 2 + j) * D
            wide[at : at + D, :] = low[j].astype(F32)
            here = wide.at[pl.ds(at, D)]
            if n == 0 and j == 1:
                store(here, grad_out)
            else:
                store(here, grad_qkv.at[:, pl.ds((2 if n == 0 else j) * D, D)])
    for k in range(3):
        for o in range(9):
            row = 16 + k * CONV_ROWS + o
            grad_kernels[o, k : k + 1] = rest[row : row + 1]
    grad_gains[0:1] = rest[57:58]
    grad_gains[4:5] = rest[80:81]
    grad_shifts[0:1] = rest[58:59]
    grad_shifts[3:6] = rest[81:84]
    for t in range(3):
        lanes = slice(t * 128, t * 128 + 128)
        for k, at in enumerate((0, 6, 64)):
            grad_gains[1 + k : 2 + k, lanes] = rest[at + 3 + t : at + 4 + t, 0:128]
            if k != 1:
                grad_shifts[1 + k // 2 : 2 + k // 2, lanes] = rest[at + t : at + t + 1, 0:128]
    for j in range(PARTS):
        grad_bias[j * PW : j * PW + PW] = rest[72 + j, 0:PW]
    finish(stores)


def last_call(*args):
    return pl.pallas_call(
        last_kernel,
        out_shape=(
            shape(1, CELLS, D), shape(1, CELLS, D), shape(5, D), shape(6, D), shape(9, 3, D), shape(D, 3 * D),
            shape(D, D), shape(D, HH), shape(HH), shape(HH, D),
        ),
        in_specs=[SM] + [ANY] * 7 + [VM],
        out_specs=(ANY, ANY, VM, VM, VM, ANY, ANY, ANY, VM, ANY),
        scratch_shapes=[
            pltpu.VMEM((2, R, D), F32),
            *(pltpu.VMEM((2 if both else 1, rows, D), BF) for rows, both in UNITS),
            pltpu.VMEM((2, 3, CELLS + 16, 128), F32), pltpu.VMEM((HH + 4 * D, D), F32),
            pltpu.VMEM((D, HH), F32), dma(7), dma(16),
        ],
        compiler_params=params(),
    )(*args)


def local(
    groups, tokens, segment_ids, gains, shifts, kernels, qkv_weight, out_weight,
    mlp_in_weight, mlp_in_bias, mlp_out_weight, cotangent,
):
    found = main_call(
        groups, segment_ids, tokens, cotangent, gains, shifts, kernels.transpose(1, 0, 2),
        qkv_weight, out_weight, mlp_in_weight, mlp_out_weight, mlp_in_bias,
    )
    outs = list(last_call(segment_ids, *found))
    outs[4] = outs[4].transpose(1, 0, 2)
    return tuple(outs)


def solution(mesh):
    groups = mesh.shape["dp"] // QUAD
    both = P(("dp", "mp"), None, None)
    return jax.shard_map(
        functools.partial(local, groups),
        mesh=mesh,
        in_specs=(
            both, P(("dp", "mp"), None), P(), P(), P(), P(), P(), P(None, "mp"), P("mp"), P("mp", None), both,
        ),
        out_specs=(both, both, P(), P(), P(), P(), P(), P(None, "mp"), P("mp"), P("mp", None)),
        check_vma=False,
    )
```

```python
import functools
import math

import jax
import jax.numpy as jnp
from jax import lax
from jax.experimental import pallas as pl
from jax.experimental.pallas import tpu as pltpu
from jax.sharding import PartitionSpec as P

F32 = jnp.float32
BF = jnp.bfloat16
MESH = pl.DeviceIdType.MESH
D = 384
IMG = 14
IMAGES = 4
CW = 64
CELLS = IMG * CW
IR = 224
GAP0 = IMAGES * IR
GAPS = 112
R = 1024
DCH = 1024
STRIDE = IR + 16
CONVR = IMAGES * STRIDE + 16
EPS = 1e-05
MASKED = -1e30
QUAD = 4
HH = 2 * D
VLIM = 62 * 2**20
SCALE = 0.125
PCH = 512


def params(**kw):
    return pltpu.CompilerParams(vmem_limit_bytes=VLIM, **kw)


VM = pl.BlockSpec(memory_space=pltpu.VMEM)
SM = pl.BlockSpec(memory_space=pltpu.SMEM)
ANY = pl.BlockSpec(memory_space=pl.ANY)


def shape(*dims, dtype=F32):
    return jax.ShapeDtypeStruct(dims, dtype)


def dot(a, b):
    return jnp.dot(a, b, preferred_element_type=F32)


def dot_t(a, b):
    return lax.dot_general(a, b, (((1,), (1,)), ((), ())), preferred_element_type=F32)


def t_dot(a, b):
    return lax.dot_general(a, b, (((0,), (0,)), ((), ())), preferred_element_type=F32)


def cell_mask(rows):
    row = lax.broadcasted_iota(jnp.int32, (rows, 1), 0)
    return (row % 16 < IMG).astype(F32)


def rows_at(start, size, align=16):
    return pl.ds(pl.multiple_of(start, align), size)


def find_columns(seg):
    def step(col, found):
        count, starts, gaps = found
        here = seg[0, col]
        starts = tuple(jnp.minimum(s, jnp.where(here == i + 1, col, CW)) for i, s in enumerate(starts))
        empty = here == 0
        gaps = tuple(jnp.where(empty & (count == k), col, g) for k, g in enumerate(gaps))
        return count + jnp.where(empty, 1, 0), starts, gaps

    start = (jnp.int32(0), (jnp.int32(CW),) * IMAGES, (jnp.int32(0),) * 8)
    _, starts, gaps = lax.fori_loop(0, CW, step, start)
    return starts, gaps


SCR = CELLS + 16
POOL = 48 * IR


def empty_before(seg):
    lane = lax.broadcasted_iota(jnp.int32, (1, 128), 1)
    ids = seg[0:1, 0:128]
    firsts = [jnp.where((ids == i + 1) & (lane < CW), lane, CW).astype(F32) for i in range(IMAGES)]
    return [jnp.min(f, -1, keepdims=True) - float(i * IMG) for i, f in enumerate(firsts)]


def to_images(pool, base, out, ahead):
    col = lax.broadcasted_iota(jnp.int32, (16, 128), 0)
    sub = lax.broadcasted_iota(jnp.int32, (8, 128), 0).astype(F32)
    before = sum([jnp.where(a <= sub, 1.0, 0.0) for a in ahead])

    def step(r, carry):
        for t in range(3):
            row = base + t * SCR + r * CW
            for i in range(IMAGES):
                window = pool[pl.ds(row + i * IMG, 16), :]
                for e in range(1, 9):
                    moved = pool[pl.ds(row + i * IMG + e, 16), :]
                    window = jnp.where(ahead[i] == float(e), moved, window)
                out[rows_at(i * IR + r * 16, 16), t * 128 : t * 128 + 128] = jnp.where(col < IMG, window, 0.0)
            block = pool[rows_at(row, 8, 8), :]
            for n in range(1, IMAGES + 1):
                block = jnp.where(before == float(n), pool[pl.ds(row + n * IMG, 8), :], block)
            out[rows_at(GAP0 + r * 8, 8, 8), t * 128 : t * 128 + 128] = block
        return carry

    lax.fori_loop(0, IMG, step, 0)
    out[GAP0 + GAPS : R, :] = jnp.zeros((R - GAP0 - GAPS, D), F32)


def to_canvas(src, scr, starts, gaps):
    def step(r, carry):
        for t in range(3):
            for i in range(IMAGES):
                block = src[rows_at(i * IR + r * 16, 16), t * 128 : t * 128 + 128]
                scr[t, pl.ds(r * CW + starts[i], 16), :] = block
            block = src[rows_at(GAP0 + r * 8, 8, 8), t * 128 : t * 128 + 128]
            for k in range(8):
                scr[t, pl.ds(r * CW + gaps[k], 1), :] = block[k : k + 1]
        return carry

    lax.fori_loop(0, IMG, step, 0)


def norm_parts(x):
    mean = jnp.sum(x, -1, keepdims=True) * (1.0 / D)
    centred = x - mean
    var = jnp.sum(centred * centred, -1, keepdims=True) * (1.0 / D)
    rstd = lax.rsqrt(var + EPS)
    return centred * rstd, rstd


def store_shifted(dst, i, t, x):
    lanes = slice(t * 128, t * 128 + 128)
    at = rows_at(i * STRIDE + 16, IR)
    dst[0, at, lanes] = pltpu.roll(x, 1, 0)
    dst[1, at, lanes] = x
    dst[2, at, lanes] = pltpu.roll(x, IR - 1, 0)


def zero_borders(dst):
    for i in range(IMAGES + 1):
        for c in range(3):
            dst[c, i * STRIDE : i * STRIDE + 16, :] = jnp.zeros((16, D), F32)


def first_norm(tokp, gains, shifts, nrm):
    zero_borders(nrm)
    mask = cell_mask(IR)

    def step(i, carry):
        xhat, _ = norm_parts(tokp[rows_at(i * IR, IR), :])
        normed = (xhat * gains[0:1] + shifts[0:1]) * mask
        for t in range(3):
            store_shifted(nrm, i, t, normed[:, t * 128 : t * 128 + 128])
        return carry

    lax.fori_loop(0, IMAGES, step, 0)


CB = 224


def conv_forward(nrm, kernels, conv, stats):
    mask = cell_mask(CB)
    blocks = IMAGES * IR // CB
    per = IR // CB
    for t in range(3):
        lanes = slice(t * 128, t * 128 + 128)
        taps = [[kernels[o, k : k + 1, lanes] for o in range(9)] for k in range(3)]

        def step(b, sums):
            base = (b // per) * STRIDE + 16 + (b % per) * CB
            acc = [jnp.zeros((CB, 128), F32)] * 3
            for o in range(9):
                x = nrm[o % 3, rows_at(base + (o // 3 - 1) * 16, CB), lanes]
                for k in range(3):
                    acc[k] = acc[k] + x * taps[k][o]
            new = []
            for k in range(3):
                conv[k, rows_at(b * CB, CB), lanes] = acc[k]
                new.append(sums[k] + jnp.sum((acc[k] * mask).reshape(CB // 8, 8, 128), 0))
            return tuple(new)

        sums = lax.fori_loop(0, blocks, step, (jnp.zeros((8, 128), F32),) * 3)
        means = [jnp.sum(s, 0, keepdims=True) * (1.0 / (IMAGES * IMG * IMG)) for s in sums]

        def spread(b, sums):
            new = []
            for k in range(3):
                away = (conv[k, rows_at(b * CB, CB), lanes] - means[k]) * mask
                new.append(sums[k] + jnp.sum((away * away).reshape(CB // 8, 8, 128), 0))
            return tuple(new)

        squares = lax.fori_loop(0, blocks, spread, (jnp.zeros((8, 128), F32),) * 3)
        for k in range(3):
            stats[k : k + 1, lanes] = means[k]
            stats[3 + k : 4 + k, lanes] = jnp.sum(squares[k], 0, keepdims=True)
        stats[6:8, lanes] = jnp.zeros((2, 128), F32)
    for k in range(3):
        conv[k, GAP0:R, :] = jnp.zeros((R - GAP0, D), F32)


class Place:
    def __init__(self, groups):
        dp = lax.axis_index("dp")
        self.mp = lax.axis_index("mp")
        self.groups = groups
        self.quad = lax.rem(dp, QUAD)
        self.z = dp // QUAD
        self.slot = self.quad * 2 + self.mp

    def in_eight(self, offset):
        other = lax.rem(self.slot + offset, 8)
        return (self.z * QUAD + other // 2, lax.rem(other, 2))

    def in_quad(self, offset):
        return (self.z * QUAD + lax.rem(self.quad + offset, QUAD), self.mp)

    def along(self, offset):
        return (lax.rem(self.z + offset, self.groups) * QUAD + self.quad, self.mp)

    def other_core(self):
        return (self.z * QUAD + self.quad, 1 - self.mp)

    def peers(self):
        return [self.in_eight(o) for o in range(1, 8)] + [self.along(o) for o in range(1, self.groups)]

    def greet(self):
        barrier = pltpu.get_barrier_semaphore()
        for peer in self.peers():
            pl.semaphore_signal(barrier, inc=1, device_id=peer, device_id_type=MESH)

    def greeted(self):
        pl.semaphore_wait(pltpu.get_barrier_semaphore(), 7 + self.groups - 1)


def remote(src, dst, send, recv, peer):
    copy = pltpu.make_async_remote_copy(
        src_ref=src, dst_ref=dst, send_sem=send, recv_sem=recv, device_id=peer, device_id_type=MESH
    )
    copy.start()
    return copy


def send_eight(place, src, rx, send, recv):
    for o in range(1, 8):
        remote(src, rx.at[place.slot], send, recv, place.in_eight(o))
    return Pending(rx.at[pl.ds(0, 7)], send, recv)


def send_along(place, src, rx, send, recv):
    for o in range(1, place.groups):
        remote(src, rx.at[place.z], send, recv, place.along(o))
    return Pending(rx.at[pl.ds(0, place.groups - 1)], send, recv)


class Pending:
    def __init__(self, ref, send, recv):
        self.ref, self.sems = ref, (send, recv)

    def wait(self):
        for sem in self.sems:
            pltpu.make_async_copy(self.ref, self.ref, sem).wait()


def finish(copies):
    for copy in copies if isinstance(copies, list) else [copies]:
        copy.wait()


def sum_slots(rx, count):
    total = rx[0].astype(F32)
    for s in range(1, count):
        total = total + rx[s].astype(F32)
    return total


class SmallSum:
    def __init__(self, place, src, rx1, rx2, sems, n, done):
        self.place, self.src, self.rx1, self.rx2, self.done = place, src, rx1, rx2, done
        self.sems = [sems.at[n, i] for i in range(3)]
        self.steps = [self.middle, self.end]

    def start(self):
        self.copies = send_eight(self.place, self.src, self.rx1, self.sems[0], self.sems[1])
        self.rx1[self.place.slot] = self.src[...]

    def step(self):
        self.steps.pop(0)()

    def middle(self):
        finish(self.copies)
        self.rx2[self.place.z] = sum_slots(self.rx1, 8).astype(self.rx2.dtype)
        self.copies = send_along(self.place, self.rx2.at[self.place.z], self.rx2, self.sems[0], self.sems[2])

    def end(self):
        finish(self.copies)
        self.done(sum_slots(self.rx2, self.place.groups))


class PairedSum:
    def __init__(self, place, src, rx_core, rx_quad, rx_z, both, sems, n, done):
        self.place, self.src, self.both, self.done = place, src, both, done
        self.rx_core, self.rx_quad, self.rx_z = rx_core, rx_quad, rx_z
        self.sems = [sems.at[n, i] for i in range(5)]
        self.steps = [self.quad, self.along, self.core_back, self.end]

    def exchange(self, stage, ref, src, dst, peers):
        for peer in peers:
            remote(src, dst, self.sems[0], self.sems[stage], peer)
        self.copies = Pending(ref, self.sems[0], self.sems[stage])

    def half(self, mp):
        return rows_at(mp * 8, 8, 8)

    def start(self):
        there = self.src.at[self.half(1 - self.place.mp)]
        self.exchange(1, self.rx_core, there, self.rx_core, [self.place.other_core()])

    def step(self):
        finish(self.copies)
        self.steps.pop(0)()

    def quad(self):
        slot = self.place.quad
        self.rx_quad[slot] = self.src[self.half(self.place.mp), :] + self.rx_core[...]
        here = self.rx_quad.at[slot]
        peers = [self.place.in_quad(o) for o in range(1, QUAD)]
        self.exchange(2, self.rx_quad.at[pl.ds(0, QUAD - 1)], here, here, peers)

    def along(self):
        self.rx_z[self.place.z] = sum_slots(self.rx_quad, QUAD)
        here = self.rx_z.at[self.place.z]
        peers = [self.place.along(o) for o in range(1, self.place.groups)]
        self.exchange(3, self.rx_z.at[pl.ds(0, self.place.groups - 1)], here, here, peers)

    def core_back(self):
        self.both[self.half(self.place.mp), :] = sum_slots(self.rx_z, self.place.groups)
        here = self.both.at[self.half(self.place.mp)]
        self.exchange(4, here, here, here, [self.place.other_core()])

    def end(self):
        self.done(self.both[...])


def merge_moments(rx, count, cells):
    mean = sum([rx[s, 0:3] for s in range(1, count)], rx[0, 0:3]) * (1.0 / count)
    m2 = sum([rx[s, 3:6] for s in range(1, count)], rx[0, 3:6])
    for s in range(count):
        away = rx[s, 0:3] - mean
        m2 = m2 + away * away * float(cells)
    return mean, m2


def dma(*n):
    return pltpu.SemaphoreType.DMA(n)


def project(conv, moments, gains, shifts, wqkv, bn, qkv):
    def step(c, carry):
        rows = rows_at(c * DCH, DCH)
        for k in range(3):
            standard = (conv[k, rows, :] - moments[k : k + 1]) * moments[3 + k : 4 + k]
            value = standard * gains[1 + k : 2 + k]
            if k != 1:
                value = value + (shifts[1:2] if k == 0 else shifts[2:3])
            value = value.astype(BF)
            bn[k, rows, :] = value
            out = dot(value, wqkv[k]).astype(BF)
            if k == 0:
                out = (out * SCALE).astype(BF)
            for p in range(3):
                qkv[k, p, rows, :] = out[:, p * 128 : p * 128 + 128]
        return carry

    lax.fori_loop(0, R // DCH, step, 0)


def key_bias():
    row = lax.broadcasted_iota(jnp.int32, (16, 256), 0)
    return jnp.where(row < IMG, 0.0, MASKED)


def query_mask():
    lane = lax.broadcasted_iota(jnp.int32, (1, 256), 1)
    return (lane < IR).astype(F32)


def by_head(x):
    lane = lax.broadcasted_iota(jnp.int32, x.shape, 1)
    zero = jnp.zeros_like(x)
    return jnp.concatenate([jnp.where(lane < 64, x, zero), jnp.where(lane < 64, zero, x)], 0)


def own_columns(x, rows):
    lane = lax.broadcasted_iota(jnp.int32, (IR, 128), 1)
    return jnp.where(lane < 64, x[:IR], x[rows : rows + IR])


def probs_at(pool, n):
    return [rows_at((2 * n + half) * IR, IR) for half in range(2)]


def attend(qkv, pool, att):
    bias = key_bias()[None]
    live = query_mask()

    def step(i, carry):
        rows = rows_at(i * IR, IR)
        for p in range(3):
            q = qkv[0, p, rows_at(i * IR, 256), :]
            both = dot_t(by_head(qkv[1, p, rows, :]), q)
            low = []
            for h in range(2):
                scores = (both[h * IR : h * IR + IR].reshape(IMG, 16, 256) + bias).reshape(IR, 256)
                largest = jnp.max(scores, 0, keepdims=True)
                expo = jnp.exp(scores - largest)
                soft = expo * (live / jnp.sum(expo, 0, keepdims=True))
                for half, at in enumerate(probs_at(pool, (i * 3 + p) * 2 + h)):
                    pool[at, :] = soft[:, half * 128 : half * 128 + 128]
                low.append(soft.astype(BF))
            out = t_dot(jnp.concatenate(low, 1), qkv[2, p, rows, :])
            att[p, rows, :] = own_columns(out, 256).astype(BF)
        return carry

    lax.fori_loop(0, IMAGES, step, 0, unroll=4)


def even_prob():
    return jnp.full((1, 1), 1.0 / GAPS, F32).astype(BF).astype(F32)


def attend_gap(qkv, att):
    for p in range(3):
        v = qkv[2, p, GAP0 : GAP0 + 16, :].astype(F32)
        out = (v * (even_prob() * float(GAPS))).astype(BF)
        for b in range((R - GAP0) // 16):
            att[p, GAP0 + b * 16 : GAP0 + b * 16 + 16, :] = out


def gelu_parts(x):
    cdf = 0.5 * (1.0 + lax.erf(x * (1.0 / math.sqrt(2.0))))
    density = jnp.exp(x * x * -0.5) * (1.0 / math.sqrt(2.0 * math.pi))
    return x * cdf, cdf + x * density


def col_sum(x):
    return jnp.sum(x, 0, keepdims=True)


def feed_forward_in(tokp, cotp, att, wout, gains, shifts, dres, n2, gm, small):
    small[...] = jnp.zeros((8, D), F32)

    def step(c, carry):
        rows = rows_at(c * DCH, DCH)
        attended = jnp.concatenate([att[p, rows, :] for p in range(3)], 1)
        residual = tokp[rows, :] + (dot(attended, wout[...]) + shifts[3:4])
        dres[rows, :] = residual
        xhat, _ = norm_parts(residual)
        n2[rows, :] = (xhat * gains[4:5] + shifts[4:5]).astype(BF)
        cot = cotp[rows, :]
        gm[rows, :] = cot.astype(BF)
        small[3:4] = small[3:4] + col_sum(cot)
        return carry

    lax.fori_loop(0, R // DCH, step, 0)


HCH = 1024
PARTS = 3
PW = HH // PARTS
BIAS_TILES = 2 * HH // 128


def hidden_part(part, n2, gm, win, wmo, bias, act, dpre, outp, acc, dbias):
    both = slice(0, 2 * PW)
    dbias[part, 0:1, :] = jnp.zeros((1, 2 * PW), F32)

    def step(c, carry):
        rows = rows_at(c * HCH, HCH)
        up = jnp.concatenate([win[part, h] for h in range(2)], 1)
        down = wmo[part].reshape(2 * PW, D)
        shift = jnp.concatenate([bias[h, 0:1, part * PW : part * PW + PW] for h in range(2)], 1)
        value, slope = gelu_parts(dot(n2[rows, :], up) + shift)
        value = value.astype(BF)
        act[rows, both] = value
        grad = dot_t(gm[rows, :], down) * slope
        dbias[part, 0:1, both] = dbias[part, 0:1, both] + col_sum(grad)
        grad = grad.astype(BF)
        dpre[rows, both] = grad
        forward = dot(value, down)
        back = dot_t(grad, up)
        outp[rows, :] = forward if part == 0 else outp[rows, :] + forward
        acc[rows, :] = back if part == 0 else acc[rows, :] + back
        return carry

    lax.fori_loop(0, R // HCH, step, 0)


def hidden_grads(half, n2, gm, act, dpre, grads):
    units = pl.ds(pl.multiple_of(half * PW, 128), PW)
    grads[half, 0:PW, :] = t_dot(dpre[:, units], n2[...]).astype(BF)
    grads[half, PW : 2 * PW, :] = t_dot(act[:, units], gm[...]).astype(BF)


def feed_forward_out(cotp, wout, gains, shifts, outp, acc, dres, gr, datt, small):
    def step(c, carry):
        rows = rows_at(c * DCH, DCH)
        residual = dres[rows, :]
        outp[rows, :] = residual + outp[rows, :] + shifts[5:6]
        xhat, rstd = norm_parts(residual)
        grad = acc[rows, :]
        scaled = grad * gains[4:5]
        one = jnp.sum(scaled, -1, keepdims=True) * (1.0 / D)
        two = jnp.sum(scaled * xhat, -1, keepdims=True) * (1.0 / D)
        total = cotp[rows, :] + rstd * (scaled - one - xhat * two)
        dres[rows, :] = total
        low = total.astype(BF)
        gr[rows, :] = low
        back = dot_t(low, wout[...]).astype(BF)
        for p in range(3):
            datt[p, rows, :] = back[:, p * 128 : p * 128 + 128]
        small[0:1] = small[0:1] + col_sum(grad * xhat)
        small[1:2] = small[1:2] + col_sum(total)
        small[2:3] = small[2:3] + col_sum(grad)
        return carry

    lax.fori_loop(0, R // DCH, step, 0)


def attend_back_values(pool, datt, dqkv):
    def step(i, carry):
        rows = rows_at(i * IR, IR)
        for p in range(3):
            low = []
            for h in range(2):
                soft = [pool[at, :] for at in probs_at(pool, (i * 3 + p) * 2 + h)]
                low.append(jnp.concatenate(soft, 1).astype(BF))
            dv = dot(jnp.concatenate(low, 0), datt[p, rows_at(i * IR, 256), :])
            dqkv[2, p, rows, :] = own_columns(dv, IR).astype(BF)
        return carry

    lax.fori_loop(0, IMAGES, step, 0)


def attend_back(first, last, qkv, pool, datt, dqkv):
    def step(i, carry):
        rows = rows_at(i * IR, IR)
        wide = rows_at(i * IR, 256)
        for p in range(3):
            both = dot_t(by_head(qkv[2, p, rows, :]), datt[p, wide, :])
            ds = []
            for h in range(2):
                soft = jnp.concatenate([pool[at, :] for at in probs_at(pool, (i * 3 + p) * 2 + h)], 1)
                grad = both[h * IR : h * IR + IR]
                delta = jnp.sum(soft * grad, 0, keepdims=True)
                ds.append((soft * (grad - delta)).astype(BF))
            dk = dot(jnp.concatenate(ds, 0), qkv[0, p, wide, :])
            dq = t_dot(jnp.concatenate(ds, 1), qkv[1, p, rows, :])
            dqkv[0, p, rows, :] = (own_columns(dq, 256) * SCALE).astype(BF)
            dqkv[1, p, rows, :] = own_columns(dk, IR).astype(BF)
        return carry

    lax.fori_loop(first, last, step, 0, unroll=2)


def attend_back_gap(datt, dqkv):
    for p in range(3):
        total = col_sum(datt[p, GAP0 : GAP0 + GAPS, :].astype(F32))
        grad = jnp.broadcast_to((total * even_prob()).astype(BF), (16, 128))
        zero = jnp.zeros((16, 128), BF)
        for b in range((R - GAP0) // 16):
            rows = slice(GAP0 + b * 16, GAP0 + b * 16 + 16)
            dqkv[0, p, rows, :] = zero
            dqkv[1, p, rows, :] = zero
            dqkv[2, p, rows, :] = grad if b < GAPS // 16 else zero


def project_back(k, conv, moments, wqkv, dqkv, dbn, sums, at):
    def step(c, carry):
        rows = rows_at(c * PCH, PCH)
        grad = jnp.concatenate([dqkv[k, p, rows, :] for p in range(3)], 1)
        back = dot_t(grad, wqkv[k])
        dbn[rows_at(k * R + c * PCH, PCH), :] = back
        standard = (conv[k, rows, :] - moments[k : k + 1]) * moments[3 + k : 4 + k]
        return carry[0] + col_sum(back), carry[1] + col_sum(back * standard)

    found = lax.fori_loop(0, R // PCH, step, (jnp.zeros((1, D), F32),) * 2)
    for n in range(2):
        for t in range(3):
            row = at + n * 3 + t
            sums[row : row + 1] = found[n][:, t * 128 : t * 128 + 128]


def project_grads(k, bn, dqkv, grads):
    for p in range(3):
        grads[:, p * 128 : p * 128 + 128] = t_dot(bn[k], dqkv[k, p]).astype(BF)


def shifted_at(c, t, row, size):
    return rows_at((c * 3 + t) * CONVR + row, size)


def conv_back_zero(pool):
    for c in range(3):
        for t in range(3):
            for i in range(IMAGES + 1):
                pool[shifted_at(c, t, i * STRIDE, 16), :] = jnp.zeros((16, 128), F32)


CONV_ROWS = 16


def conv_back(k, t, first, last, dbn, conv, moments, sums, at, gains, shifts, nrm, pool, kernels, dn, dker, inverse_total):
    mask = cell_mask(IR)
    cells = cell_mask(CB)
    lanes = slice(t * 128, t * 128 + 128)
    inv = moments[3 + k : 4 + k, lanes]

    def spread(i, carry):
        rows = rows_at(i * IR, IR)
        standard = (conv[k, rows, lanes] - moments[k : k + 1, lanes]) * inv
        shift = (sums[at + t : at + t + 1] + standard * sums[at + 3 + t : at + 4 + t]) * inverse_total
        grad = dbn[rows_at(k * R + i * IR, IR), lanes]
        grad = (gains[1 + k : 2 + k, lanes] * inv) * (grad - mask * shift)
        pool[shifted_at(0, t, i * STRIDE + 16, IR), :] = pltpu.roll(grad, 1, 0)
        pool[shifted_at(1, t, i * STRIDE + 16, IR), :] = grad
        pool[shifted_at(2, t, i * STRIDE + 16, IR), :] = pltpu.roll(grad, IR - 1, 0)
        return carry

    lax.fori_loop(0, IMAGES, spread, 0)
    taps = [kernels[o, k : k + 1, lanes] for o in range(9)]

    def step(b, found):
        base = b * STRIDE + 16
        here = nrm[1, rows_at(base, CB), lanes]
        acc = jnp.zeros((CB, 128), F32)
        new = []
        for o in range(9):
            x = pool[shifted_at(2 - o % 3, t, base - (o // 3 - 1) * 16, CB), :]
            acc = acc + x * taps[o]
            new.append(found[o] + jnp.sum((x * here).reshape(CB // 8, 8, 128), 0))
        rows = rows_at(b * CB, CB)
        if not first:
            acc = acc + dn[rows, lanes]
        dn[rows, lanes] = acc
        if last:
            new.append(found[9] + jnp.sum((acc * here).reshape(CB // 8, 8, 128), 0))
            new.append(found[10] + jnp.sum((acc * cells).reshape(CB // 8, 8, 128), 0))
        return tuple(new)

    found = lax.fori_loop(0, IMAGES, step, (jnp.zeros((8, 128), F32),) * (11 if last else 9))
    found = [col_sum(f) for f in found]
    if last:
        found[9] = (found[9] - found[10] * shifts[0:1, lanes]) / gains[0:1, lanes]
    found += [jnp.zeros((1, 128), F32)] * (CONV_ROWS - len(found))
    dker[k, :, lanes] = jnp.concatenate(found, 0)


def last_norm_back(tokp, dres, dn, gains, gtok):
    mask = cell_mask(IR)

    def step(i, carry):
        rows = rows_at(i * IR, IR)
        xhat, rstd = norm_parts(tokp[rows, :])
        scaled = dn[rows, :] * mask * gains[0:1]
        one = jnp.sum(scaled, -1, keepdims=True) * (1.0 / D)
        two = jnp.sum(scaled * xhat, -1, keepdims=True) * (1.0 / D)
        gtok[rows, :] = dres[rows, :] + rstd * (scaled - one - xhat * two)
        return carry

    lax.fori_loop(0, IMAGES, step, 0)
    gtok[GAP0:R, :] = dres[GAP0:R, :]


class GradSum:
    def __init__(self, place, grads, bufs, sems, both):
        self.place, self.grads, self.both = place, grads, both
        self.rx_core, self.rx_one, self.mid, self.rx_z, self.fin, self.done = bufs
        self.own = grads.at[place.mp]
        self.slot = place.mp if both else 0
        self.rows = grads.shape[1]
        self.quarter = self.rows // QUAD
        self.part = z_part(self.rows, place.groups)
        self.block = min(self.quarter, 128)
        self.sems = sems
        self.stage = 0
        self.pending = []
        self.steps = [[self.core_start], [self.core_end, self.quad_start], [self.quad_end, self.z_start]]
        self.steps += [[self.z_end, self.z_back_start], [self.z_back_end, self.quad_back_start]]
        self.steps += [[self.end, self.core_back_start], [self.end]] if both else [[self.end]]

    def step(self):
        for part in self.steps.pop(0):
            part()

    def copies(self, ref, triples):
        self.stage += 1
        for src, dst, peer in triples:
            remote(src, dst, self.sems.at[0], self.sems.at[self.stage], peer)
        self.pending = [Pending(ref, self.sems.at[0], self.sems.at[self.stage])]

    def end(self):
        finish(self.pending)
        self.pending = []

    def add(self, dst, dst_at, mine, mine_at, theirs, rows, lanes):
        def step(b, carry):
            at = b * self.block
            total = mine[rows_at(mine_at + at, self.block), lanes].astype(F32)
            for ref in theirs:
                total = total + ref[rows_at(at, self.block), lanes].astype(F32)
            dst[rows_at(dst_at + at, self.block), lanes] = total.astype(BF)
            return carry

        lax.fori_loop(0, rows // self.block, step, 0)

    def core_start(self):
        self.copies(self.rx_core, [(self.grads.at[1 - self.place.mp], self.rx_core, self.place.other_core())])

    def core_end(self):
        self.end()
        self.add(self.own, 0, self.own, 0, [self.rx_core], self.rows, slice(None))

    def fill(self):
        if self.part * self.place.groups > self.quarter:
            self.mid[self.quarter :, :] = jnp.zeros((self.part * self.place.groups - self.quarter, D), BF)

    def quad_start(self):
        triples = []
        for o in range(1, QUAD):
            there = rows_at(lax.rem(self.place.quad + o, QUAD) * self.quarter, self.quarter)
            triples.append((self.own.at[there], self.rx_one.at[o - 1], self.place.in_quad(o)))
        self.copies(self.rx_one, triples)

    def quad_end(self):
        self.end()
        theirs = [self.rx_one.at[o] for o in range(QUAD - 1)]
        self.add(self.mid, 0, self.own, self.place.quad * self.quarter, theirs, self.quarter, slice(None))
        self.fill()

    def z_start(self):
        triples = []
        for o in range(1, self.place.groups):
            there = rows_at(lax.rem(self.place.z + o, self.place.groups) * self.part, self.part)
            triples.append((self.mid.at[there], self.rx_z.at[o - 1], self.place.along(o)))
        self.copies(self.rx_z, triples)

    def z_end(self):
        self.end()
        here = rows_at(self.place.z * self.part, self.part)
        total = self.mid[here, :].astype(F32)
        for o in range(self.place.groups - 1):
            total = total + self.rx_z[o].astype(F32)
        self.fin[here, :] = total.astype(BF)

    def z_back_start(self):
        here = self.fin.at[rows_at(self.place.z * self.part, self.part)]
        self.copies(self.rx_z, [(here, here, self.place.along(o)) for o in range(1, self.place.groups)])

    def z_back_end(self):
        self.end()
        here = rows_at(self.place.quad * self.quarter, self.quarter)
        self.done[self.slot, here, :] = self.fin[0 : self.quarter, :]

    def quad_back_start(self):
        here = self.done.at[self.slot, rows_at(self.place.quad * self.quarter, self.quarter)]
        self.copies(self.rx_one, [(here, here, self.place.in_quad(o)) for o in range(1, QUAD)])

    def core_back_start(self):
        here = self.done.at[self.place.mp]
        self.copies(self.rx_core, [(here, here, self.place.other_core())])


def z_part(rows, groups):
    return -(-rows // QUAD // (16 * groups)) * 16


UNITS = ((2 * PW, False), (2 * PW, False), (2 * PW, False), (D, True), (D, True))


def unit_buffers(groups, rows, both):
    span = z_part(rows, groups) * groups
    dims = [(rows, D), (QUAD - 1, rows // QUAD, D), (span, D)]
    dims += [(groups - 1, span // groups, D), (span, D), (2 if both else 1, rows, D)]
    return [pltpu.VMEM((2, rows, D), BF)] + [pltpu.VMEM(d, BF) for d in dims]


def main_kernel(
    groups, seg, tokens, cot, gains, shifts, kernels, wqkv, wout, win, wmo, bias_h,
    out_hbm, gtok_hbm, dw0, dw1, dw2, dw3, dw4, rest_out,
    pool, tokp, cotp, conv, nrm, dbn, outp, dres, bn, qkv, att, n2, gm, gr, act, dpre, datt, dqkv,
    wqkv_b, wout_b, win_f, wmo_f, bias_f, stats, moments, sums, sums_v, small, dbias, dker,
    mx1, mx2, sx1, sx2, lx1, lx2, vx1, vx2, kx1, kx2, kx3, kx4,
    in_sems, w_sems, pair_s, pair_r, sems, unit_sems, out_sems, dw_sems, *unit_flat,
):
    dws = (dw0, dw1, dw2, dw3, dw4)
    unit_refs = [unit_flat[n * 7 : n * 7 + 7] for n in range(len(UNITS))]
    place = Place(groups)
    place.greet()

    def load(n, src):
        copies = []
        for t in range(3):
            copy = pltpu.make_async_copy(
                src.at[0, :, pl.ds(t * 128, 128)], pool.at[pl.ds((n * 3 + t) * SCR, CELLS)], in_sems.at[n, t]
            )
            copy.start()
            copies.append(copy)
        return copies

    finish(load(0, tokens))
    loads = load(1, cot)
    blocks = [(wqkv.at[:, pl.ds(k * D, D)], dbn.at[pl.ds(k * D, D)]) for k in range(3)]
    blocks.append((wout, dbn.at[pl.ds(3 * D, D)]))
    for j in range(PARTS):
        blocks.append((win.at[:, pl.ds(j * PW, PW)], dbn.at[pl.ds((4 + j) * D, D), pl.ds(0, PW)]))
    blocks.append((wmo, dres.at[pl.ds(0, HH)]))
    weights = []
    for n, (src, dst) in enumerate(blocks):
        copy = pltpu.make_async_copy(src, dst, w_sems.at[n])
        copy.start()
        weights.append(copy)
    ahead = empty_before(seg)
    to_images(pool, 0, tokp, ahead)
    first_norm(tokp, gains, shifts, nrm)
    conv_forward(nrm, kernels, conv, stats)
    place.greeted()

    cells = IMAGES * IMG * IMG
    copies = send_eight(place, stats, mx1, sems.at[0, 0], sems.at[0, 1])
    mx1[place.slot] = stats[...]
    finish(weights)
    for k in range(3):
        wqkv_b[k] = dbn[k * D : k * D + D, :].astype(BF)
    wout_b[...] = dbn[3 * D : 4 * D, :].astype(BF)
    for j in range(PARTS):
        win_f[j, place.mp] = dbn[(4 + j) * D : (5 + j) * D, 0:PW].astype(BF)
        wmo_f[j, place.mp] = dres[j * PW : j * PW + PW, :].astype(BF)
    bias_f[place.mp] = jnp.broadcast_to(bias_h[...].reshape(1, HH), (8, HH))
    pairs = [
        remote(ref, ref, pair_s.at[n], pair_r.at[n], place.other_core())
        for n, ref in enumerate((win_f.at[:, place.mp], wmo_f.at[:, place.mp], bias_f.at[place.mp]))
    ]
    finish(loads)
    to_images(pool, 3 * SCR, cotp, ahead)
    finish(copies)
    mean, m2 = merge_moments(mx1, 8, cells)
    mx2[place.z, 0:3] = mean
    mx2[place.z, 3:6] = m2
    mx2[place.z, 6:8] = jnp.zeros((2, D), F32)
    finish(send_along(place, mx2.at[place.z], mx2, sems.at[0, 0], sems.at[0, 2]))
    mean, m2 = merge_moments(mx2, groups, 8 * cells)
    moments[0:3] = mean
    moments[3:6] = lax.rsqrt(m2 * (1.0 / (cells * 8 * groups)) + EPS)
    moments[6:8] = jnp.zeros((2, D), F32)

    project(conv, moments, gains, shifts, wqkv_b, bn, qkv)
    attend(qkv, pool, att)
    attend_gap(qkv, att)
    feed_forward_in(tokp, cotp, att, wout_b, gains, shifts, dres, n2, gm, small)
    finish(pairs)

    units = []
    for n, (rows, both) in enumerate(UNITS):
        units.append(GradSum(place, unit_refs[n][0], unit_refs[n][1:], unit_sems.at[n], both))
    ua, ub, ue, uc, ud = units
    grads = [refs[0] for refs in unit_refs]
    acc = dbn.at[pl.ds(0, R)]
    mine, theirs = place.mp, 1 - place.mp
    stores = []

    def keep(at, ref=None):
        def done(total):
            rest_out[at : at + total.shape[0], 0 : total.shape[1]] = total
            if ref is not None:
                ref[...] = total

        return done

    def keep_small(total):
        rest_out[80:88] = total
        tiles = [total[4 + c // 3 : 5 + c // 3, c % 3 * 128 : c % 3 * 128 + 128] for c in range(BIAS_TILES)]
        for c in range(BIAS_TILES // 2):
            at = c // 2 * 4 + c % 2
            kept = jnp.where(place.mp == 0, tiles[at], tiles[at + 2])
            rest_out[72 + c // 2 : 73 + c // 2, c % 2 * 128 : c % 2 * 128 + 128] = kept

    small_sum = SmallSum(place, small, lx1, lx2, sems, 2, keep_small)
    sum_v = SmallSum(place, sums_v, vx1, vx2, sems, 6, keep(64, sums_v))
    sum_qk = SmallSum(place, sums, sx1, sx2, sems, 1, keep(0, sums))
    ker_sums = [
        PairedSum(place, dker.at[k], *(x.at[k] for x in (kx1, kx2, kx3, kx4)), sems, 3 + k, keep(16 + 16 * k))
        for k in range(3)
    ]

    def forward(part):
        hidden_part(part, n2, gm, win_f, wmo_f, bias_f, act, dpre, outp, acc, dbias)

    def hidden(half, part):
        hidden_grads(half, n2, gm, act, dpre, grads[part])
        if half is theirs:
            units[part].step()

    def values():
        attend_back_values(pool, datt, dqkv)

    def after_forward():
        feed_forward_out(cotp, wout_b, gains, shifts, outp, acc, dres, gr, datt, small)
        for c in range(BIAS_TILES):
            tile = slice(c % 4 * 128, c % 4 * 128 + 128)
            small[4 + c // 3 : 5 + c // 3, c % 3 * 128 : c % 3 * 128 + 128] = dbias[c // 4, 0:1, tile]
        small_sum.start()
        attend_back_gap(datt, dqkv)
        stores.append(pltpu.make_async_copy(outp, out_hbm, out_sems.at[0]))
        stores[0].start()

    def out_grad():
        for p in range(3):
            grads[3][1, p * 128 : p * 128 + 128, :] = t_dot(att[p], gr[...]).astype(BF)

    def value_grads():
        project_grads(2, bn, dqkv, grads[3].at[0])
        uc.step()

    def query_grads():
        for k in range(2):
            project_grads(k, bn, dqkv, grads[4].at[k])
        ud.step()

    def value_back():
        project_back(2, conv, moments, wqkv_b, dqkv, dbn, sums_v, 0)
        sum_v.start()

    def query_back(k):
        project_back(k, conv, moments, wqkv_b, dqkv, dbn, sums, 6 * k)
        if k == 1:
            sum_qk.start()

    def back(k, t):
        held, at = (sums_v, 0) if k == 2 else (sums, 6 * k)
        conv_back(
            k, t, k == 0, k == 2, dbn, conv, moments, held, at, gains, shifts, nrm, pool, kernels, cotp, dker,
            1.0 / (cells * 8 * groups),
        )
        if t == 2:
            ker_sums[k].start()

    def last_norm():
        stores[0].wait()
        last_norm_back(tokp, dres, cotp, gains, outp)
        stores.append(pltpu.make_async_copy(outp, gtok_hbm, out_sems.at[1]))
        stores[-1].start()

    def unit(n):
        units[n].step()
        if not units[n].steps:
            stores.append(pltpu.make_async_copy(units[n].done, dws[n], dw_sems.at[n]))
            stores[-1].start()

    forward(0)
    hidden(theirs, 0)
    hidden(mine, 0)
    forward(1)
    unit(0)
    hidden(theirs, 1)
    hidden(mine, 1)
    forward(2)
    unit(1)
    hidden(theirs, 2)
    hidden(mine, 2)
    after_forward()
    unit(0)
    unit(2)
    attend_back(0, 2, qkv, pool, datt, dqkv)
    attend_back(2, 4, qkv, pool, datt, dqkv)
    unit(0)
    small_sum.step()
    unit(1)
    query_back(0)
    query_back(1)
    values()
    unit(0)
    unit(2)
    out_grad()
    value_grads()
    sum_qk.step()
    small_sum.step()
    unit(1)
    unit(3)
    query_grads()
    unit(2)
    value_back()
    unit(0)
    unit(4)
    sum_qk.step()
    unit(1)
    conv_back_zero(pool)
    back(0, 0)
    back(0, 1)
    unit(3)
    unit(2)
    back(0, 2)
    sum_v.step()
    back(1, 0)
    ker_sums[0].step()
    back(1, 1)
    unit(4)
    back(1, 2)
    unit(3)
    ker_sums[1].step()
    sum_v.step()
    back(2, 0)
    back(2, 1)
    unit(1)
    unit(4)
    back(2, 2)
    last_norm()
    ker_sums[2].step()
    unit(3)
    unit(2)
    ker_sums[0].step()
    ker_sums[1].step()
    unit(4)
    ker_sums[2].step()
    unit(3)
    ker_sums[0].step()
    ker_sums[1].step()
    unit(3)
    ker_sums[2].step()
    unit(4)
    ker_sums[1].step()
    ker_sums[2].step()
    ker_sums[0].step()
    unit(4)
    finish(stores[1:])


def main_call(groups, *args):
    units = [buf for unit in UNITS for buf in unit_buffers(groups, *unit)]
    return pl.pallas_call(
        functools.partial(main_kernel, groups),
        out_shape=(shape(R, D), shape(R, D))
        + tuple(shape(2 if both else 1, rows, D, dtype=BF) for rows, both in UNITS)
        + (shape(88, D),),
        in_specs=[VM, ANY, ANY, VM, VM, VM, ANY, ANY, ANY, ANY, VM],
        out_specs=(ANY,) * 7 + (VM,),
        scratch_shapes=[
            pltpu.VMEM((POOL, 128), F32),
            pltpu.VMEM((R, D), F32), pltpu.VMEM((R, D), F32), pltpu.VMEM((3, R, D), F32),
            pltpu.VMEM((3, CONVR, D), F32), pltpu.VMEM((3 * R, D), F32),
            pltpu.VMEM((R, D), F32), pltpu.VMEM((R, D), F32),
            pltpu.VMEM((3, R, D), BF), pltpu.VMEM((3, 3, R, 128), BF), pltpu.VMEM((3, R, 128), BF),
            pltpu.VMEM((R, D), BF), pltpu.VMEM((R, D), BF), pltpu.VMEM((R, D), BF),
            pltpu.VMEM((R, 512), BF), pltpu.VMEM((R, 512), BF), pltpu.VMEM((3, R, 128), BF), pltpu.VMEM((3, 3, R, 128), BF),
            pltpu.VMEM((3, D, D), BF), pltpu.VMEM((D, D), BF), pltpu.VMEM((PARTS, 2, D, PW), BF), pltpu.VMEM((PARTS, 2, PW, D), BF),
            pltpu.VMEM((2, 8, HH), F32),
            pltpu.VMEM((8, D), F32), pltpu.VMEM((8, D), F32), pltpu.VMEM((16, 128), F32), pltpu.VMEM((8, 128), F32),
            pltpu.VMEM((8, D), F32), pltpu.VMEM((PARTS, 8, 2 * PW), F32), pltpu.VMEM((3, CONV_ROWS, D), F32),
            pltpu.VMEM((8, 8, D), F32), pltpu.VMEM((groups, 8, D), F32),
            pltpu.VMEM((8, 16, 128), F32), pltpu.VMEM((groups, 16, 128), F32),
            pltpu.VMEM((8, 8, D), F32), pltpu.VMEM((groups, 8, D), F32),
            pltpu.VMEM((8, 8, 128), F32), pltpu.VMEM((groups, 8, 128), F32),
            pltpu.VMEM((3, 8, D), F32), pltpu.VMEM((3, QUAD, 8, D), F32), pltpu.VMEM((3, groups, 8, D), F32),
            pltpu.VMEM((3, CONV_ROWS, D), F32),
            dma(2, 3), dma(8), dma(3), dma(3), dma(7, 5), dma(5, 7), dma(2), dma(5),
        ] + units,
        compiler_params=params(collective_id=0, has_side_effects=True),
    )(*args)


def last_kernel(
    seg, outp, gtok, dwa, dwb, dwe, dwc, dwd, rest,
    output, grad_tokens, grad_gains, grad_shifts, grad_kernels, grad_qkv, grad_out, grad_in, grad_bias, grad_down,
    held, lowa, lowb, lowe, lowc, lowd, scr, wide, turned, in_sems, out_sems,
):
    loads = []
    pairs = ((outp, held.at[0]), (gtok, held.at[1]))
    pairs += ((dwa, lowa), (dwb, lowb), (dwe, lowe), (dwc, lowc), (dwd, lowd))
    for n, (src, dst) in enumerate(pairs):
        copy = pltpu.make_async_copy(src, dst, in_sems.at[n])
        copy.start()
        loads.append(copy)
    starts, gaps = find_columns(seg)
    stores = []

    def store(src, dst):
        copy = pltpu.make_async_copy(src, dst, out_sems.at[len(stores)])
        copy.start()
        stores.append(copy)

    for n, dst in enumerate((output, grad_tokens)):
        loads[n].wait()
        to_canvas(held.at[n], scr.at[n], starts, gaps)
        for t in range(3):
            store(scr.at[n, t, pl.ds(0, CELLS)], dst.at[0, :, pl.ds(t * 128, 128)])
    for n, low in enumerate((lowa, lowb, lowe)):
        loads[2 + n].wait()
        start, size = n * PW, PW
        turned[:, start : start + size] = low[0, 0:size, :].astype(F32).T
        wide[start : start + size, :] = low[0, size : 2 * size, :].astype(F32)
        store(turned.at[:, pl.ds(start, size)], grad_in.at[:, pl.ds(start, size)])
        store(wide.at[pl.ds(start, size)], grad_down.at[pl.ds(start, size)])
    for n, low in enumerate((lowc, lowd)):
        loads[5 + n].wait()
        for j in range(2):
            at = HH + (n * 2 + j) * D
            wide[at : at + D, :] = low[j].astype(F32)
            here = wide.at[pl.ds(at, D)]
            if n == 0 and j == 1:
                store(here, grad_out)
            else:
                store(here, grad_qkv.at[:, pl.ds((2 if n == 0 else j) * D, D)])
    for k in range(3):
        for o in range(9):
            row = 16 + k * CONV_ROWS + o
            grad_kernels[o, k : k + 1] = rest[row : row + 1]
    grad_gains[0:1] = rest[57:58]
    grad_gains[4:5] = rest[80:81]
    grad_shifts[0:1] = rest[58:59]
    grad_shifts[3:6] = rest[81:84]
    for t in range(3):
        lanes = slice(t * 128, t * 128 + 128)
        for k, at in enumerate((0, 6, 64)):
            grad_gains[1 + k : 2 + k, lanes] = rest[at + 3 + t : at + 4 + t, 0:128]
            if k != 1:
                grad_shifts[1 + k // 2 : 2 + k // 2, lanes] = rest[at + t : at + t + 1, 0:128]
    for j in range(PARTS):
        grad_bias[j * PW : j * PW + PW] = rest[72 + j, 0:PW]
    finish(stores)


def last_call(*args):
    return pl.pallas_call(
        last_kernel,
        out_shape=(
            shape(1, CELLS, D), shape(1, CELLS, D), shape(5, D), shape(6, D), shape(9, 3, D), shape(D, 3 * D),
            shape(D, D), shape(D, HH), shape(HH), shape(HH, D),
        ),
        in_specs=[SM] + [ANY] * 7 + [VM],
        out_specs=(ANY, ANY, VM, VM, VM, ANY, ANY, ANY, VM, ANY),
        scratch_shapes=[
            pltpu.VMEM((2, R, D), F32),
            *(pltpu.VMEM((2 if both else 1, rows, D), BF) for rows, both in UNITS),
            pltpu.VMEM((2, 3, CELLS + 16, 128), F32), pltpu.VMEM((HH + 4 * D, D), F32),
            pltpu.VMEM((D, HH), F32), dma(7), dma(16),
        ],
        compiler_params=params(),
    )(*args)


def local(
    groups, tokens, segment_ids, gains, shifts, kernels, qkv_weight, out_weight,
    mlp_in_weight, mlp_in_bias, mlp_out_weight, cotangent,
):
    found = main_call(
        groups, segment_ids, tokens, cotangent, gains, shifts, kernels.transpose(1, 0, 2),
        qkv_weight, out_weight, mlp_in_weight, mlp_out_weight, mlp_in_bias,
    )
    outs = list(last_call(segment_ids, *found))
    outs[4] = outs[4].transpose(1, 0, 2)
    return tuple(outs)


def solution(mesh):
    groups = mesh.shape["dp"] // QUAD
    both = P(("dp", "mp"), None, None)
    return jax.shard_map(
        functools.partial(local, groups),
        mesh=mesh,
        in_specs=(
            both, P(("dp", "mp"), None), P(), P(), P(), P(), P(), P(None, "mp"), P("mp"), P("mp", None), both,
        ),
        out_specs=(both, both, P(), P(), P(), P(), P(), P(None, "mp"), P("mp"), P("mp", None)),
        check_vma=False,
    )
```

```python
import functools
import math

import jax
import jax.numpy as jnp
from jax import lax
from jax.experimental import pallas as pl
from jax.experimental.pallas import tpu as pltpu
from jax.sharding import PartitionSpec as P

F32 = jnp.float32
BF = jnp.bfloat16
MESH = pl.DeviceIdType.MESH
D = 384
IMG = 14
IMAGES = 4
CW = 64
CELLS = IMG * CW
IR = 224
GAP0 = IMAGES * IR
GAPS = 112
R = 1024
DCH = 1024
STRIDE = IR + 16
CONVR = IMAGES * STRIDE + 16
EPS = 1e-05
MASKED = -1e30
QUAD = 4
HH = 2 * D
VLIM = 62 * 2**20
SCALE = 0.125
PCH = 512


def params(**kw):
    return pltpu.CompilerParams(vmem_limit_bytes=VLIM, **kw)


VM = pl.BlockSpec(memory_space=pltpu.VMEM)
SM = pl.BlockSpec(memory_space=pltpu.SMEM)
ANY = pl.BlockSpec(memory_space=pl.ANY)


def shape(*dims, dtype=F32):
    return jax.ShapeDtypeStruct(dims, dtype)


def dot(a, b):
    return jnp.dot(a, b, preferred_element_type=F32)


def dot_t(a, b):
    return lax.dot_general(a, b, (((1,), (1,)), ((), ())), preferred_element_type=F32)


def t_dot(a, b):
    return lax.dot_general(a, b, (((0,), (0,)), ((), ())), preferred_element_type=F32)


def cell_mask(rows):
    row = lax.broadcasted_iota(jnp.int32, (rows, 1), 0)
    return (row % 16 < IMG).astype(F32)


def rows_at(start, size, align=16):
    return pl.ds(pl.multiple_of(start, align), size)


def find_columns(seg):
    def step(col, found):
        count, starts, gaps = found
        here = seg[0, col]
        starts = tuple(jnp.minimum(s, jnp.where(here == i + 1, col, CW)) for i, s in enumerate(starts))
        empty = here == 0
        gaps = tuple(jnp.where(empty & (count == k), col, g) for k, g in enumerate(gaps))
        return count + jnp.where(empty, 1, 0), starts, gaps

    start = (jnp.int32(0), (jnp.int32(CW),) * IMAGES, (jnp.int32(0),) * 8)
    _, starts, gaps = lax.fori_loop(0, CW, step, start)
    return starts, gaps


SCR = CELLS + 16
POOL = 48 * IR


def empty_before(seg):
    lane = lax.broadcasted_iota(jnp.int32, (1, 128), 1)
    ids = seg[0:1, 0:128]
    firsts = [jnp.where((ids == i + 1) & (lane < CW), lane, CW).astype(F32) for i in range(IMAGES)]
    return [jnp.min(f, -1, keepdims=True) - float(i * IMG) for i, f in enumerate(firsts)]


def to_images(pool, base, out, ahead):
    col = lax.broadcasted_iota(jnp.int32, (16, 128), 0)
    sub = lax.broadcasted_iota(jnp.int32, (8, 128), 0).astype(F32)
    before = sum([jnp.where(a <= sub, 1.0, 0.0) for a in ahead])

    def step(r, carry):
        for t in range(3):
            row = base + t * SCR + r * CW
            for i in range(IMAGES):
                window = pool[pl.ds(row + i * IMG, 16), :]
                for e in range(1, 9):
                    moved = pool[pl.ds(row + i * IMG + e, 16), :]
                    window = jnp.where(ahead[i] == float(e), moved, window)
                out[rows_at(i * IR + r * 16, 16), t * 128 : t * 128 + 128] = jnp.where(col < IMG, window, 0.0)
            block = pool[rows_at(row, 8, 8), :]
            for n in range(1, IMAGES + 1):
                block = jnp.where(before == float(n), pool[pl.ds(row + n * IMG, 8), :], block)
            out[rows_at(GAP0 + r * 8, 8, 8), t * 128 : t * 128 + 128] = block
        return carry

    lax.fori_loop(0, IMG, step, 0)
    out[GAP0 + GAPS : R, :] = jnp.zeros((R - GAP0 - GAPS, D), F32)


def to_canvas(src, scr, starts, gaps):
    def step(r, carry):
        for t in range(3):
            for i in range(IMAGES):
                block = src[rows_at(i * IR + r * 16, 16), t * 128 : t * 128 + 128]
                scr[t, pl.ds(r * CW + starts[i], 16), :] = block
            block = src[rows_at(GAP0 + r * 8, 8, 8), t * 128 : t * 128 + 128]
            for k in range(8):
                scr[t, pl.ds(r * CW + gaps[k], 1), :] = block[k : k + 1]
        return carry

    lax.fori_loop(0, IMG, step, 0)


def norm_parts(x):
    mean = jnp.sum(x, -1, keepdims=True) * (1.0 / D)
    centred = x - mean
    var = jnp.sum(centred * centred, -1, keepdims=True) * (1.0 / D)
    rstd = lax.rsqrt(var + EPS)
    return centred * rstd, rstd


def store_shifted(dst, i, t, x):
    lanes = slice(t * 128, t * 128 + 128)
    at = rows_at(i * STRIDE + 16, IR)
    dst[0, at, lanes] = pltpu.roll(x, 1, 0)
    dst[1, at, lanes] = x
    dst[2, at, lanes] = pltpu.roll(x, IR - 1, 0)


def zero_borders(dst):
    for i in range(IMAGES + 1):
        for c in range(3):
            dst[c, i * STRIDE : i * STRIDE + 16, :] = jnp.zeros((16, D), F32)


def first_norm(tokp, gains, shifts, nrm):
    zero_borders(nrm)
    mask = cell_mask(IR)

    def step(i, carry):
        xhat, _ = norm_parts(tokp[rows_at(i * IR, IR), :])
        normed = (xhat * gains[0:1] + shifts[0:1]) * mask
        for t in range(3):
            store_shifted(nrm, i, t, normed[:, t * 128 : t * 128 + 128])
        return carry

    lax.fori_loop(0, IMAGES, step, 0)


CB = 224


def conv_forward(nrm, kernels, conv, stats):
    mask = cell_mask(IR)
    count = float(IMG * IMG)
    for t in range(3):
        lanes = slice(t * 128, t * 128 + 128)
        taps = [[kernels[o, k : k + 1, lanes] for o in range(9)] for k in range(3)]

        def convolve(b):
            base = b * STRIDE + 16
            acc = [jnp.zeros((IR, 128), F32)] * 3
            for o in range(9):
                x = nrm[o % 3, rows_at(base + (o // 3 - 1) * 16, IR), lanes]
                for k in range(3):
                    acc[k] = acc[k] + x * taps[k][o]
            for k in range(3):
                conv[k, rows_at(b * IR, IR), lanes] = acc[k]
            return acc

        def spread(acc, centres, sums):
            new = []
            for k in range(3):
                away = (acc[k] - centres[k]) * mask
                new.append(sums[2 * k] + jnp.sum(away.reshape(IR // 8, 8, 128), 0))
                new.append(sums[2 * k + 1] + jnp.sum((away * away).reshape(IR // 8, 8, 128), 0))
            return tuple(new)

        acc = convolve(0)
        centres = [jnp.sum(a * mask, 0, keepdims=True) * (1.0 / count) for a in acc]
        sums = spread(acc, centres, (jnp.zeros((8, 128), F32),) * 6)
        sums = lax.fori_loop(1, IMAGES, lambda b, found: spread(convolve(b), centres, found), sums)
        sums = [jnp.sum(x, 0, keepdims=True) for x in sums]
        for k in range(3):
            one, two = sums[2 * k] * (1.0 / (IMAGES * count)), sums[2 * k + 1]
            stats[k : k + 1, lanes] = centres[k] + one
            stats[3 + k : 4 + k, lanes] = two - one * one * (IMAGES * count)
        stats[6:8, lanes] = jnp.zeros((2, 128), F32)
    for k in range(3):
        conv[k, GAP0:R, :] = jnp.zeros((R - GAP0, D), F32)


class Place:
    def __init__(self, groups):
        dp = lax.axis_index("dp")
        self.mp = lax.axis_index("mp")
        self.groups = groups
        self.quad = lax.rem(dp, QUAD)
        self.z = dp // QUAD
        self.slot = self.quad * 2 + self.mp

    def in_eight(self, offset):
        other = lax.rem(self.slot + offset, 8)
        return (self.z * QUAD + other // 2, lax.rem(other, 2))

    def in_quad(self, offset):
        return (self.z * QUAD + lax.rem(self.quad + offset, QUAD), self.mp)

    def along(self, offset):
        return (lax.rem(self.z + offset, self.groups) * QUAD + self.quad, self.mp)

    def other_core(self):
        return (self.z * QUAD + self.quad, 1 - self.mp)

    def peers(self):
        return [self.in_eight(o) for o in range(1, 8)] + [self.along(o) for o in range(1, self.groups)]

    def greet(self):
        barrier = pltpu.get_barrier_semaphore()
        for peer in self.peers():
            pl.semaphore_signal(barrier, inc=1, device_id=peer, device_id_type=MESH)

    def greeted(self):
        pl.semaphore_wait(pltpu.get_barrier_semaphore(), 7 + self.groups - 1)


def remote(src, dst, send, recv, peer):
    copy = pltpu.make_async_remote_copy(
        src_ref=src, dst_ref=dst, send_sem=send, recv_sem=recv, device_id=peer, device_id_type=MESH
    )
    copy.start()
    return copy


def send_eight(place, src, rx, send, recv):
    for o in range(1, 8):
        remote(src, rx.at[place.slot], send, recv, place.in_eight(o))
    return Pending(rx.at[pl.ds(0, 7)], send, recv)


def send_along(place, src, rx, send, recv):
    for o in range(1, place.groups):
        remote(src, rx.at[place.z], send, recv, place.along(o))
    return Pending(rx.at[pl.ds(0, place.groups - 1)], send, recv)


class Pending:
    def __init__(self, ref, send, recv):
        self.ref, self.sems = ref, (send, recv)

    def wait(self):
        for sem in self.sems:
            pltpu.make_async_copy(self.ref, self.ref, sem).wait()


def finish(copies):
    for copy in copies if isinstance(copies, list) else [copies]:
        copy.wait()


def sum_slots(rx, count):
    total = rx[0].astype(F32)
    for s in range(1, count):
        total = total + rx[s].astype(F32)
    return total


class SmallSum:
    def __init__(self, place, src, rx1, rx2, sems, n, done):
        self.place, self.src, self.rx1, self.rx2, self.done = place, src, rx1, rx2, done
        self.sems = [sems.at[n, i] for i in range(3)]
        self.steps = [self.middle, self.end]

    def start(self):
        self.copies = send_eight(self.place, self.src, self.rx1, self.sems[0], self.sems[1])
        self.rx1[self.place.slot] = self.src[...]

    def step(self):
        self.steps.pop(0)()

    def middle(self):
        finish(self.copies)
        self.rx2[self.place.z] = sum_slots(self.rx1, 8).astype(self.rx2.dtype)
        self.copies = send_along(self.place, self.rx2.at[self.place.z], self.rx2, self.sems[0], self.sems[2])

    def end(self):
        finish(self.copies)
        self.done(sum_slots(self.rx2, self.place.groups))


class PairedSum:
    def __init__(self, place, src, rx_core, rx_quad, rx_z, both, sems, n, done):
        self.place, self.src, self.both, self.done = place, src, both, done
        self.rx_core, self.rx_quad, self.rx_z = rx_core, rx_quad, rx_z
        self.sems = [sems.at[n, i] for i in range(5)]
        self.steps = [self.quad, self.along, self.core_back, self.end]

    def exchange(self, stage, ref, src, dst, peers):
        for peer in peers:
            remote(src, dst, self.sems[0], self.sems[stage], peer)
        self.copies = Pending(ref, self.sems[0], self.sems[stage])

    def half(self, mp):
        return rows_at(mp * 8, 8, 8)

    def start(self):
        there = self.src.at[self.half(1 - self.place.mp)]
        self.exchange(1, self.rx_core, there, self.rx_core, [self.place.other_core()])

    def step(self):
        finish(self.copies)
        self.steps.pop(0)()

    def quad(self):
        slot = self.place.quad
        self.rx_quad[slot] = self.src[self.half(self.place.mp), :] + self.rx_core[...]
        here = self.rx_quad.at[slot]
        peers = [self.place.in_quad(o) for o in range(1, QUAD)]
        self.exchange(2, self.rx_quad.at[pl.ds(0, QUAD - 1)], here, here, peers)

    def along(self):
        self.rx_z[self.place.z] = sum_slots(self.rx_quad, QUAD)
        here = self.rx_z.at[self.place.z]
        peers = [self.place.along(o) for o in range(1, self.place.groups)]
        self.exchange(3, self.rx_z.at[pl.ds(0, self.place.groups - 1)], here, here, peers)

    def core_back(self):
        self.both[self.half(self.place.mp), :] = sum_slots(self.rx_z, self.place.groups)
        here = self.both.at[self.half(self.place.mp)]
        self.exchange(4, here, here, here, [self.place.other_core()])

    def end(self):
        self.done(self.both[...])


def merge_moments(rx, count, cells):
    mean = sum([rx[s, 0:3] for s in range(1, count)], rx[0, 0:3]) * (1.0 / count)
    m2 = sum([rx[s, 3:6] for s in range(1, count)], rx[0, 3:6])
    for s in range(count):
        away = rx[s, 0:3] - mean
        m2 = m2 + away * away * float(cells)
    return mean, m2


def dma(*n):
    return pltpu.SemaphoreType.DMA(n)


def project(conv, moments, gains, shifts, wqkv, bn, qkv):
    def step(c, carry):
        rows = rows_at(c * DCH, DCH)
        for k in range(3):
            standard = (conv[k, rows, :] - moments[k : k + 1]) * moments[3 + k : 4 + k]
            value = standard * gains[1 + k : 2 + k]
            if k != 1:
                value = value + (shifts[1:2] if k == 0 else shifts[2:3])
            value = value.astype(BF)
            bn[k, rows, :] = value
            out = dot(value, wqkv[k]).astype(BF)
            if k == 0:
                out = (out * SCALE).astype(BF)
            for p in range(3):
                qkv[k, p, rows, :] = out[:, p * 128 : p * 128 + 128]
        return carry

    lax.fori_loop(0, R // DCH, step, 0)


def key_bias():
    row = lax.broadcasted_iota(jnp.int32, (16, 256), 0)
    return jnp.where(row < IMG, 0.0, MASKED)


def query_mask():
    lane = lax.broadcasted_iota(jnp.int32, (1, 256), 1)
    return (lane < IR).astype(F32)


def by_head(x):
    lane = lax.broadcasted_iota(jnp.int32, x.shape, 1)
    zero = jnp.zeros_like(x)
    return jnp.concatenate([jnp.where(lane < 64, x, zero), jnp.where(lane < 64, zero, x)], 0)


def own_columns(x, rows):
    lane = lax.broadcasted_iota(jnp.int32, (IR, 128), 1)
    return jnp.where(lane < 64, x[:IR], x[rows : rows + IR])


def probs_at(pool, n):
    return [rows_at((2 * n + half) * IR, IR) for half in range(2)]


def attend(qkv, pool, att):
    bias = key_bias()[None]
    live = query_mask()

    def step(i, carry):
        rows = rows_at(i * IR, IR)
        for p in range(3):
            q = qkv[0, p, rows_at(i * IR, 256), :]
            both = dot_t(by_head(qkv[1, p, rows, :]), q)
            low = []
            for h in range(2):
                scores = (both[h * IR : h * IR + IR].reshape(IMG, 16, 256) + bias).reshape(IR, 256)
                largest = jnp.max(scores, 0, keepdims=True)
                expo = jnp.exp(scores - largest)
                soft = expo * (live / jnp.sum(expo, 0, keepdims=True))
                for half, at in enumerate(probs_at(pool, (i * 3 + p) * 2 + h)):
                    pool[at, :] = soft[:, half * 128 : half * 128 + 128]
                low.append(soft.astype(BF))
            out = t_dot(jnp.concatenate(low, 1), qkv[2, p, rows, :])
            att[p, rows, :] = own_columns(out, 256).astype(BF)
        return carry

    lax.fori_loop(0, IMAGES, step, 0, unroll=4)


def even_prob():
    return jnp.full((1, 1), 1.0 / GAPS, F32).astype(BF).astype(F32)


def attend_gap(qkv, att):
    for p in range(3):
        v = qkv[2, p, GAP0 : GAP0 + 16, :].astype(F32)
        out = (v * (even_prob() * float(GAPS))).astype(BF)
        for b in range((R - GAP0) // 16):
            att[p, GAP0 + b * 16 : GAP0 + b * 16 + 16, :] = out


def gelu_parts(x):
    cdf = 0.5 * (1.0 + lax.erf(x * (1.0 / math.sqrt(2.0))))
    density = jnp.exp(x * x * -0.5) * (1.0 / math.sqrt(2.0 * math.pi))
    return x * cdf, cdf + x * density


def col_sum(x):
    return jnp.sum(x, 0, keepdims=True)


def feed_forward_in(tokp, att, wout, gains, shifts, dres, n2):

    def step(c, carry):
        rows = rows_at(c * DCH, DCH)
        attended = jnp.concatenate([att[p, rows, :] for p in range(3)], 1)
        residual = tokp[rows, :] + (dot(attended, wout[...]) + shifts[3:4])
        dres[rows, :] = residual
        xhat, _ = norm_parts(residual)
        n2[rows, :] = (xhat * gains[4:5] + shifts[4:5]).astype(BF)
        return carry

    lax.fori_loop(0, R // DCH, step, 0)


def cotangent_parts(cotp, gm, small):
    small[...] = jnp.zeros((8, D), F32)

    def step(c, carry):
        rows = rows_at(c * DCH, DCH)
        cot = cotp[rows, :]
        gm[rows, :] = cot.astype(BF)
        small[3:4] = small[3:4] + col_sum(cot)
        return carry

    lax.fori_loop(0, R // DCH, step, 0)


HCH = 1024
PARTS = 3
PW = HH // PARTS
BIAS_TILES = 2 * HH // 128


def hidden_part(part, n2, gm, win, wmo, bias, act, dpre, outp, acc, dbias):
    both = slice(0, 2 * PW)
    dbias[part, 0:1, :] = jnp.zeros((1, 2 * PW), F32)

    def step(c, carry):
        rows = rows_at(c * HCH, HCH)
        up = jnp.concatenate([win[part, h] for h in range(2)], 1)
        down = wmo[part].reshape(2 * PW, D)
        shift = jnp.concatenate([bias[h, 0:1, part * PW : part * PW + PW] for h in range(2)], 1)
        value, slope = gelu_parts(dot(n2[rows, :], up) + shift)
        value = value.astype(BF)
        act[rows, both] = value
        grad = dot_t(gm[rows, :], down) * slope
        dbias[part, 0:1, both] = dbias[part, 0:1, both] + col_sum(grad)
        grad = grad.astype(BF)
        dpre[rows, both] = grad
        forward = dot(value, down)
        back = dot_t(grad, up)
        outp[rows, :] = forward if part == 0 else outp[rows, :] + forward
        acc[rows, :] = back if part == 0 else acc[rows, :] + back
        return carry

    lax.fori_loop(0, R // HCH, step, 0)


def hidden_grads(half, n2, gm, act, dpre, grads):
    units = pl.ds(pl.multiple_of(half * PW, 128), PW)
    grads[half, 0:PW, :] = t_dot(dpre[:, units], n2[...]).astype(BF)
    grads[half, PW : 2 * PW, :] = t_dot(act[:, units], gm[...]).astype(BF)


def feed_forward_out(cotp, wout, gains, shifts, outp, acc, dres, gr, datt, small):
    def step(c, carry):
        rows = rows_at(c * DCH, DCH)
        residual = dres[rows, :]
        outp[rows, :] = residual + outp[rows, :] + shifts[5:6]
        xhat, rstd = norm_parts(residual)
        grad = acc[rows, :]
        scaled = grad * gains[4:5]
        one = jnp.sum(scaled, -1, keepdims=True) * (1.0 / D)
        two = jnp.sum(scaled * xhat, -1, keepdims=True) * (1.0 / D)
        total = cotp[rows, :] + rstd * (scaled - one - xhat * two)
        dres[rows, :] = total
        low = total.astype(BF)
        gr[rows, :] = low
        back = dot_t(low, wout[...]).astype(BF)
        for p in range(3):
            datt[p, rows, :] = back[:, p * 128 : p * 128 + 128]
        small[0:1] = small[0:1] + col_sum(grad * xhat)
        small[1:2] = small[1:2] + col_sum(total)
        small[2:3] = small[2:3] + col_sum(grad)
        return carry

    lax.fori_loop(0, R // DCH, step, 0)


def attend_back_values(pool, datt, dqkv):
    def step(i, carry):
        rows = rows_at(i * IR, IR)
        for p in range(3):
            low = []
            for h in range(2):
                soft = [pool[at, :] for at in probs_at(pool, (i * 3 + p) * 2 + h)]
                low.append(jnp.concatenate(soft, 1).astype(BF))
            dv = dot(jnp.concatenate(low, 0), datt[p, rows_at(i * IR, 256), :])
            dqkv[2, p, rows, :] = own_columns(dv, IR).astype(BF)
        return carry

    lax.fori_loop(0, IMAGES, step, 0)


def attend_back(first, last, qkv, pool, datt, dqkv):
    def step(i, carry):
        rows = rows_at(i * IR, IR)
        wide = rows_at(i * IR, 256)
        for p in range(3):
            both = dot_t(by_head(qkv[2, p, rows, :]), datt[p, wide, :])
            ds = []
            for h in range(2):
                soft = jnp.concatenate([pool[at, :] for at in probs_at(pool, (i * 3 + p) * 2 + h)], 1)
                grad = both[h * IR : h * IR + IR]
                delta = jnp.sum(soft * grad, 0, keepdims=True)
                ds.append((soft * (grad - delta)).astype(BF))
            dk = dot(jnp.concatenate(ds, 0), qkv[0, p, wide, :])
            dq = t_dot(jnp.concatenate(ds, 1), qkv[1, p, rows, :])
            dqkv[0, p, rows, :] = (own_columns(dq, 256) * SCALE).astype(BF)
            dqkv[1, p, rows, :] = own_columns(dk, IR).astype(BF)
        return carry

    lax.fori_loop(first, last, step, 0, unroll=2)


def attend_back_gap(datt, dqkv):
    for p in range(3):
        total = col_sum(datt[p, GAP0 : GAP0 + GAPS, :].astype(F32))
        grad = jnp.broadcast_to((total * even_prob()).astype(BF), (16, 128))
        zero = jnp.zeros((16, 128), BF)
        for b in range((R - GAP0) // 16):
            rows = slice(GAP0 + b * 16, GAP0 + b * 16 + 16)
            dqkv[0, p, rows, :] = zero
            dqkv[1, p, rows, :] = zero
            dqkv[2, p, rows, :] = grad if b < GAPS // 16 else zero


def project_back(k, conv, moments, wqkv, dqkv, dbn, sums, at):
    def step(c, carry):
        rows = rows_at(c * PCH, PCH)
        grad = jnp.concatenate([dqkv[k, p, rows, :] for p in range(3)], 1)
        back = dot_t(grad, wqkv[k])
        dbn[rows_at(k * R + c * PCH, PCH), :] = back
        standard = (conv[k, rows, :] - moments[k : k + 1]) * moments[3 + k : 4 + k]
        return carry[0] + col_sum(back), carry[1] + col_sum(back * standard)

    found = lax.fori_loop(0, R // PCH, step, (jnp.zeros((1, D), F32),) * 2)
    for n in range(2):
        for t in range(3):
            row = at + n * 3 + t
            sums[row : row + 1] = found[n][:, t * 128 : t * 128 + 128]


def project_grads(k, bn, dqkv, grads):
    for p in range(3):
        grads[:, p * 128 : p * 128 + 128] = t_dot(bn[k], dqkv[k, p]).astype(BF)


def shifted_at(c, t, row, size):
    return rows_at((c * 3 + t) * CONVR + row, size)


def conv_back_zero(pool):
    for c in range(3):
        for t in range(3):
            for i in range(IMAGES + 1):
                pool[shifted_at(c, t, i * STRIDE, 16), :] = jnp.zeros((16, 128), F32)


CONV_ROWS = 16


def conv_back(k, t, first, last, dbn, conv, moments, sums, at, gains, shifts, nrm, pool, kernels, dn, dker, inverse_total):
    mask = cell_mask(IR)
    cells = cell_mask(CB)
    lanes = slice(t * 128, t * 128 + 128)
    inv = moments[3 + k : 4 + k, lanes]

    def spread(i, carry):
        rows = rows_at(i * IR, IR)
        standard = (conv[k, rows, lanes] - moments[k : k + 1, lanes]) * inv
        shift = (sums[at + t : at + t + 1] + standard * sums[at + 3 + t : at + 4 + t]) * inverse_total
        grad = dbn[rows_at(k * R + i * IR, IR), lanes]
        grad = (gains[1 + k : 2 + k, lanes] * inv) * (grad - mask * shift)
        pool[shifted_at(0, t, i * STRIDE + 16, IR), :] = pltpu.roll(grad, 1, 0)
        pool[shifted_at(1, t, i * STRIDE + 16, IR), :] = grad
        pool[shifted_at(2, t, i * STRIDE + 16, IR), :] = pltpu.roll(grad, IR - 1, 0)
        return carry

    lax.fori_loop(0, IMAGES, spread, 0)
    taps = [kernels[o, k : k + 1, lanes] for o in range(9)]

    def step(b, found):
        base = b * STRIDE + 16
        here = nrm[1, rows_at(base, CB), lanes]
        acc = jnp.zeros((CB, 128), F32)
        new = []
        for o in range(9):
            x = pool[shifted_at(2 - o % 3, t, base - (o // 3 - 1) * 16, CB), :]
            acc = acc + x * taps[o]
            new.append(found[o] + jnp.sum((x * here).reshape(CB // 8, 8, 128), 0))
        rows = rows_at(b * CB, CB)
        if not first:
            acc = acc + dn[rows, lanes]
        dn[rows, lanes] = acc
        if last:
            new.append(found[9] + jnp.sum((acc * here).reshape(CB // 8, 8, 128), 0))
            new.append(found[10] + jnp.sum((acc * cells).reshape(CB // 8, 8, 128), 0))
        return tuple(new)

    found = lax.fori_loop(0, IMAGES, step, (jnp.zeros((8, 128), F32),) * (11 if last else 9))
    found = [col_sum(f) for f in found]
    if last:
        found[9] = (found[9] - found[10] * shifts[0:1, lanes]) / gains[0:1, lanes]
    found += [jnp.zeros((1, 128), F32)] * (CONV_ROWS - len(found))
    dker[k, :, lanes] = jnp.concatenate(found, 0)


def last_norm_back(tokp, dres, dn, gains, gtok):
    mask = cell_mask(IR)

    def step(i, carry):
        rows = rows_at(i * IR, IR)
        xhat, rstd = norm_parts(tokp[rows, :])
        scaled = dn[rows, :] * mask * gains[0:1]
        one = jnp.sum(scaled, -1, keepdims=True) * (1.0 / D)
        two = jnp.sum(scaled * xhat, -1, keepdims=True) * (1.0 / D)
        gtok[rows, :] = dres[rows, :] + rstd * (scaled - one - xhat * two)
        return carry

    lax.fori_loop(0, IMAGES, step, 0)
    gtok[GAP0:R, :] = dres[GAP0:R, :]


class GradSum:
    def __init__(self, place, grads, bufs, sems, both):
        self.place, self.grads, self.both = place, grads, both
        self.rx_core, self.rx_one, self.mid, self.rx_z, self.fin, self.done = bufs
        self.own = grads.at[place.mp]
        self.slot = place.mp if both else 0
        self.rows = grads.shape[1]
        self.quarter = self.rows // QUAD
        self.part = z_part(self.rows, place.groups)
        self.block = min(self.quarter, 128)
        self.sems = sems
        self.stage = 0
        self.pending = []
        self.steps = [[self.core_start], [self.core_end, self.quad_start], [self.quad_end, self.z_start]]
        self.steps += [[self.z_end, self.z_back_start], [self.z_back_end, self.quad_back_start]]
        self.steps += [[self.end, self.core_back_start], [self.end]] if both else [[self.end]]

    def step(self):
        for part in self.steps.pop(0):
            part()

    def copies(self, ref, triples):
        self.stage += 1
        for src, dst, peer in triples:
            remote(src, dst, self.sems.at[0], self.sems.at[self.stage], peer)
        self.pending = [Pending(ref, self.sems.at[0], self.sems.at[self.stage])]

    def end(self):
        finish(self.pending)
        self.pending = []

    def add(self, dst, dst_at, mine, mine_at, theirs, rows, lanes):
        def step(b, carry):
            at = b * self.block
            total = mine[rows_at(mine_at + at, self.block), lanes].astype(F32)
            for ref in theirs:
                total = total + ref[rows_at(at, self.block), lanes].astype(F32)
            dst[rows_at(dst_at + at, self.block), lanes] = total.astype(BF)
            return carry

        lax.fori_loop(0, rows // self.block, step, 0)

    def core_start(self):
        self.copies(self.rx_core, [(self.grads.at[1 - self.place.mp], self.rx_core, self.place.other_core())])

    def core_end(self):
        self.end()
        self.add(self.own, 0, self.own, 0, [self.rx_core], self.rows, slice(None))

    def fill(self):
        if self.part * self.place.groups > self.quarter:
            self.mid[self.quarter :, :] = jnp.zeros((self.part * self.place.groups - self.quarter, D), BF)

    def quad_start(self):
        triples = []
        for o in range(1, QUAD):
            there = rows_at(lax.rem(self.place.quad + o, QUAD) * self.quarter, self.quarter)
            triples.append((self.own.at[there], self.rx_one.at[o - 1], self.place.in_quad(o)))
        self.copies(self.rx_one, triples)

    def quad_end(self):
        self.end()
        theirs = [self.rx_one.at[o] for o in range(QUAD - 1)]
        self.add(self.mid, 0, self.own, self.place.quad * self.quarter, theirs, self.quarter, slice(None))
        self.fill()

    def z_start(self):
        triples = []
        for o in range(1, self.place.groups):
            there = rows_at(lax.rem(self.place.z + o, self.place.groups) * self.part, self.part)
            triples.append((self.mid.at[there], self.rx_z.at[o - 1], self.place.along(o)))
        self.copies(self.rx_z, triples)

    def z_end(self):
        self.end()
        here = rows_at(self.place.z * self.part, self.part)
        total = self.mid[here, :].astype(F32)
        for o in range(self.place.groups - 1):
            total = total + self.rx_z[o].astype(F32)
        self.fin[here, :] = total.astype(BF)

    def z_back_start(self):
        here = self.fin.at[rows_at(self.place.z * self.part, self.part)]
        self.copies(self.rx_z, [(here, here, self.place.along(o)) for o in range(1, self.place.groups)])

    def z_back_end(self):
        self.end()
        here = rows_at(self.place.quad * self.quarter, self.quarter)
        self.done[self.slot, here, :] = self.fin[0 : self.quarter, :]

    def quad_back_start(self):
        here = self.done.at[self.slot, rows_at(self.place.quad * self.quarter, self.quarter)]
        self.copies(self.rx_one, [(here, here, self.place.in_quad(o)) for o in range(1, QUAD)])

    def core_back_start(self):
        here = self.done.at[self.place.mp]
        self.copies(self.rx_core, [(here, here, self.place.other_core())])


def z_part(rows, groups):
    return -(-rows // QUAD // (16 * groups)) * 16


UNITS = ((2 * PW, False), (2 * PW, False), (2 * PW, False), (D, True), (D, True))


def unit_buffers(groups, rows, both):
    span = z_part(rows, groups) * groups
    dims = [(rows, D), (QUAD - 1, rows // QUAD, D), (span, D)]
    dims += [(groups - 1, span // groups, D), (span, D), (2 if both else 1, rows, D)]
    return [pltpu.VMEM((2, rows, D), BF)] + [pltpu.VMEM(d, BF) for d in dims]


def main_kernel(
    groups, seg, tokens, cot, gains, shifts, kernels, wqkv, wout, win, wmo, bias_h,
    out_hbm, gtok_hbm, dw0, dw1, dw2, dw3, dw4, rest_out,
    pool, tokp, cotp, conv, nrm, dbn, outp, dres, bn, qkv, att, n2, gm, gr, act, dpre, datt, dqkv,
    wqkv_b, wout_b, win_f, wmo_f, bias_f, stats, moments, sums, sums_v, small, dbias, dker,
    mx1, mx2, sx1, sx2, lx1, lx2, vx1, vx2, kx1, kx2, kx3, kx4,
    in_sems, w_sems, pair_s, pair_r, sems, unit_sems, out_sems, dw_sems, *unit_flat,
):
    dws = (dw0, dw1, dw2, dw3, dw4)
    unit_refs = [unit_flat[n * 7 : n * 7 + 7] for n in range(len(UNITS))]
    place = Place(groups)
    place.greet()

    def load(n, src):
        copies = []
        for t in range(3):
            copy = pltpu.make_async_copy(
                src.at[0, :, pl.ds(t * 128, 128)], pool.at[pl.ds((n * 3 + t) * SCR, CELLS)], in_sems.at[n, t]
            )
            copy.start()
            copies.append(copy)
        return copies

    finish(load(0, tokens))
    loads = load(1, cot)
    blocks = [(wqkv.at[:, pl.ds(k * D, D)], dbn.at[pl.ds(k * D, D)]) for k in range(3)]
    blocks.append((wout, dbn.at[pl.ds(3 * D, D)]))
    for j in range(PARTS):
        blocks.append((win.at[:, pl.ds(j * PW, PW)], dbn.at[pl.ds((4 + j) * D, D), pl.ds(0, PW)]))
    blocks.append((wmo, dres.at[pl.ds(0, HH)]))
    weights = []
    for n, (src, dst) in enumerate(blocks):
        copy = pltpu.make_async_copy(src, dst, w_sems.at[n])
        copy.start()
        weights.append(copy)
    ahead = empty_before(seg)
    to_images(pool, 0, tokp, ahead)
    first_norm(tokp, gains, shifts, nrm)
    conv_forward(nrm, kernels, conv, stats)
    place.greeted()

    cells = IMAGES * IMG * IMG
    copies = send_eight(place, stats, mx1, sems.at[0, 0], sems.at[0, 1])
    mx1[place.slot] = stats[...]
    finish(weights)
    for k in range(3):
        wqkv_b[k] = dbn[k * D : k * D + D, :].astype(BF)
    wout_b[...] = dbn[3 * D : 4 * D, :].astype(BF)
    for j in range(PARTS):
        win_f[j, place.mp] = dbn[(4 + j) * D : (5 + j) * D, 0:PW].astype(BF)
        wmo_f[j, place.mp] = dres[j * PW : j * PW + PW, :].astype(BF)
    bias_f[place.mp] = jnp.broadcast_to(bias_h[...].reshape(1, HH), (8, HH))
    pairs = [
        remote(ref, ref, pair_s.at[n], pair_r.at[n], place.other_core())
        for n, ref in enumerate((win_f.at[:, place.mp], wmo_f.at[:, place.mp], bias_f.at[place.mp]))
    ]
    finish(loads)
    to_images(pool, 3 * SCR, cotp, ahead)
    cotangent_parts(cotp, gm, small)
    finish(copies)
    mean, m2 = merge_moments(mx1, 8, cells)
    mx2[place.z, 0:3] = mean
    mx2[place.z, 3:6] = m2
    mx2[place.z, 6:8] = jnp.zeros((2, D), F32)
    finish(send_along(place, mx2.at[place.z], mx2, sems.at[0, 0], sems.at[0, 2]))
    mean, m2 = merge_moments(mx2, groups, 8 * cells)
    moments[0:3] = mean
    moments[3:6] = lax.rsqrt(m2 * (1.0 / (cells * 8 * groups)) + EPS)
    moments[6:8] = jnp.zeros((2, D), F32)

    project(conv, moments, gains, shifts, wqkv_b, bn, qkv)
    attend(qkv, pool, att)
    attend_gap(qkv, att)
    feed_forward_in(tokp, att, wout_b, gains, shifts, dres, n2)
    finish(pairs)

    units = []
    for n, (rows, both) in enumerate(UNITS):
        units.append(GradSum(place, unit_refs[n][0], unit_refs[n][1:], unit_sems.at[n], both))
    ua, ub, ue, uc, ud = units
    grads = [refs[0] for refs in unit_refs]
    acc = dbn.at[pl.ds(0, R)]
    mine, theirs = place.mp, 1 - place.mp
    stores = []

    def keep(at, ref=None):
        def done(total):
            rest_out[at : at + total.shape[0], 0 : total.shape[1]] = total
            if ref is not None:
                ref[...] = total

        return done

    def keep_small(total):
        rest_out[80:88] = total
        tiles = [total[4 + c // 3 : 5 + c // 3, c % 3 * 128 : c % 3 * 128 + 128] for c in range(BIAS_TILES)]
        for c in range(BIAS_TILES // 2):
            at = c // 2 * 4 + c % 2
            kept = jnp.where(place.mp == 0, tiles[at], tiles[at + 2])
            rest_out[72 + c // 2 : 73 + c // 2, c % 2 * 128 : c % 2 * 128 + 128] = kept

    small_sum = SmallSum(place, small, lx1, lx2, sems, 2, keep_small)
    sum_v = SmallSum(place, sums_v, vx1, vx2, sems, 6, keep(64, sums_v))
    sum_qk = SmallSum(place, sums, sx1, sx2, sems, 1, keep(0, sums))
    ker_sums = [
        PairedSum(place, dker.at[k], *(x.at[k] for x in (kx1, kx2, kx3, kx4)), sems, 3 + k, keep(16 + 16 * k))
        for k in range(3)
    ]

    def forward(part):
        hidden_part(part, n2, gm, win_f, wmo_f, bias_f, act, dpre, outp, acc, dbias)

    def hidden(half, part):
        hidden_grads(half, n2, gm, act, dpre, grads[part])
        if half is theirs:
            units[part].step()

    def values():
        attend_back_values(pool, datt, dqkv)

    def after_forward():
        feed_forward_out(cotp, wout_b, gains, shifts, outp, acc, dres, gr, datt, small)
        for c in range(BIAS_TILES):
            tile = slice(c % 4 * 128, c % 4 * 128 + 128)
            small[4 + c // 3 : 5 + c // 3, c % 3 * 128 : c % 3 * 128 + 128] = dbias[c // 4, 0:1, tile]
        small_sum.start()
        attend_back_gap(datt, dqkv)
        stores.append(pltpu.make_async_copy(outp, out_hbm, out_sems.at[0]))
        stores[0].start()

    def out_grad():
        for p in range(3):
            grads[3][1, p * 128 : p * 128 + 128, :] = t_dot(att[p], gr[...]).astype(BF)

    def value_grads():
        project_grads(2, bn, dqkv, grads[3].at[0])
        uc.step()

    def query_grads():
        for k in range(2):
            project_grads(k, bn, dqkv, grads[4].at[k])
        ud.step()

    def value_back():
        project_back(2, conv, moments, wqkv_b, dqkv, dbn, sums_v, 0)
        sum_v.start()

    def query_back(k):
        project_back(k, conv, moments, wqkv_b, dqkv, dbn, sums, 6 * k)
        if k == 1:
            sum_qk.start()

    def back(k, t):
        held, at = (sums_v, 0) if k == 2 else (sums, 6 * k)
        conv_back(
            k, t, k == 1, k == 2, dbn, conv, moments, held, at, gains, shifts, nrm, pool, kernels, cotp, dker,
            1.0 / (cells * 8 * groups),
        )
        if t == 2:
            ker_sums[k].start()

    def last_norm():
        stores[0].wait()
        last_norm_back(tokp, dres, cotp, gains, outp)
        stores.append(pltpu.make_async_copy(outp, gtok_hbm, out_sems.at[1]))
        stores[-1].start()

    def unit(n):
        units[n].step()
        if not units[n].steps:
            stores.append(pltpu.make_async_copy(units[n].done, dws[n], dw_sems.at[n]))
            stores[-1].start()

    forward(0)
    hidden(theirs, 0)
    hidden(mine, 0)
    forward(1)
    unit(0)
    hidden(theirs, 1)
    hidden(mine, 1)
    forward(2)
    unit(1)
    hidden(theirs, 2)
    hidden(mine, 2)
    after_forward()
    unit(0)
    unit(2)
    attend_back(0, 2, qkv, pool, datt, dqkv)
    attend_back(2, 4, qkv, pool, datt, dqkv)
    unit(0)
    small_sum.step()
    unit(1)
    query_back(0)
    query_back(1)
    values()
    unit(0)
    unit(2)
    query_grads()
    small_sum.step()
    sum_qk.step()
    unit(1)
    unit(4)
    out_grad()
    value_grads()
    unit(2)
    value_back()
    unit(0)
    unit(3)
    sum_qk.step()
    unit(1)
    conv_back_zero(pool)
    back(1, 0)
    back(1, 1)
    unit(4)
    unit(2)
    back(1, 2)
    sum_v.step()
    back(0, 0)
    ker_sums[1].step()
    back(0, 1)
    unit(3)
    back(0, 2)
    unit(4)
    ker_sums[0].step()
    sum_v.step()
    back(2, 0)
    back(2, 1)
    unit(1)
    unit(3)
    back(2, 2)
    last_norm()
    ker_sums[2].step()
    unit(4)
    unit(2)
    ker_sums[1].step()
    ker_sums[0].step()
    unit(3)
    ker_sums[2].step()
    unit(4)
    ker_sums[1].step()
    ker_sums[0].step()
    ker_sums[1].step()
    ker_sums[2].step()
    unit(3)
    ker_sums[0].step()
    ker_sums[2].step()
    unit(4)
    unit(3)
    finish(stores[1:])


def main_call(groups, *args):
    units = [buf for unit in UNITS for buf in unit_buffers(groups, *unit)]
    return pl.pallas_call(
        functools.partial(main_kernel, groups),
        out_shape=(shape(R, D), shape(R, D))
        + tuple(shape(2 if both else 1, rows, D, dtype=BF) for rows, both in UNITS)
        + (shape(88, D),),
        in_specs=[VM, ANY, ANY, VM, VM, VM, ANY, ANY, ANY, ANY, VM],
        out_specs=(ANY,) * 7 + (VM,),
        scratch_shapes=[
            pltpu.VMEM((POOL, 128), F32),
            pltpu.VMEM((R, D), F32), pltpu.VMEM((R, D), F32), pltpu.VMEM((3, R, D), F32),
            pltpu.VMEM((3, CONVR, D), F32), pltpu.VMEM((3 * R, D), F32),
            pltpu.VMEM((R, D), F32), pltpu.VMEM((R, D), F32),
            pltpu.VMEM((3, R, D), BF), pltpu.VMEM((3, 3, R, 128), BF), pltpu.VMEM((3, R, 128), BF),
            pltpu.VMEM((R, D), BF), pltpu.VMEM((R, D), BF), pltpu.VMEM((R, D), BF),
            pltpu.VMEM((R, 512), BF), pltpu.VMEM((R, 512), BF), pltpu.VMEM((3, R, 128), BF), pltpu.VMEM((3, 3, R, 128), BF),
            pltpu.VMEM((3, D, D), BF), pltpu.VMEM((D, D), BF), pltpu.VMEM((PARTS, 2, D, PW), BF), pltpu.VMEM((PARTS, 2, PW, D), BF),
            pltpu.VMEM((2, 8, HH), F32),
            pltpu.VMEM((8, D), F32), pltpu.VMEM((8, D), F32), pltpu.VMEM((16, 128), F32), pltpu.VMEM((8, 128), F32),
            pltpu.VMEM((8, D), F32), pltpu.VMEM((PARTS, 8, 2 * PW), F32), pltpu.VMEM((3, CONV_ROWS, D), F32),
            pltpu.VMEM((8, 8, D), F32), pltpu.VMEM((groups, 8, D), F32),
            pltpu.VMEM((8, 16, 128), F32), pltpu.VMEM((groups, 16, 128), F32),
            pltpu.VMEM((8, 8, D), F32), pltpu.VMEM((groups, 8, D), F32),
            pltpu.VMEM((8, 8, 128), F32), pltpu.VMEM((groups, 8, 128), F32),
            pltpu.VMEM((3, 8, D), F32), pltpu.VMEM((3, QUAD, 8, D), F32), pltpu.VMEM((3, groups, 8, D), F32),
            pltpu.VMEM((3, CONV_ROWS, D), F32),
            dma(2, 3), dma(8), dma(3), dma(3), dma(7, 5), dma(5, 7), dma(2), dma(5),
        ] + units,
        compiler_params=params(collective_id=0, has_side_effects=True),
    )(*args)


def last_kernel(
    seg, outp, gtok, dwa, dwb, dwe, dwc, dwd, rest,
    output, grad_tokens, grad_gains, grad_shifts, grad_kernels, grad_qkv, grad_out, grad_in, grad_bias, grad_down,
    held, lowa, lowb, lowe, lowc, lowd, scr, wide, turned, in_sems, out_sems,
):
    loads = []
    pairs = ((outp, held.at[0]), (gtok, held.at[1]))
    pairs += ((dwa, lowa), (dwb, lowb), (dwe, lowe), (dwc, lowc), (dwd, lowd))
    for n, (src, dst) in enumerate(pairs):
        copy = pltpu.make_async_copy(src, dst, in_sems.at[n])
        copy.start()
        loads.append(copy)
    starts, gaps = find_columns(seg)
    stores = []

    def store(src, dst):
        copy = pltpu.make_async_copy(src, dst, out_sems.at[len(stores)])
        copy.start()
        stores.append(copy)

    for n, dst in enumerate((output, grad_tokens)):
        loads[n].wait()
        to_canvas(held.at[n], scr.at[n], starts, gaps)
        for t in range(3):
            store(scr.at[n, t, pl.ds(0, CELLS)], dst.at[0, :, pl.ds(t * 128, 128)])
    for n, low in enumerate((lowa, lowb, lowe)):
        loads[2 + n].wait()
        start, size = n * PW, PW
        turned[:, start : start + size] = low[0, 0:size, :].astype(F32).T
        wide[start : start + size, :] = low[0, size : 2 * size, :].astype(F32)
        store(turned.at[:, pl.ds(start, size)], grad_in.at[:, pl.ds(start, size)])
        store(wide.at[pl.ds(start, size)], grad_down.at[pl.ds(start, size)])
    for n, low in enumerate((lowc, lowd)):
        loads[5 + n].wait()
        for j in range(2):
            at = HH + (n * 2 + j) * D
            wide[at : at + D, :] = low[j].astype(F32)
            here = wide.at[pl.ds(at, D)]
            if n == 0 and j == 1:
                store(here, grad_out)
            else:
                store(here, grad_qkv.at[:, pl.ds((2 if n == 0 else j) * D, D)])
    for k in range(3):
        for o in range(9):
            row = 16 + k * CONV_ROWS + o
            grad_kernels[o, k : k + 1] = rest[row : row + 1]
    grad_gains[0:1] = rest[57:58]
    grad_gains[4:5] = rest[80:81]
    grad_shifts[0:1] = rest[58:59]
    grad_shifts[3:6] = rest[81:84]
    for t in range(3):
        lanes = slice(t * 128, t * 128 + 128)
        for k, at in enumerate((0, 6, 64)):
            grad_gains[1 + k : 2 + k, lanes] = rest[at + 3 + t : at + 4 + t, 0:128]
            if k != 1:
                grad_shifts[1 + k // 2 : 2 + k // 2, lanes] = rest[at + t : at + t + 1, 0:128]
    for j in range(PARTS):
        grad_bias[j * PW : j * PW + PW] = rest[72 + j, 0:PW]
    finish(stores)


def last_call(*args):
    return pl.pallas_call(
        last_kernel,
        out_shape=(
            shape(1, CELLS, D), shape(1, CELLS, D), shape(5, D), shape(6, D), shape(9, 3, D), shape(D, 3 * D),
            shape(D, D), shape(D, HH), shape(HH), shape(HH, D),
        ),
        in_specs=[SM] + [ANY] * 7 + [VM],
        out_specs=(ANY, ANY, VM, VM, VM, ANY, ANY, ANY, VM, ANY),
        scratch_shapes=[
            pltpu.VMEM((2, R, D), F32),
            *(pltpu.VMEM((2 if both else 1, rows, D), BF) for rows, both in UNITS),
            pltpu.VMEM((2, 3, CELLS + 16, 128), F32), pltpu.VMEM((HH + 4 * D, D), F32),
            pltpu.VMEM((D, HH), F32), dma(7), dma(16),
        ],
        compiler_params=params(),
    )(*args)


def local(
    groups, tokens, segment_ids, gains, shifts, kernels, qkv_weight, out_weight,
    mlp_in_weight, mlp_in_bias, mlp_out_weight, cotangent,
):
    found = main_call(
        groups, segment_ids, tokens, cotangent, gains, shifts, kernels.transpose(1, 0, 2),
        qkv_weight, out_weight, mlp_in_weight, mlp_out_weight, mlp_in_bias,
    )
    outs = list(last_call(segment_ids, *found))
    outs[4] = outs[4].transpose(1, 0, 2)
    return tuple(outs)


def solution(mesh):
    groups = mesh.shape["dp"] // QUAD
    both = P(("dp", "mp"), None, None)
    return jax.shard_map(
        functools.partial(local, groups),
        mesh=mesh,
        in_specs=(
            both, P(("dp", "mp"), None), P(), P(), P(), P(), P(), P(None, "mp"), P("mp"), P("mp", None), both,
        ),
        out_specs=(both, both, P(), P(), P(), P(), P(), P(None, "mp"), P("mp"), P("mp", None)),
        check_vma=False,
    )
```
